32 devices in a mesh: section: 2 (over x), batch: 4 (over z), tensor: 4 (over y, core).
Axes of the slice: x: 2, y: 2, z: 4, core: 2. Of those that a mesh axis runs over, the one named last changes fastest.
Arguments:
- patches: bfloat16 [2, 3200, 768], P(None, ('batch', 'tensor')), may hold values from -6 to 6
- cotangent: bfloat16 [2, 3200, 768], P(None, ('batch', 'tensor')), may hold values from -6 to 6
- image_lengths: int32 [2, 4, 60], P(None, 'batch'), may hold values from 0 to 800, as said below
- attn_gain: bfloat16 [2, 768], P('section'), may hold values from 0.5 to 1.5
- qkv_weight: bfloat16 [2, 768, 3, 768], P('section', None, None, 'tensor'), may hold values from -0.21875 to 0.21875
- query_gain: bfloat16 [2, 12, 64], P('section', 'tensor'), may hold values from 0.25 to 1.75
- key_gain: bfloat16 [2, 12, 64], P('section', 'tensor'), may hold values from 0.25 to 1.75
- out_weight: bfloat16 [2, 768, 768], P('section', 'tensor'), may hold values from -0.875 to 0.875
- mlp_gain: bfloat16 [2, 768], P('section'), may hold values from 0.5 to 1.5
- up_weight: bfloat16 [2, 768, 3072], P('section', None, 'tensor'), may hold values from -0.21875 to 0.21875
- down_weight: bfloat16 [2, 3072, 768], P('section', 'tensor'), may hold values from -0.109375 to 0.109375
Outputs:
- layer_outs: bfloat16 [2, 2, 3200, 768], P('section', None, ('batch', 'tensor'))
- input_grads: float32 [2, 2, 3200, 768], P('section', None, ('batch', 'tensor'))
- grad_attn_gain: float32 [2, 768], P('section')
- grad_qkv: float32 [2, 768, 3, 768], P('section', None, None, 'tensor')
- grad_query_gain: float32 [2, 12, 64], P('section', 'tensor')
- grad_key_gain: float32 [2, 12, 64], P('section', 'tensor')
- grad_out: float32 [2, 768, 768], P('section', 'tensor')
- grad_mlp_gain: float32 [2, 768], P('section')
- grad_up: float32 [2, 768, 3072], P('section', None, 'tensor')
- grad_down: float32 [2, 3072, 768], P('section', 'tensor')
The draws below stay inside these ranges and needn't reach their ends.
Inputs may be any that keep to these rules, and one draw needn't show every extreme that they name: Row s of image_lengths lists the patch counts of the images of packed sequence s: 1 to 60 images, each of 1 patch or more, come first and the remaining entries are 0; a row sums to at most 800, and its slots past that sum are padding. The sizes are heavy-tailed.
All inputs are finite; a program needn't handle non-finite values.
Results may differ from the reference program's by a relative error of at most 0.035.
Values may be sent and summed in bfloat16 or wider, within the bound.
A program may use at most 192 MiB of HBM per device.

```python
import math
import jax
import jax.numpy as jnp
from jax import lax

D = 768
HEADS = 12
HEAD = 64
FF = 3072
LENGTH = 800
SLOTS = 60
MICRO = 2
MB_TOKENS = 3200
SEQS = 8
N_TENSOR = 4


def draw_image_lengths(key, part):
    key = jax.random.fold_in(key, 11)
    keys_all = jax.random.split(key, 4)
    counts = jax.random.randint(keys_all[0], (SEQS,), 1, SLOTS + 1)
    counts = counts.at[0].set(1).at[1].set(SLOTS)
    padding = jax.random.randint(keys_all[1], (SEQS,), 0, LENGTH // 4 + 1)
    padding = padding.at[0].set(0)
    powers = jax.random.randint(keys_all[2], (SEQS, SLOTS), 0, 8)
    factors = jax.random.randint(keys_all[3], (SEQS, SLOTS), 1, 5)
    raw_sizes = factors * jnp.left_shift(jnp.ones_like(powers), powers)
    slot_ids = jnp.arange(SLOTS, dtype=jnp.int32)[None, :]
    is_live = slot_ids < counts[:, None]
    raw_sizes = jnp.where(is_live, raw_sizes, 0)
    spare_len = LENGTH - padding - counts
    extra_len = raw_sizes * spare_len[:, None] // jnp.sum(raw_sizes, axis=1, keepdims=True)
    table = jnp.where(is_live, 1 + extra_len, 0).astype(jnp.int32)
    return table.reshape(MICRO, SEQS // MICRO, SLOTS)


def block_scale(stream_key, shape, cuts, smallest, high):
    factor_of = 1.0
    for position, shards_of in cuts:
        heights = jax.random.uniform(jax.random.fold_in(jax.random.fold_in(stream_key, 6), position), (shards_of,), jnp.float32, smallest / len(cuts), high / len(cuts))
        factor_of = factor_of * jnp.repeat(jnp.exp(heights), shape[position] // shards_of).reshape((-1,) + (1,) * (len(shape) - 1 - position))
    return factor_of


def centred(rng, shape, scale, most, cuts=(), held_as=jnp.bfloat16):
    array = jax.random.normal(rng, shape, jnp.float32) * scale
    if len(cuts) > 0:
        array = block_scale(rng, shape, cuts, -0.22, 0.18) * array
    return jnp.clip(array, min=-most, max=most).astype(held_as)


def setup_inputs(seed: int = 0) -> dict:
    key_of = jax.random.split(jax.random.key(seed), 12)
    return {
        "patches": centred(key_of[0], (MICRO, MB_TOKENS, D), 1.0, 6.0, ((1, 16),)),
        "cotangent": centred(key_of[1], (MICRO, MB_TOKENS, D), 1.0, 6.0, ((1, 16),)),
        "image_lengths": draw_image_lengths(jax.random.fold_in(key_of[11], 71), 0),
        "attn_gain": jnp.clip(1.0 + 0.1 * jax.random.normal(key_of[3], (2, D), jnp.float32), 0.5, 1.5).astype(jnp.bfloat16),
        "qkv_weight": centred(key_of[4], (2, D, 3, D), D ** -0.5, 0.21875, ((0, 2), (3, 4))),
        "query_gain": jnp.clip(1.0 + 0.15 * jax.random.normal(key_of[5], (2, HEADS, HEAD), jnp.float32), 0.25, 1.75).astype(jnp.bfloat16),
        "key_gain": jnp.clip(1.0 + 0.15 * jax.random.normal(key_of[6], (2, HEADS, HEAD), jnp.float32), 0.25, 1.75).astype(jnp.bfloat16),
        "out_weight": centred(key_of[7], (2, D, D), (D // 16) ** -0.5, 0.875, ((0, 2), (1, 4))),
        "mlp_gain": jnp.clip(1.0 + 0.1 * jax.random.normal(key_of[8], (2, D), jnp.float32), 0.5, 1.5).astype(jnp.bfloat16),
        "up_weight": centred(key_of[9], (2, D, FF), D ** -0.5, 0.21875, ((0, 2), (2, 4))),
        "down_weight": centred(key_of[10], (2, FF, D), FF ** -0.5, 0.109375, ((0, 2), (1, 4))),
    }


@jax.custom_vjp
def low(v):
    return lax.optimization_barrier(v.astype(jnp.bfloat16)).astype(jnp.float32)

@jax.custom_vjp
def low_back(v):
    return v

def low_keep(v):
    return (low(v), None)

def low_pass(kept, grad):
    return (grad,)

def back_keep(v):
    return (v, None)

def back_low(kept, grad):
    return (low(grad),)
low.defvjp(low_keep, low_pass)
low_back.defvjp(back_keep, back_low)
epsilon = 1e-06
neg_fill = -1000000000.0
highest = lax.Precision.HIGHEST

def norm_rows(rows_in, gain_vec):
    centre = rows_in - lax.optimization_barrier(jnp.mean(rows_in, axis=-1, keepdims=True))
    spread = lax.optimization_barrier(jnp.mean(centre * centre, axis=-1, keepdims=True))
    return centre * lax.rsqrt(spread + epsilon) * gain_vec

def segment_ids(len_table):
    bounds = jnp.cumsum(len_table, axis=-1, dtype=jnp.int32)
    places = jnp.arange(LENGTH, dtype=jnp.int32)
    return lax.optimization_barrier(jnp.sum((places[None, :, None] >= bounds[:, None, :]).astype(jnp.int32), axis=-1)).astype(jnp.int32)

def layer(layer_in, len_table, weights):
    attn_gain, qkv_weight, query_gain, key_gain, out_weight, mlp_gain, up_weight, down_weight = weights
    row_count = layer_in.shape[0]
    seq_count = len_table.shape[0]
    local_heads = HEADS // N_TENSOR
    head_cols = local_heads * HEAD
    hidden = FF // N_TENSOR
    normed = low(norm_rows(layer_in, attn_gain))
    pieces = []
    for group_index in range(N_TENSOR):
        block_weight = qkv_weight[:, :, group_index * head_cols:(group_index + 1) * head_cols].reshape(D, 3 * head_cols)
        pieces.append(jnp.dot(normed, block_weight, precision=highest).reshape(row_count, 3, local_heads, HEAD))
    projected = low_back(jnp.concatenate(pieces, axis=2))
    grid_shape = (seq_count, LENGTH, HEADS, HEAD)
    queries = low_back(low(norm_rows(projected[:, 0], query_gain))).reshape(grid_shape)
    key_rows = low_back(low(norm_rows(projected[:, 1], key_gain))).reshape(grid_shape)
    value_rows = low(projected[:, 2]).reshape(grid_shape)
    segments = segment_ids(len_table)
    same_seg = (segments[:, :, None] == segments[:, None, :])[:, None]
    scores = low_back(HEAD ** (-0.5) * jnp.einsum('sqhd,skhd->shqk', queries, key_rows, precision=highest))
    scores = jnp.where(same_seg, scores, neg_fill)
    row_max = lax.optimization_barrier(jnp.max(scores, axis=-1, keepdims=True))
    exp_scores = jnp.exp(scores - row_max)
    probs_low = low(exp_scores / lax.optimization_barrier(jnp.sum(exp_scores, axis=-1, keepdims=True)))
    mixed_out = jnp.einsum('shqk,skhd->sqhd', probs_low, value_rows, precision=highest).reshape(row_count, D)
    mixed_out = low_back(low(mixed_out))
    attended = jnp.zeros((row_count, D), jnp.float32)
    for group_index in range(N_TENSOR):
        cols_from = group_index * head_cols
        attended = attended + low(jnp.dot(mixed_out[:, cols_from:cols_from + head_cols], out_weight[cols_from:cols_from + head_cols], precision=highest))
    residual = layer_in + low_back(attended)
    second = low(norm_rows(residual, mlp_gain))
    ups = []
    for group_index in range(N_TENSOR):
        ups.append(jnp.dot(second, up_weight[:, group_index * hidden:(group_index + 1) * hidden], precision=highest))
    upper = low_back(jnp.concatenate(ups, axis=1))
    activated = low(jax.nn.gelu(upper, approximate=False))
    down_sum = jnp.zeros((row_count, D), jnp.float32)
    for group_index in range(N_TENSOR):
        cols_from = group_index * hidden
        down_sum = down_sum + low(jnp.dot(activated[:, cols_from:cols_from + hidden], down_weight[cols_from:cols_from + hidden], precision=highest))
    return residual + low_back(down_sum)

def reference(patches, cotangent, image_lengths, attn_gain, qkv_weight, query_gain, key_gain, out_weight, mlp_gain, up_weight, down_weight):
    group_size = math.gcd(SEQS, 4)
    step_count = SEQS // group_size
    row_count = group_size * LENGTH
    params = tuple((w.astype(jnp.float32) for w in (attn_gain, qkv_weight, query_gain, key_gain, out_weight, mlp_gain, up_weight, down_weight)))
    inputs = patches.astype(jnp.float32).reshape(step_count, row_count, D)
    len_tables = image_lengths.reshape(step_count, group_size, SLOTS)
    tap_rows = jnp.zeros((step_count, row_count, D), jnp.float32)
    seed_rows = cotangent.astype(jnp.float32).reshape(step_count, row_count, D)

    def forward(layer_inputs, tap_inputs, param_set):
        first = tuple((w[0] for w in param_set))
        later = tuple((w[1] for w in param_set))

        def both_layers(layer_in, len_table, tap_in):
            sent_out = low_back(low(layer(layer_in, len_table, first) + tap_in))
            return (sent_out, layer(sent_out, len_table, later))
        checked = jax.checkpoint(both_layers)

        def scan_step(carried, scan_item):
            return (carried, checked(scan_item[0], scan_item[1], scan_item[2]))
        carried, results = lax.scan(scan_step, jnp.zeros((), jnp.float32), (layer_inputs, len_tables, tap_inputs))
        return results
    results, pullback = jax.vjp(forward, inputs, tap_rows, params)
    grad_in, grad_tap, grads = pullback((jnp.zeros_like(results[0]), seed_rows))
    layer_outs = jnp.stack([results[0].reshape(MICRO, MB_TOKENS, D), results[1].reshape(MICRO, MB_TOKENS, D)]).astype(jnp.bfloat16)
    input_grads = jnp.stack([grad_in.reshape(MICRO, MB_TOKENS, D), grad_tap.reshape(MICRO, MB_TOKENS, D)])
    return (layer_outs, input_grads, grads[0], grads[1], grads[2], grads[3], grads[4], grads[5], grads[6], grads[7])
```

```python
import functools

import jax
import jax.numpy as jnp
from jax import lax
from jax.experimental import pallas as pl
from jax.experimental.pallas import tpu as pltpu
from jax.sharding import PartitionSpec as P

HEAD = 64
EPS = 1e-06
MESH = pl.DeviceIdType.MESH
BF = jnp.bfloat16
F32 = jnp.float32
KEY_BLOCK = 64
COLS = 256


def ceil_to(n, m):
    return -(-n // m) * m


def mm(a, b):
    return lax.dot_general(a, b, (((1,), (0,)), ((), ())), preferred_element_type=F32)


def mm_nt(a, b):
    return lax.dot_general(a, b, (((1,), (1,)), ((), ())), preferred_element_type=F32)


def mm_tn(a, b):
    return lax.dot_general(a, b, (((0,), (0,)), ((), ())), preferred_element_type=F32)


def normed(v):
    centre = v - jnp.mean(v, axis=-1, keepdims=True)
    r = lax.rsqrt(jnp.mean(centre * centre, axis=-1, keepdims=True) + EPS)
    return centre * r, r


def normed_back(dv, gain, xh, r):
    g = dv * gain
    return r * (g - jnp.mean(g, axis=-1, keepdims=True) - xh * jnp.mean(g * xh, axis=-1, keepdims=True))


def body(
    x_ref, ct_ref, segc_ref, segr_ref, sml_in, qkg_in, wq_in, wo_in, wu_in, wd_in,
    y_out, ig_out, gq_out, go_out, gu_out, gd_out, gg_out, gh_out,
    wq, wo, wu, wd, sml, qkg,
    xres, xh1, r1, xh2, r2,
    a_all, b_all, dm_all, da_all,
    qkh, qkr, qkvb, lse, o_t, g_all, gp_all,
    rows_buf, part, sendbuf, ysend, crecv, yrecv,
    e_buf, d_buf, dot_buf, dqkv_t,
    ybuf, dxbuf, ylo, dxlo,
    w_loc, w_send, w_recv, ag_s, ag_r, rs_s, rs_r, x_s, x_r,
):
    s, b, t = lax.axis_index("section"), lax.axis_index("batch"), lax.axis_index("tensor")
    y, c = t // 2, lax.rem(t, 2)
    core_id = (s, b, y * 2 + 1 - c)
    y_id = (s, b, (1 - y) * 2 + c)
    x_id = (1 - s, b, t)
    R, D = x_ref.shape
    N = 4 * R
    FF = wu.shape[2]
    HD = wo.shape[1]
    NH = HD // HEAD
    NB = N // KEY_BLOCK
    pos = c * 2 + y
    ypos = c * 2 + 1 - y
    own_rows = pl.ds(pl.multiple_of(pos * R, 16), R)
    y_rows = pl.ds(pl.multiple_of(ypos * R, 16), R)

    barrier = pltpu.get_barrier_semaphore()
    for peer in (core_id, y_id, x_id):
        pl.semaphore_signal(barrier, inc=1, device_id=peer, device_id_type=MESH)
    pl.semaphore_wait(barrier, 3)

    def remote(src, dst, ss, rs, peer):
        return pltpu.make_async_remote_copy(
            src_ref=src, dst_ref=dst, send_sem=ss, recv_sem=rs, device_id=peer, device_id_type=MESH
        )

    def arrived(ref, sem):
        pltpu.make_async_copy(ref, ref, sem).wait()

    moves = ((sml_in, sml), (qkg_in, qkg), (wq_in, wq), (wo_in, wo), (wu_in, wu), (wd_in, wd))
    for i, (src, dst) in enumerate(moves):
        remote(src, dst.at[s], w_send.at[i], w_recv.at[s, i], x_id).start()
        pltpu.make_async_copy(src, dst.at[s], w_loc.at[i]).start()
    for i, (src, dst) in enumerate(moves):
        pltpu.make_async_copy(src, dst.at[s], w_loc.at[i]).wait()

    def weights_here(l, i):
        @pl.when(l != s)
        def _():
            arrived(moves[i][1].at[1 - s], w_recv.at[1 - s, i])

    def gather_start(buf, l, op):
        mine = buf.at[l, own_rows]
        remote(mine, mine, ag_s.at[l, op, 0], ag_r.at[l, op, 0], core_id).start()
        remote(mine, mine, ag_s.at[l, op, 1], ag_r.at[l, op, 1], y_id).start()

    def gather_finish(buf, l, op):
        mine = buf.at[l, own_rows]
        theirs = buf.at[l, y_rows]
        arrived(theirs, ag_r.at[l, op, 1])
        third = remote(theirs, theirs, ag_s.at[l, op, 2], ag_r.at[l, op, 2], core_id)
        third.start()
        arrived(mine, ag_r.at[l, op, 0])
        arrived(mine, ag_r.at[l, op, 2])
        arrived(mine, ag_s.at[l, op, 0])
        arrived(mine, ag_s.at[l, op, 1])
        arrived(theirs, ag_s.at[l, op, 2])

    def scatter_start(product, l, op):
        slot = op % 2

        def send_tile(j, carry):
            cols = pl.ds(pl.multiple_of(j * COLS, COLS), COLS)
            sendbuf[:, cols] = product(pl.multiple_of((1 - c) * 2 * R, 16), cols).astype(BF)
            return carry

        lax.fori_loop(0, D // COLS, send_tile, 0)
        first = remote(sendbuf, crecv.at[slot], rs_s.at[l, op, 0], rs_r.at[l, op, 0], core_id)
        first.start()

        def own_tile(j, carry):
            cols = pl.ds(pl.multiple_of(j * COLS, COLS), COLS)
            part[:, cols] = product(pl.multiple_of(c * 2 * R, 16), cols)
            return carry

        lax.fori_loop(0, D // COLS, own_tile, 0)
        arrived(sendbuf, rs_r.at[l, op, 0])
        other = pl.ds(pl.multiple_of((1 - y) * R, 16), R)
        ysend[...] = (part[other] + crecv[slot, other].astype(F32)).astype(BF)
        remote(ysend, yrecv.at[slot], rs_s.at[l, op, 1], rs_r.at[l, op, 1], y_id).start()

    def scatter_finish(l, op):
        slot = op % 2
        mine = pl.ds(pl.multiple_of(y * R, 16), R)
        arrived(sendbuf, rs_s.at[l, op, 0])
        arrived(ysend, rs_s.at[l, op, 1])
        arrived(ysend, rs_r.at[l, op, 1])
        return part[mine] + crecv[slot, mine].astype(F32) + yrecv[slot].astype(F32)

    def q_rows(h):
        return pl.ds(pl.multiple_of(h * HEAD, HEAD), HEAD)

    def forward(l):
        weights_here(l, 0)
        weights_here(l, 1)
        xh, r = normed(xres[...])
        xh1[l] = xh
        r1[l] = r
        a_all[l, own_rows] = (xh * sml[l, 0:1]).astype(BF)
        gather_start(a_all, l, 0)
        weights_here(l, 2)
        gather_finish(a_all, l, 0)

        def project(i, carry):
            rows = pl.ds(pl.multiple_of(i * HD, HEAD), HD)
            qkvb[l, rows] = mm_nt(wq[l, rows], a_all[l]).astype(BF)
            return carry

        def project_normed(i, carry):
            rows = pl.ds(pl.multiple_of(i * HD, HEAD), HD)
            v = mm_nt(wq[l, rows], a_all[l])
            for h in range(NH):
                u = v[h * HEAD : (h + 1) * HEAD]
                u = u - jnp.mean(u, axis=0, keepdims=True)
                rr = lax.rsqrt(jnp.mean(u * u, axis=0, keepdims=True) + EPS)
                u = u * rr
                at = pl.ds(pl.multiple_of(i * HD + h * HEAD, HEAD), HEAD)
                qkh[l, at] = u
                qkr[l, i, pl.ds(h, 1)] = rr
                scale = jnp.where(i == 0, HEAD**-0.5, 1.0).astype(F32)
                gain = jnp.where(i == 0, qkg[l, :, h : h + 1], qkg[l, :, NH + h : NH + h + 1])
                qkvb[l, at] = ((u * gain).astype(BF).astype(F32) * scale).astype(BF)
            return carry

        lax.fori_loop(0, 2, project_normed, 0)
        project(2, 0)

        def head(h, carry):
            q_t = qkvb[l, q_rows(h)]
            k_rows = qkvb[l, q_rows(NH + h)].astype(F32).T.astype(BF)
            v_t = qkvb[l, q_rows(2 * NH + h)]
            rows_buf[0, :, :HEAD] = k_rows

            def block(i, total):
                at = pl.ds(pl.multiple_of(i * KEY_BLOCK, KEY_BLOCK), KEY_BLOCK)
                sc = mm(rows_buf[0, at, :HEAD], q_t)
                e = jnp.where(segc_ref[at] == segr_ref[...], jnp.exp(sc), 0.0)
                e_buf[at] = e.astype(BF)
                return total + jnp.sum(e, axis=0, keepdims=True)

            total = lax.fori_loop(0, NB, block, jnp.zeros((1, N), F32))
            lse[l, pl.ds(h, 1)] = jnp.log(total)
            o_t[l, q_rows(h)] = (mm(v_t, e_buf[...]) * (1.0 / total)).astype(BF)
            return carry

        lax.fori_loop(0, NH, head, 0)
        rows_buf[1, :, :HD] = o_t[l].astype(F32).T.astype(BF)
        weights_here(l, 3)
        scatter_start(lambda at, cols: mm(rows_buf[1, pl.ds(at, 2 * R), :HD], wo[l, :, cols]), l, 0)
        residual = xres[...] + scatter_finish(l, 0)
        xres[...] = residual
        xh, r = normed(residual)
        xh2[l] = xh
        r2[l] = r
        b_all[l, own_rows] = (xh * sml[l, 1:2]).astype(BF)
        gather_start(b_all, l, 1)
        weights_here(l, 4)
        gather_finish(b_all, l, 1)

        def hidden(i, carry):
            rows = pl.ds(pl.multiple_of(lax.rem(i, 4) * R, 16), R)
            cols = pl.ds(pl.multiple_of((i // 4) * COLS, COLS), COLS)
            u = mm(b_all[l, rows], wu[l, :, cols])
            cdf = 0.5 * (1.0 + lax.erf(u * 0.7071067811865476))
            pdf = jnp.exp(-0.5 * u * u) * 0.3989422804014327
            g_all[l, rows, cols] = (u * cdf).astype(BF)
            gp_all[l, rows, cols] = (cdf + u * pdf).astype(BF)
            return carry

        lax.fori_loop(0, 4 * (FF // COLS), hidden, 0)
        weights_here(l, 5)
        scatter_start(lambda at, cols: mm(g_all[l, pl.ds(at, 2 * R)], wd[l, :, cols]), l, 1)
        out = xres[...] + scatter_finish(l, 1)
        rounded = out.astype(BF)
        ybuf[l] = rounded
        xres[...] = rounded.astype(F32)

    xres[...] = x_ref[...].astype(F32)

    def forward_step(l, carry):
        forward(l)
        return carry

    lax.fori_loop(0, 2, forward_step, 0)
    y_move = remote(ybuf.at[1 - s], ylo, x_s.at[0], x_r.at[0], x_id)
    y_move.start()

    def backward(l):
        dm_all[l, own_rows] = xres[...].astype(BF)
        gather_start(dm_all, l, 2)
        gather_finish(dm_all, l, 2)

        def hidden(i, carry):
            rows = pl.ds(pl.multiple_of(lax.rem(i, 4) * R, 16), R)
            cols = pl.ds(pl.multiple_of((i // 4) * COLS, COLS), COLS)
            dg = mm_nt(dm_all[l, rows], wd[l, cols])
            gp_all[l, rows, cols] = (dg * gp_all[l, rows, cols].astype(F32)).astype(BF)
            return carry

        lax.fori_loop(0, 4 * (FF // COLS), hidden, 0)
        scatter_start(lambda at, cols: mm_nt(gp_all[l, pl.ds(at, 2 * R)], wu[l, cols]), l, 2)

        def hidden_grads(i, carry):
            cols = pl.ds(pl.multiple_of(i * COLS, COLS), COLS)
            gd_out[l, cols] = mm_tn(g_all[l, :, cols], dm_all[l]).astype(BF)
            gu_out[l, cols] = mm_tn(b_all[l, :, cols], gp_all[l]).astype(BF)
            return carry

        lax.fori_loop(0, FF // COLS, hidden_grads, 0)
        db = scatter_finish(l, 2)
        gg_out[l, 1:2] = jnp.sum(db * xh2[l], axis=0, keepdims=True)
        dh = xres[...] + normed_back(db, sml[l, 1:2], xh2[l], r2[l])
        xres[...] = dh
        da_all[l, own_rows] = dh.astype(BF)
        gather_start(da_all, l, 3)
        gather_finish(da_all, l, 3)
        dot_buf[...] = mm_nt(wo[l], da_all[l]).astype(BF)
        go_out[l] = mm(o_t[l], da_all[l]).astype(BF)

        def head(h, carry):
            q_t = qkvb[l, q_rows(h)]
            k_t = qkvb[l, q_rows(NH + h)]
            v_t = qkvb[l, q_rows(2 * NH + h)]
            rows_buf[0, :, :HEAD] = k_t.astype(F32).T.astype(BF)
            rows_buf[1, :, :HEAD] = v_t.astype(F32).T.astype(BF)
            do_t = dot_buf[q_rows(h)]
            delta = jnp.sum(do_t.astype(F32) * o_t[l, q_rows(h)].astype(F32), axis=0, keepdims=True)
            log_total = lse[l, pl.ds(h, 1)]

            def block(i, carry):
                at = pl.ds(pl.multiple_of(i * KEY_BLOCK, KEY_BLOCK), KEY_BLOCK)
                sc = mm(rows_buf[0, at, :HEAD], q_t)
                p = jnp.where(segc_ref[at] == segr_ref[...], jnp.exp(sc - log_total), 0.0)
                dp = mm(rows_buf[1, at, :HEAD], do_t)
                e_buf[at] = p.astype(BF)
                d_buf[at] = (p * (dp - delta)).astype(BF)
                return carry

            lax.fori_loop(0, NB, block, 0)
            dqkv_t[q_rows(2 * NH + h)] = mm_nt(do_t, e_buf[...]).astype(BF)
            dk = mm_nt(q_t, d_buf[...])
            dq = mm(k_t, d_buf[...]) * (HEAD**-0.5)
            for i, dv in ((0, dq), (1, dk)):
                at = q_rows(i * NH + h)
                dv = dv.astype(BF).astype(F32)
                uh = qkh[l, at]
                gh_out[l, i, h] = jnp.sum(dv * uh, axis=1, keepdims=True)
                gain = gains_of(l, i, h)
                g = dv * gain
                back = g - jnp.mean(g, axis=0, keepdims=True) - uh * jnp.mean(g * uh, axis=0, keepdims=True)
                dqkv_t[at] = (qkr[l, i, pl.ds(h, 1)] * back).astype(BF)
            return carry

        def gains_of(l, i, h):
            out = qkg[l, :, i * NH : i * NH + 1]
            for k in range(1, NH):
                out = jnp.where(h == k, qkg[l, :, i * NH + k : i * NH + k + 1], out)
            return out

        lax.fori_loop(0, NH, head, 0)
        rows_buf[0] = dqkv_t[...].astype(F32).T.astype(BF)
        scatter_start(lambda at, cols: mm(rows_buf[0, pl.ds(at, 2 * R)], wq[l, :, cols]), l, 3)
        gq_out[l] = mm(dqkv_t[...], a_all[l]).astype(BF)
        da = scatter_finish(l, 3)
        gg_out[l, 0:1] = jnp.sum(da * xh1[l], axis=0, keepdims=True)
        dx = xres[...] + normed_back(da, sml[l, 0:1], xh1[l], r1[l])
        rounded = dx.astype(BF)
        dxbuf[l] = rounded
        kept = jnp.where(l == 0, dx, rounded.astype(F32))
        xres[...] = rounded.astype(F32)

        @pl.when(l == s)
        def _():
            ig_out[s] = kept

    xres[...] = ct_ref[...].astype(F32)

    def backward_step(i, carry):
        backward(1 - i)
        return carry

    lax.fori_loop(0, 2, backward_step, 0)
    dx_move = remote(dxbuf.at[1 - s], dxlo, x_s.at[1], x_r.at[1], x_id)
    dx_move.start()
    y_move.wait()
    y_out[s] = ybuf[s]
    y_out[1 - s] = ylo[...]
    for i, (src, dst) in enumerate(moves):
        arrived(dst.at[s], w_send.at[i])
    dx_move.wait()
    ig_out[1 - s] = dxlo[...].astype(F32)


def fused(x, ct, segc, segr, small, qk_gain, wq, wo, wu, wd):
    R, D = x.shape
    N = 4 * R
    QD, HD, FF = wq.shape[0], wo.shape[0], wu.shape[1]
    NH = HD // HEAD
    vmem = pl.BlockSpec(memory_space=pltpu.VMEM)
    hbm = pl.BlockSpec(memory_space=pl.ANY)
    shape = jax.ShapeDtypeStruct
    V = pltpu.VMEM
    dma = pltpu.SemaphoreType.DMA
    return pl.pallas_call(
        body,
        out_shape=(
            shape((2, R, D), BF),
            shape((2, R, D), F32),
            shape((2, QD, D), BF),
            shape((2, HD, D), BF),
            shape((2, D, FF), BF),
            shape((2, FF, D), BF),
            shape((2, 8, D), F32),
            shape((2, 2, NH, HEAD, 1), F32),
        ),
        in_specs=[vmem] * 4 + [hbm] * 6,
        out_specs=(vmem,) * 8,
        scratch_shapes=[
            V((2, QD, D), BF), V((2, HD, D), BF), V((2, D, FF), BF), V((2, FF, D), BF),
            V((2, 8, D), F32), V((2, HEAD, 128), F32),
            V((R, D), F32), V((2, R, D), F32), V((2, R, 1), F32), V((2, R, D), F32), V((2, R, 1), F32),
            V((2, N, D), BF), V((2, N, D), BF), V((2, N, D), BF), V((2, N, D), BF),
            V((2, 2 * HD, N), F32), V((2, 2, 8, N), F32), V((2, QD, N), BF), V((2, 8, N), F32),
            V((2, HD, N), BF), V((2, N, FF), BF), V((2, N, FF), BF),
            V((2, N, QD), BF), V((2 * R, D), F32), V((2 * R, D), BF), V((R, D), BF),
            V((2, 2 * R, D), BF), V((2, R, D), BF),
            V((N, N), BF), V((N, N), BF), V((HD, N), BF), V((QD, N), BF),
            V((2, R, D), BF), V((2, R, D), BF), V((R, D), BF), V((R, D), BF),
            dma((6,)), dma((6,)), dma((2, 6)),
            dma((2, 4, 3)), dma((2, 4, 3)), dma((2, 4, 2)), dma((2, 4, 2)), dma((2,)), dma((2,)),
        ],
        name="layers",
        compiler_params=pltpu.CompilerParams(
            collective_id=0, has_side_effects=True, vmem_limit_bytes=63 * 2**20
        ),
    )(x, ct, segc, segr, small, qk_gain, wq, wo, wu, wd)


def shards(
    patches, cotangent, image_lengths, attn_gain, qkv_weight, query_gain, key_gain, out_weight,
    mlp_gain, up_weight, down_weight,
):
    s = lax.axis_index("section")
    _, own, D = patches.shape
    seq_len = 4 * own
    R = ceil_to(own, 16)
    N = 4 * R
    HD = out_weight.shape[1]
    NH = HD // HEAD
    pad = ((0, R - own), (0, 0))
    x = jnp.pad(lax.dynamic_index_in_dim(patches, s, 0, keepdims=False), pad)
    ct = jnp.pad(lax.dynamic_index_in_dim(cotangent, s, 0, keepdims=False), pad)
    lengths = lax.dynamic_index_in_dim(image_lengths, s, 0, keepdims=False)[0]
    bounds = jnp.cumsum(lengths, dtype=jnp.int32)
    places = jnp.arange(seq_len, dtype=jnp.int32)
    seg = jnp.sum((places[:, None] >= bounds[None, :]).astype(jnp.int32), axis=-1)
    seg = seg.reshape(2, 2, own).transpose(1, 0, 2).reshape(4, own)
    seg = jnp.pad(seg, ((0, 0), (0, R - own)), constant_values=-1).reshape(N)
    small = jnp.zeros((8, D), F32).at[0].set(attn_gain[0].astype(F32)).at[1].set(mlp_gain[0].astype(F32))
    qk_gain = jnp.concatenate([query_gain[0], key_gain[0]], axis=0).astype(F32).T
    qk_gain = jnp.pad(qk_gain, ((0, 0), (0, 128 - 2 * NH)))
    wq = qkv_weight[0].reshape(D, 3 * HD).T
    y, ig, gq, go, gu, gd, gg, gh = fused(
        x, ct, seg[:, None], seg[None, :], small, qk_gain, wq, out_weight[0], up_weight[0], down_weight[0]
    )

    def reduced(g):
        theirs = lax.ppermute(g[1 - s], "section", [(0, 1), (1, 0)])
        both = (g[s].astype(F32) + theirs.astype(F32)).astype(g.dtype)
        return both

    big = [reduced(g) for g in (gq, go, gu, gd)]
    gq, go, gu, gd = lax.psum(tuple(big), "batch")
    gg = lax.psum(gg[:, :2], ("section", "batch", "tensor"))[s]
    gh = lax.psum(gh[..., 0], ("section", "batch"))[s]
    return (
        y[:, :own][None],
        ig[:, :own][None],
        gg[0][None],
        gq.astype(F32).T.reshape(D, 3, HD)[None],
        gh[0][None],
        gh[1][None],
        go.astype(F32)[None],
        gg[1][None],
        gu.astype(F32)[None],
        gd.astype(F32)[None],
    )


def solution(mesh):
    return jax.shard_map(
        shards,
        mesh=mesh,
        in_specs=(
            P(None, ("batch", "tensor"), None),
            P(None, ("batch", "tensor"), None),
            P(None, "batch", None),
            P("section", None),
            P("section", None, None, "tensor"),
            P("section", "tensor", None),
            P("section", "tensor", None),
            P("section", "tensor", None),
            P("section", None),
            P("section", None, "tensor"),
            P("section", "tensor", None),
        ),
        out_specs=(
            P("section", None, ("batch", "tensor"), None),
            P("section", None, ("batch", "tensor"), None),
            P("section", None),
            P("section", None, None, "tensor"),
            P("section", "tensor", None),
            P("section", "tensor", None),
            P("section", "tensor", None),
            P("section", None),
            P("section", None, "tensor"),
            P("section", "tensor", None),
        ),
        check_vma=False,
    )
```

```python
import functools

import jax
import jax.numpy as jnp
from jax import lax
from jax.experimental import pallas as pl
from jax.experimental.pallas import tpu as pltpu
from jax.sharding import PartitionSpec as P

HEAD = 64
EPS = 1e-06
MESH = pl.DeviceIdType.MESH
BF = jnp.bfloat16
F32 = jnp.float32
KEY_BLOCK = 64
COLS = 256
SUB = 192
TAKEN = ((0, 0, 0, 1, 2, 3, 5, 7, 9, 10, 11, 12), (2, 3, 4, 6, 7, 9, 10, 11, 12, 12, 12, 12))
LAYER_POINTS = 7


def ceil_to(n, m):
    return -(-n // m) * m


def mm(a, b):
    return lax.dot_general(a, b, (((1,), (0,)), ((), ())), preferred_element_type=F32)


def mm_nt(a, b):
    return lax.dot_general(a, b, (((1,), (1,)), ((), ())), preferred_element_type=F32)


def mm_tn(a, b):
    return lax.dot_general(a, b, (((0,), (0,)), ((), ())), preferred_element_type=F32)


def normed(v):
    centre = v - jnp.mean(v, axis=-1, keepdims=True)
    r = lax.rsqrt(jnp.mean(centre * centre, axis=-1, keepdims=True) + EPS)
    return centre * r, r


def normed_back(dv, gain, xh, r):
    g = dv * gain
    return r * (g - jnp.mean(g, axis=-1, keepdims=True) - xh * jnp.mean(g * xh, axis=-1, keepdims=True))


def body(
    chain,
    x_ref, ct_ref, segc_ref, segr_ref, sml_in, qkg_in, wq_in, wo_in, wu_in, wd_in,
    y_out, ig_out, g_out, gg_out, gh_out,
    wq, wo, wu, wd, sml, qkg,
    xres, xh1, r1, xh2, r2,
    a_all, b_all, dm_all, da_all,
    qkh, qkr, qkvb, lse, o_t, g_all, gp_all,
    rows_buf, part, sendbuf, ysend, crecv, yrecv,
    e_buf, d_buf, dot_buf, dqkv_t,
    ybuf, dxbuf, ylo, dxlo,
    grads, gains, hgains,
    w_loc, w_send, w_recv, ag_s, ag_r, rs_s, rs_r, x_s, x_r,
    gx, gz, gpart, gfin, gains_x, hgains_x, gains_z, hgains_z, gains_t,
    gx_s, gx_r, gz_s, gz_r, g_loc, sm_s, sm_r,
):
    s, b, t = lax.axis_index("section"), lax.axis_index("batch"), lax.axis_index("tensor")
    y, c = t // 2, lax.rem(t, 2)
    core_id = (s, b, y * 2 + 1 - c)
    y_id = (s, b, (1 - y) * 2 + c)
    x_id = (1 - s, b, t)
    R, D = x_ref.shape
    N = 4 * R
    FF = wu.shape[2]
    HD = wo.shape[1]
    NH = HD // HEAD
    NB = N // KEY_BLOCK
    pos = c * 2 + y
    ypos = c * 2 + 1 - y
    own_rows = pl.ds(pl.multiple_of(pos * R, 16), R)
    y_rows = pl.ds(pl.multiple_of(ypos * R, 16), R)

    diag_id = (s, b, (1 - y) * 2 + 1 - c)
    z_ids = [(s, lax.rem(b + k, 4), t) for k in (1, 2, 3)] if chain else []
    barrier = pltpu.get_barrier_semaphore()
    for peer in [core_id, y_id, diag_id, x_id] + z_ids:
        pl.semaphore_signal(barrier, inc=1, device_id=peer, device_id_type=MESH)
    pl.semaphore_wait(barrier, 4 + len(z_ids))

    def remote(src, dst, ss, rs, peer):
        return pltpu.make_async_remote_copy(
            src_ref=src, dst_ref=dst, send_sem=ss, recv_sem=rs, device_id=peer, device_id_type=MESH
        )

    def arrived(ref, sem):
        pltpu.make_async_copy(ref, ref, sem).wait()

    moves = ((sml_in, sml), (qkg_in, qkg), (wq_in, wq), (wo_in, wo), (wu_in, wu), (wd_in, wd))
    for i, (src, dst) in enumerate(moves):
        remote(src, dst.at[s], w_send.at[i], w_recv.at[s, i], x_id).start()
        pltpu.make_async_copy(src, dst.at[s], w_loc.at[i]).start()
    for i, (src, dst) in enumerate(moves):
        pltpu.make_async_copy(src, dst.at[s], w_loc.at[i]).wait()

    def weights_here(l, i):
        @pl.when(l != s)
        def _():
            arrived(moves[i][1].at[1 - s], w_recv.at[1 - s, i])

    def gather_start(buf, l, op):
        part_of = l if op < 2 else 0
        mine = buf.at[part_of, own_rows]
        remote(mine, mine, ag_s.at[l, op, 0], ag_r.at[l, op, 0], core_id).start()
        remote(mine, mine, ag_s.at[l, op, 1], ag_r.at[l, op, 1], y_id).start()

    def gather_finish(buf, l, op):
        part_of = l if op < 2 else 0
        mine = buf.at[part_of, own_rows]
        theirs = buf.at[part_of, y_rows]
        arrived(theirs, ag_r.at[l, op, 1])
        third = remote(theirs, theirs, ag_s.at[l, op, 2], ag_r.at[l, op, 2], core_id)
        third.start()
        arrived(mine, ag_r.at[l, op, 0])
        arrived(mine, ag_r.at[l, op, 2])
        arrived(mine, ag_s.at[l, op, 0])
        arrived(mine, ag_s.at[l, op, 1])
        arrived(theirs, ag_s.at[l, op, 2])

    def scatter_start(product, l, op):
        slot = op % 2

        def send_tile(j, carry):
            cols = pl.ds(pl.multiple_of(j * COLS, COLS), COLS)
            sendbuf[:, cols] = product(pl.multiple_of((1 - c) * 2 * R, 16), cols).astype(BF)
            return carry

        lax.fori_loop(0, D // COLS, send_tile, 0)
        first = remote(sendbuf, crecv.at[slot], rs_s.at[l, op, 0], rs_r.at[l, op, 0], core_id)
        first.start()

        def own_tile(j, carry):
            cols = pl.ds(pl.multiple_of(j * COLS, COLS), COLS)
            part[:, cols] = product(pl.multiple_of(c * 2 * R, 16), cols)
            return carry

        lax.fori_loop(0, D // COLS, own_tile, 0)
        arrived(sendbuf, rs_r.at[l, op, 0])
        other = pl.ds(pl.multiple_of((1 - y) * R, 16), R)
        ysend[...] = (part[other] + crecv[slot, other].astype(F32)).astype(BF)
        remote(ysend, yrecv.at[slot], rs_s.at[l, op, 1], rs_r.at[l, op, 1], y_id).start()

    def scatter_finish(l, op):
        slot = op % 2
        mine = pl.ds(pl.multiple_of(y * R, 16), R)
        arrived(sendbuf, rs_s.at[l, op, 0])
        arrived(ysend, rs_s.at[l, op, 1])
        arrived(ysend, rs_r.at[l, op, 1])
        return part[mine] + crecv[slot, mine].astype(F32) + yrecv[slot].astype(F32)

    FD, UP, OUT = 0, FF, FF + D
    QKV = OUT + HD
    KS = grads.shape[1] // SUB
    HALF = SUB // 2
    middle = (b == 1) | (b == 2)
    end = jnp.logical_not(middle)
    inner_id = (s, jnp.where(b == 0, 1, 2), t)
    outer_id = (s, jnp.where(b == 1, 0, 3), t)
    partner_id = (s, jnp.where(b == 1, 2, 1), t)
    mine_at = jnp.where(b == 1, 0, HALF)
    other_at = HALF - mine_at

    def sub_rows(k):
        return pl.ds(pl.multiple_of(k * SUB, 16), SUB)

    def half_rows(k, at):
        return pl.ds(pl.multiple_of(k * SUB + at, 16), HALF)

    def send_grads(l, lo, hi):
        if not chain:
            return

        @pl.when(l != s)
        def _():
            def one(k, carry):
                rows = sub_rows(k)
                remote(grads.at[l, rows], gx.at[rows], gx_s.at[k], gx_r.at[k], x_id).start()
                return carry

            lax.fori_loop(lo, hi, one, 0)

    def step1(k, carry):
        rows = sub_rows(k)
        arrived(gx.at[rows], gx_r.at[k])
        grads[s, rows] = (grads[s, rows].astype(F32) + gx[rows].astype(F32)).astype(BF)

        @pl.when(end)
        def _():
            remote(grads.at[s, rows], gz.at[rows], gz_s.at[0, k], gz_r.at[0, k], inner_id).start()

        return carry

    def step2(k, carry):
        @pl.when(middle)
        def _():
            rows = sub_rows(k)
            arrived(gz.at[rows], gz_r.at[0, k])
            grads[s, rows] = (grads[s, rows].astype(F32) + gz[rows].astype(F32)).astype(BF)
            other = grads.at[s, half_rows(k, other_at)]
            remote(other, gpart.at[k], gz_s.at[0, k], gz_r.at[1, k], partner_id).start()

        return carry

    def step3(k, carry):
        @pl.when(middle)
        def _():
            rows = half_rows(k, mine_at)
            arrived(gpart.at[k], gz_r.at[1, k])
            grads[s, rows] = (grads[s, rows].astype(F32) + gpart[k].astype(F32)).astype(BF)
            done = grads.at[s, rows]
            remote(done, gfin.at[k], gz_s.at[1, k], gz_r.at[2, k], partner_id).start()
            remote(done, gz.at[rows], gz_s.at[2, k], gz_r.at[0, k], outer_id).start()
            pltpu.make_async_copy(done, g_out.at[rows], g_loc.at[0, k]).start()

        return carry

    def step4(k, carry):
        @pl.when(middle)
        def _():
            rows = half_rows(k, other_at)
            arrived(gfin.at[k], gz_r.at[2, k])
            remote(gfin.at[k], gz.at[rows], gz_s.at[3, k], gz_r.at[1, k], outer_id).start()
            pltpu.make_async_copy(gfin.at[k], g_out.at[rows], g_loc.at[1, k]).start()

        return carry

    def step5(k, carry):
        @pl.when(end)
        def _():
            rows = sub_rows(k)
            arrived(gz.at[half_rows(k, 0)], gz_r.at[0, k])
            arrived(gz.at[half_rows(k, HALF)], gz_r.at[1, k])
            pltpu.make_async_copy(gz.at[rows], g_out.at[rows], g_loc.at[0, k]).start()

        return carry

    steps = (step1, step2, step3, step4, step5)
    last_point = len(TAKEN[0]) + len(steps) - 1

    def progress(point, live):
        if not chain:
            return

        def taken(p):
            if p < 0:
                return 0
            p = min(p, len(TAKEN[0]) - 1)
            return jnp.where(live, jnp.where(s == 0, TAKEN[0][p], TAKEN[1][p]), 0)

        for i, step in enumerate(steps):
            lax.fori_loop(taken(point - i - 1), taken(point - i), step, 0)

    def finish_grads():
        def one(k, carry):
            rows = sub_rows(k)
            half = grads.at[1 - s, half_rows(k, 0)]
            arrived(grads.at[1 - s, rows], gx_s.at[k])

            @pl.when(end)
            def _():
                arrived(grads.at[s, rows], gz_s.at[0, k])
                arrived(g_out.at[rows], g_loc.at[0, k])

            @pl.when(middle)
            def _():
                for j in range(4):
                    arrived(half, gz_s.at[j, k])
                for j in range(2):
                    arrived(g_out.at[half_rows(k, 0)], g_loc.at[j, k])

            return carry

        lax.fori_loop(0, KS, one, 0)

    def q_rows(h):
        return pl.ds(pl.multiple_of(h * HEAD, HEAD), HEAD)

    def forward(l):
        weights_here(l, 0)
        weights_here(l, 1)
        xh, r = normed(xres[...])
        xh1[l] = xh
        r1[l] = r
        a_all[l, own_rows] = (xh * sml[l, 0:1]).astype(BF)
        gather_start(a_all, l, 0)
        weights_here(l, 2)
        gather_finish(a_all, l, 0)

        def project(i, carry):
            rows = pl.ds(pl.multiple_of(i * HD, HEAD), HD)
            qkvb[l, rows] = mm_nt(wq[l, rows], a_all[l]).astype(BF)
            return carry

        def project_normed(i, carry):
            rows = pl.ds(pl.multiple_of(i * HD, HEAD), HD)
            v = mm_nt(wq[l, rows], a_all[l])
            for h in range(NH):
                u = v[h * HEAD : (h + 1) * HEAD]
                u = u - jnp.mean(u, axis=0, keepdims=True)
                rr = lax.rsqrt(jnp.mean(u * u, axis=0, keepdims=True) + EPS)
                u = u * rr
                at = pl.ds(pl.multiple_of(i * HD + h * HEAD, HEAD), HEAD)
                qkh[l, at] = u
                qkr[l, i, pl.ds(h, 1)] = rr
                scale = jnp.where(i == 0, HEAD**-0.5, 1.0).astype(F32)
                gain = jnp.where(i == 0, qkg[l, :, h : h + 1], qkg[l, :, NH + h : NH + h + 1])
                qkvb[l, at] = ((u * gain).astype(BF).astype(F32) * scale).astype(BF)
            return carry

        lax.fori_loop(0, 2, project_normed, 0)
        project(2, 0)

        def head(h, carry):
            q_t = qkvb[l, q_rows(h)]
            k_rows = qkvb[l, q_rows(NH + h)].astype(F32).T.astype(BF)
            v_t = qkvb[l, q_rows(2 * NH + h)]
            rows_buf[0, :, :HEAD] = k_rows

            def block(i, total):
                at = pl.ds(pl.multiple_of(i * KEY_BLOCK, KEY_BLOCK), KEY_BLOCK)
                sc = mm(rows_buf[0, at, :HEAD], q_t)
                e = jnp.where(segc_ref[at] == segr_ref[...], jnp.exp(sc), 0.0)
                e_buf[at] = e.astype(BF)
                return total + jnp.sum(e, axis=0, keepdims=True)

            total = lax.fori_loop(0, NB, block, jnp.zeros((1, N), F32))
            lse[l, pl.ds(h, 1)] = jnp.log(total)
            o_t[l, q_rows(h)] = (mm(v_t, e_buf[...]) * (1.0 / total)).astype(BF)
            return carry

        lax.fori_loop(0, NH, head, 0)
        rows_buf[1, :, :HD] = o_t[l].astype(F32).T.astype(BF)
        weights_here(l, 3)
        scatter_start(lambda at, cols: mm(rows_buf[1, pl.ds(at, 2 * R), :HD], wo[l, :, cols]), l, 0)
        residual = xres[...] + scatter_finish(l, 0)
        xres[...] = residual
        xh, r = normed(residual)
        xh2[l] = xh
        r2[l] = r
        b_all[l, own_rows] = (xh * sml[l, 1:2]).astype(BF)
        gather_start(b_all, l, 1)
        weights_here(l, 4)
        gather_finish(b_all, l, 1)

        def hidden(i, carry):
            rows = pl.ds(pl.multiple_of(lax.rem(i, 4) * R, 16), R)
            cols = pl.ds(pl.multiple_of((i // 4) * COLS, COLS), COLS)
            u = mm(b_all[l, rows], wu[l, :, cols])
            cdf = 0.5 * (1.0 + lax.erf(u * 0.7071067811865476))
            pdf = jnp.exp(-0.5 * u * u) * 0.3989422804014327
            g_all[l, rows, cols] = (u * cdf).astype(BF)
            gp_all[l, rows, cols] = (cdf + u * pdf).astype(BF)
            return carry

        lax.fori_loop(0, 4 * (FF // COLS), hidden, 0)
        weights_here(l, 5)
        scatter_start(lambda at, cols: mm(g_all[l, pl.ds(at, 2 * R)], wd[l, :, cols]), l, 1)
        out = xres[...] + scatter_finish(l, 1)
        rounded = out.astype(BF)
        ybuf[l] = rounded
        xres[...] = rounded.astype(F32)

    xres[...] = x_ref[...].astype(F32)

    def forward_step(l, carry):
        forward(l)
        return carry

    lax.fori_loop(0, 2, forward_step, 0)
    y_move = remote(ybuf.at[1 - s], ylo, x_s.at[0], x_r.at[0], x_id)
    y_move.start()

    def backward(l):
        live = l == 0
        dm_all[0, own_rows] = xres[...].astype(BF)
        gather_start(dm_all, l, 2)
        progress(0, live)
        gather_finish(dm_all, l, 2)

        def hidden(i, carry):
            rows = pl.ds(pl.multiple_of(lax.rem(i, 4) * R, 16), R)
            cols = pl.ds(pl.multiple_of((i // 4) * COLS, COLS), COLS)
            dg = mm_nt(dm_all[0, rows], wd[l, cols])
            gp_all[l, rows, cols] = (dg * gp_all[l, rows, cols].astype(F32)).astype(BF)
            return carry

        lax.fori_loop(0, 4 * (FF // COLS), hidden, 0)
        progress(1, live)
        scatter_start(lambda at, cols: mm_nt(gp_all[l, pl.ds(at, 2 * R)], wu[l, cols]), l, 2)

        def hidden_grads(i, carry):
            cols = pl.ds(pl.multiple_of(i * COLS, COLS), COLS)
            grads[l, pl.ds(pl.multiple_of(FD + i * COLS, COLS), COLS)] = mm_tn(
                g_all[l, :, cols], dm_all[0]
            ).astype(BF)
            grads[l, pl.ds(pl.multiple_of(UP + i * COLS, COLS), COLS)] = mm_tn(
                b_all[l, :, cols], gp_all[l]
            ).astype(BF)
            return carry

        lax.fori_loop(0, FF // COLS, hidden_grads, 0)
        send_grads(l, 0, OUT // SUB)
        progress(2, live)
        db = scatter_finish(l, 2)
        gains[l, 1:2] = jnp.sum(db * xh2[l], axis=0, keepdims=True)
        dh = xres[...] + normed_back(db, sml[l, 1:2], xh2[l], r2[l])
        xres[...] = dh
        da_all[0, own_rows] = dh.astype(BF)
        gather_start(da_all, l, 3)
        progress(3, live)
        gather_finish(da_all, l, 3)
        dot_buf[...] = mm_nt(wo[l], da_all[0]).astype(BF)
        grads[l, OUT:QKV] = mm(o_t[l], da_all[0]).astype(BF)
        send_grads(l, OUT // SUB, QKV // SUB)
        progress(4, live)

        def head(h, carry):
            q_t = qkvb[l, q_rows(h)]
            k_t = qkvb[l, q_rows(NH + h)]
            v_t = qkvb[l, q_rows(2 * NH + h)]
            rows_buf[0, :, :HEAD] = k_t.astype(F32).T.astype(BF)
            rows_buf[1, :, :HEAD] = v_t.astype(F32).T.astype(BF)
            do_t = dot_buf[q_rows(h)]
            delta = jnp.sum(do_t.astype(F32) * o_t[l, q_rows(h)].astype(F32), axis=0, keepdims=True)
            log_total = lse[l, pl.ds(h, 1)]

            def block(i, carry):
                at = pl.ds(pl.multiple_of(i * KEY_BLOCK, KEY_BLOCK), KEY_BLOCK)
                sc = mm(rows_buf[0, at, :HEAD], q_t)
                p = jnp.where(segc_ref[at] == segr_ref[...], jnp.exp(sc - log_total), 0.0)
                dp = mm(rows_buf[1, at, :HEAD], do_t)
                e_buf[at] = p.astype(BF)
                d_buf[at] = (p * (dp - delta)).astype(BF)
                return carry

            lax.fori_loop(0, NB, block, 0)
            dqkv_t[q_rows(2 * NH + h)] = mm_nt(do_t, e_buf[...]).astype(BF)
            dk = mm_nt(q_t, d_buf[...])
            dq = mm(k_t, d_buf[...]) * (HEAD**-0.5)
            for i, dv in ((0, dq), (1, dk)):
                at = q_rows(i * NH + h)
                dv = dv.astype(BF).astype(F32)
                uh = qkh[l, at]
                lanes = lax.broadcasted_iota(jnp.int32, (HEAD, 128), 1) == i * NH + h
                hgains[l] = jnp.where(lanes, jnp.sum(dv * uh, axis=1, keepdims=True), hgains[l])
                gain = gains_of(l, i, h)
                g = dv * gain
                back = g - jnp.mean(g, axis=0, keepdims=True) - uh * jnp.mean(g * uh, axis=0, keepdims=True)
                dqkv_t[at] = (qkr[l, i, pl.ds(h, 1)] * back).astype(BF)
            return carry

        def gains_of(l, i, h):
            out = qkg[l, :, i * NH : i * NH + 1]
            for k in range(1, NH):
                out = jnp.where(h == k, qkg[l, :, i * NH + k : i * NH + k + 1], out)
            return out

        hgains[l] = jnp.zeros((HEAD, 128), F32)
        gains[l] = jnp.where(lax.broadcasted_iota(jnp.int32, (8, D), 0) == 1, gains[l], 0.0)
        lax.fori_loop(0, NH, head, 0)
        progress(5, live)
        rows_buf[0] = dqkv_t[...].astype(F32).T.astype(BF)
        scatter_start(lambda at, cols: mm(rows_buf[0, pl.ds(at, 2 * R)], wq[l, :, cols]), l, 3)
        grads[l, QKV:] = mm(dqkv_t[...], a_all[l]).astype(BF)
        send_grads(l, QKV // SUB, KS)
        progress(6, live)
        da = scatter_finish(l, 3)
        gains[l, 0:1] = jnp.sum(da * xh1[l], axis=0, keepdims=True)
        dx = xres[...] + normed_back(da, sml[l, 0:1], xh1[l], r1[l])
        rounded = dx.astype(BF)
        dxbuf[l] = rounded
        kept = jnp.where(l == 0, dx, rounded.astype(F32))
        xres[...] = rounded.astype(F32)

        @pl.when(l == s)
        def _():
            ig_out[s] = kept

        @pl.when(l != s)
        def _():
            remote(dxbuf.at[1 - s], dxlo, x_s.at[1], x_r.at[1], x_id).start()
            if chain:
                remote(gains.at[1 - s], gains_x, sm_s.at[0], sm_r.at[0], x_id).start()
                remote(hgains.at[1 - s], hgains_x, sm_s.at[1], sm_r.at[1], x_id).start()

    xres[...] = ct_ref[...].astype(F32)

    def backward_step(i, carry):
        backward(1 - i)
        return carry

    lax.fori_loop(0, 2, backward_step, 0)
    progress(LAYER_POINTS, True)
    if chain:
        arrived(gains_x, sm_r.at[0])
        arrived(hgains_x, sm_r.at[1])
        gains_z[b] = gains[s] + gains_x[...]
        hgains_z[b] = hgains[s] + hgains_x[...]
        for i, peer in enumerate(z_ids):
            remote(gains_z.at[b], gains_z.at[b], sm_s.at[2 + i], sm_r.at[2 + i], peer).start()
            remote(hgains_z.at[b], hgains_z.at[b], sm_s.at[5 + i], sm_r.at[5 + i], peer).start()
        progress(LAYER_POINTS + 1, True)
        for i in range(3):
            arrived(gains_x, sm_r.at[2 + i])
            arrived(hgains_x, sm_r.at[5 + i])
        gh_out[...] = hgains_z[0] + hgains_z[1] + hgains_z[2] + hgains_z[3]
        gains_t[t] = gains_z[0] + gains_z[1] + gains_z[2] + gains_z[3]
        for i, peer in enumerate((core_id, y_id, diag_id)):
            remote(gains_t.at[t], gains_t.at[t], sm_s.at[8 + i], sm_r.at[8 + i], peer).start()
        progress(LAYER_POINTS + 2, True)
        for i in range(3):
            arrived(gains_x, sm_r.at[8 + i])
        gg_out[...] = gains_t[0] + gains_t[1] + gains_t[2] + gains_t[3]
        for point in range(LAYER_POINTS + 3, last_point):
            progress(point, True)
    else:
        g_out[...] = grads[...]
        gg_out[...] = gains[...]
        gh_out[...] = hgains[...]
    y_move.wait()
    y_out[s] = ybuf[s]
    y_out[1 - s] = ylo[...]
    for i, (src, dst) in enumerate(moves):
        arrived(dst.at[s], w_send.at[i])
    arrived(dxlo, x_s.at[1])
    arrived(dxlo, x_r.at[1])
    ig_out[1 - s] = dxlo[...].astype(F32)
    if chain:
        finish_grads()
        for i in range(2, 5):
            arrived(gains_x, sm_s.at[i])
            arrived(hgains_x, sm_s.at[3 + i])
            arrived(gains_x, sm_s.at[6 + i])
        arrived(gains_x, sm_s.at[0])
        arrived(hgains_x, sm_s.at[1])


def fused(chain, x, ct, segc, segr, small, qk_gain, wq, wo, wu, wd):
    R, D = x.shape
    N = 4 * R
    QD, HD, FF = wq.shape[0], wo.shape[0], wu.shape[1]
    NH = HD // HEAD
    vmem = pl.BlockSpec(memory_space=pltpu.VMEM)
    hbm = pl.BlockSpec(memory_space=pl.ANY)
    shape = jax.ShapeDtypeStruct
    V = pltpu.VMEM
    dma = pltpu.SemaphoreType.DMA
    G = FF + D + HD + QD
    KS = G // SUB
    ahead = () if chain else (2,)
    extra = [
        V((G, D), BF), V((G, D), BF), V((KS, SUB // 2, D), BF), V((KS, SUB // 2, D), BF),
        V((8, D), F32), V((HEAD, 128), F32), V((4, 8, D), F32), V((4, HEAD, 128), F32), V((4, 8, D), F32),
        dma((KS,)), dma((KS,)), dma((4, KS)), dma((3, KS)), dma((2, KS)), dma((11,)), dma((11,)),
    ]
    if not chain:
        extra = [V((8, 128), F32)] * 9 + [dma((1,))] * 7
    return pl.pallas_call(
        functools.partial(body, chain),
        out_shape=(
            shape((2, R, D), BF),
            shape((2, R, D), F32),
            shape(ahead + (G, D), BF),
            shape(ahead + (8, D), F32),
            shape(ahead + (HEAD, 128), F32),
        ),
        in_specs=[vmem] * 4 + [hbm] * 6,
        out_specs=(vmem, vmem, hbm if chain else vmem, vmem, vmem),
        scratch_shapes=[
            V((2, QD, D), BF), V((2, HD, D), BF), V((2, D, FF), BF), V((2, FF, D), BF),
            V((2, 8, D), F32), V((2, HEAD, 128), F32),
            V((R, D), F32), V((2, R, D), F32), V((2, R, 1), F32), V((2, R, D), F32), V((2, R, 1), F32),
            V((2, N, D), BF), V((2, N, D), BF), V((1, N, D), BF), V((1, N, D), BF),
            V((2, 2 * HD, N), F32), V((2, 2, 8, N), F32), V((2, QD, N), BF), V((2, 8, N), F32),
            V((2, HD, N), BF), V((2, N, FF), BF), V((2, N, FF), BF),
            V((2, N, QD), BF), V((2 * R, D), F32), V((2 * R, D), BF), V((R, D), BF),
            V((2, 2 * R, D), BF), V((2, R, D), BF),
            V((N, N), BF), V((N, N), BF), V((HD, N), BF), V((QD, N), BF),
            V((2, R, D), BF), V((2, R, D), BF), V((R, D), BF), V((R, D), BF),
            V((2, G, D), BF), V((2, 8, D), F32), V((2, HEAD, 128), F32),
            dma((6,)), dma((6,)), dma((2, 6)),
            dma((2, 4, 3)), dma((2, 4, 3)), dma((2, 4, 2)), dma((2, 4, 2)), dma((2,)), dma((2,)),
        ] + extra,
        name="layers",
        compiler_params=pltpu.CompilerParams(
            collective_id=0, has_side_effects=True, vmem_limit_bytes=63 * 2**20
        ),
    )(x, ct, segc, segr, small, qk_gain, wq, wo, wu, wd)


def shards(
    patches, cotangent, image_lengths, attn_gain, qkv_weight, query_gain, key_gain, out_weight,
    mlp_gain, up_weight, down_weight,
):
    s = lax.axis_index("section")
    _, own, D = patches.shape
    seq_len = 4 * own
    R = ceil_to(own, 16)
    N = 4 * R
    HD = out_weight.shape[1]
    NH = HD // HEAD
    pad = ((0, R - own), (0, 0))
    x = jnp.pad(lax.dynamic_index_in_dim(patches, s, 0, keepdims=False), pad)
    ct = jnp.pad(lax.dynamic_index_in_dim(cotangent, s, 0, keepdims=False), pad)
    lengths = lax.dynamic_index_in_dim(image_lengths, s, 0, keepdims=False)[0]
    bounds = jnp.cumsum(lengths, dtype=jnp.int32)
    places = jnp.arange(seq_len, dtype=jnp.int32)
    seg = jnp.sum((places[:, None] >= bounds[None, :]).astype(jnp.int32), axis=-1)
    seg = seg.reshape(2, 2, own).transpose(1, 0, 2).reshape(4, own)
    seg = jnp.pad(seg, ((0, 0), (0, R - own)), constant_values=-1).reshape(N)
    small = jnp.zeros((8, D), F32).at[0].set(attn_gain[0].astype(F32)).at[1].set(mlp_gain[0].astype(F32))
    qk_gain = jnp.concatenate([query_gain[0], key_gain[0]], axis=0).astype(F32).T
    qk_gain = jnp.pad(qk_gain, ((0, 0), (0, 128 - 2 * NH)))
    wq = qkv_weight[0].reshape(D, 3 * HD).T
    chain = lax.axis_size("batch") == 4
    y, ig, g, gg, gh = fused(
        chain, x, ct, seg[:, None], seg[None, :], small, qk_gain, wq, out_weight[0], up_weight[0],
        down_weight[0],
    )
    if not chain:
        theirs = lax.ppermute(g[1 - s], "section", [(0, 1), (1, 0)])
        g = lax.psum((g[s].astype(F32) + theirs.astype(F32)).astype(BF), "batch")
        gg = lax.psum(gg, ("section", "batch", "tensor"))[s]
        gh = lax.psum(gh, ("section", "batch"))[s]
    FF = up_weight.shape[2]
    gd, gu, go, gq = (g[:FF], g[FF : FF + D], g[FF + D : FF + D + HD], g[FF + D + HD :])
    gh = gh[:, : 2 * NH].T.reshape(2, NH, HEAD)
    return (
        y[:, :own][None],
        ig[:, :own][None],
        gg[0][None],
        gq.astype(F32).T.reshape(D, 3, HD)[None],
        gh[0][None],
        gh[1][None],
        go.astype(F32)[None],
        gg[1][None],
        gu.astype(F32)[None],
        gd.astype(F32)[None],
    )


def solution(mesh):
    return jax.shard_map(
        shards,
        mesh=mesh,
        in_specs=(
            P(None, ("batch", "tensor"), None),
            P(None, ("batch", "tensor"), None),
            P(None, "batch", None),
            P("section", None),
            P("section", None, None, "tensor"),
            P("section", "tensor", None),
            P("section", "tensor", None),
            P("section", "tensor", None),
            P("section", None),
            P("section", None, "tensor"),
            P("section", "tensor", None),
        ),
        out_specs=(
            P("section", None, ("batch", "tensor"), None),
            P("section", None, ("batch", "tensor"), None),
            P("section", None),
            P("section", None, None, "tensor"),
            P("section", "tensor", None),
            P("section", "tensor", None),
            P("section", "tensor", None),
            P("section", None),
            P("section", None, "tensor"),
            P("section", "tensor", None),
        ),
        check_vma=False,
    )
```

```python
import functools

import jax
import jax.numpy as jnp
from jax import lax
from jax.experimental import pallas as pl
from jax.experimental.pallas import tpu as pltpu
from jax.sharding import PartitionSpec as P

HEAD = 64
EPS = 1e-06
MESH = pl.DeviceIdType.MESH
BF = jnp.bfloat16
F32 = jnp.float32
KEY_BLOCK = 64
COLS = 256
SUB = 192
CHUNKS = 2
TAKEN = ((0, 0, 0, 1, 2, 3, 5, 7, 9, 10, 11, 12), (2, 3, 4, 6, 7, 9, 10, 11, 12, 12, 12, 12))
LAYER_POINTS = 7


def ceil_to(n, m):
    return -(-n // m) * m


def chunks_of(rows):
    step = max(32, rows // CHUNKS // 32 * 32)
    starts = [i * step for i in range(CHUNKS) if i * step < rows]
    return [(a, b - a) for a, b in zip(starts, starts[1:] + [rows])]


def mm(a, b):
    return lax.dot_general(a, b, (((1,), (0,)), ((), ())), preferred_element_type=F32)


def mm_nt(a, b):
    return lax.dot_general(a, b, (((1,), (1,)), ((), ())), preferred_element_type=F32)


def mm_tn(a, b):
    return lax.dot_general(a, b, (((0,), (0,)), ((), ())), preferred_element_type=F32)


def normed(v):
    centre = v - jnp.mean(v, axis=-1, keepdims=True)
    r = lax.rsqrt(jnp.mean(centre * centre, axis=-1, keepdims=True) + EPS)
    return centre * r, r


def normed_back(dv, gain, xh, r):
    g = dv * gain
    return r * (g - jnp.mean(g, axis=-1, keepdims=True) - xh * jnp.mean(g * xh, axis=-1, keepdims=True))


def body(
    chain,
    x_ref, ct_ref, segc_ref, segr_ref, sml_in, qkg_in, wq_in, wo_in, wu_in, wd_in,
    y_out, ig_out, g_out, gg_out, gh_out,
    wq, wo, wu, wd, sml, qkg,
    xres, xh1, r1, xh2, r2,
    a_all, b_all, dm_all, da_all,
    qkh, qkr, qkvb, lse, o_t, g_all, gp_all,
    rows_buf, part, sendbuf, ysend, crecv, yrecv,
    e_buf, d_buf, dot_buf, dqkv_t,
    ybuf, dxbuf, ylo, dxlo,
    grads, gains, hgains,
    w_loc, w_send, w_recv, wz_s, wz_r, ag_s, ag_r, rs_s, rs_r, x_s, x_r,
    gx, gz, gpart, gfin, gains_x, hgains_x, gains_z, hgains_z, gains_t,
    gx_s, gx_r, gz_s, gz_r, g_loc, sm_s, sm_r,
):
    s, b, t = lax.axis_index("section"), lax.axis_index("batch"), lax.axis_index("tensor")
    y, c = t // 2, lax.rem(t, 2)
    core_id = (s, b, y * 2 + 1 - c)
    y_id = (s, b, (1 - y) * 2 + c)
    x_id = (1 - s, b, t)
    R, D = x_ref.shape
    N = 4 * R
    FF = wu.shape[2]
    HD = wo.shape[1]
    NH = HD // HEAD
    NB = N // KEY_BLOCK
    pos = c * 2 + y
    ypos = c * 2 + 1 - y
    CH = chunks_of(R)

    def block_rows(k, at):
        off, n = CH[k]
        return pl.ds(pl.multiple_of(4 * off + at * n, 16), n)

    def own_rows(k):
        return pl.ds(CH[k][0], CH[k][1])

    diag_id = (s, b, (1 - y) * 2 + 1 - c)
    z_ids = [(s, lax.rem(b + k, 4), t) for k in (1, 2, 3)] if chain else []
    barrier = pltpu.get_barrier_semaphore()
    for peer in [core_id, y_id, diag_id, x_id] + z_ids:
        pl.semaphore_signal(barrier, inc=1, device_id=peer, device_id_type=MESH)
    pl.semaphore_wait(barrier, 4 + len(z_ids))

    def remote(src, dst, ss, rs, peer):
        return pltpu.make_async_remote_copy(
            src_ref=src, dst_ref=dst, send_sem=ss, recv_sem=rs, device_id=peer, device_id_type=MESH
        )

    def arrived(ref, sem):
        pltpu.make_async_copy(ref, ref, sem).wait()

    moves = ((sml_in, sml), (qkg_in, qkg), (wq_in, wq), (wo_in, wo), (wu_in, wu), (wd_in, wd))
    pair_id = (s, b + 1 - 2 * lax.rem(b, 2), t)
    near = lax.rem(b, 2)
    blocks = []
    for i in range(2, 6):
        rows = moves[i][0].shape[0]
        step = min(rows, 2 * SUB if i > 3 else SUB)
        blocks += [(i, at, step) for at in range(0, rows, step)]

    def half_block(ref, j, h):
        _, at, n = blocks[j]
        return ref.at[pl.ds(pl.multiple_of(at + h * (n // 2), 16), n // 2)]

    def send_block(j):
        src, dst = moves[blocks[j][0]]
        if chain:
            remote(half_block(src, j, near), half_block(dst.at[s], j, near), w_send.at[j], w_recv.at[j], x_id).start()
        else:
            _, at, n = blocks[j]
            remote(src.at[at : at + n], dst.at[s, at : at + n], w_send.at[j], w_recv.at[j], x_id).start()

    def forward_blocks(lo, hi):
        if chain:
            for j in range(lo, hi):
                got = half_block(moves[blocks[j][0]][1].at[1 - s], j, near)
                arrived(got, w_recv.at[j])
                remote(got, got, wz_s.at[j], wz_r.at[j], pair_id).start()

    for i, (src, dst) in enumerate(moves):
        if i < 2:
            remote(src, dst.at[s], w_send.at[len(blocks) + i], w_recv.at[len(blocks) + i], x_id).start()
        else:
            for j in range(len(blocks)):
                if blocks[j][0] == i:
                    send_block(j)
        pltpu.make_async_copy(src, dst.at[s], w_loc.at[i]).start()

    def weights_here(l, i):
        src, dst = moves[i]

        @pl.when(l == s)
        def _():
            pltpu.make_async_copy(src, dst.at[s], w_loc.at[i]).wait()

        @pl.when(l != s)
        def _():
            if i < 2:
                arrived(dst.at[1 - s], w_recv.at[len(blocks) + i])
            for j in range(len(blocks)):
                if blocks[j][0] == i:
                    if chain:
                        arrived(half_block(dst.at[1 - s], j, 1 - near), wz_r.at[j])
                    else:
                        _, at, n = blocks[j]
                        arrived(dst.at[1 - s, at : at + n], w_recv.at[j])

    def finish_weights():
        for i in range(2):
            arrived(moves[i][1].at[s], w_send.at[len(blocks) + i])
        for j in range(len(blocks)):
            i, at, n = blocks[j]
            if chain:
                arrived(half_block(moves[i][1].at[s], j, near), w_send.at[j])
                arrived(half_block(moves[i][1].at[1 - s], j, near), wz_s.at[j])
            else:
                arrived(moves[i][1].at[s, at : at + n], w_send.at[j])

    def gather_start(buf, slot, l, op, k):
        mine = buf.at[slot, block_rows(k, pos)]
        remote(mine, mine, ag_s.at[l, op, 0, k], ag_r.at[l, op, 0, k], core_id).start()
        remote(mine, mine, ag_s.at[l, op, 1, k], ag_r.at[l, op, 1, k], y_id).start()

    def gather_pass(buf, slot, l, op, k):
        theirs = buf.at[slot, block_rows(k, ypos)]
        arrived(theirs, ag_r.at[l, op, 1, k])
        remote(theirs, theirs, ag_s.at[l, op, 2, k], ag_r.at[l, op, 2, k], core_id).start()

    def gather_finish(buf, slot, l, op, k):
        mine = buf.at[slot, block_rows(k, pos)]
        arrived(mine, ag_r.at[l, op, 0, k])
        arrived(mine, ag_r.at[l, op, 2, k])
        arrived(mine, ag_s.at[l, op, 0, k])
        arrived(mine, ag_s.at[l, op, 1, k])
        arrived(mine, ag_s.at[l, op, 2, k])

    def pair_rows(k):
        return pl.ds(2 * CH[k][0], 2 * CH[k][1])

    def scatter_start(product, l, op, k):
        slot = op % 2
        off, n = CH[k]

        def send_tile(j, carry):
            cols = pl.ds(pl.multiple_of(j * COLS, COLS), COLS)
            at = pl.ds(pl.multiple_of(4 * off + (1 - c) * 2 * n, 16), 2 * n)
            sendbuf[pair_rows(k), cols] = product(at, cols).astype(BF)
            return carry

        lax.fori_loop(0, D // COLS, send_tile, 0)
        mine = sendbuf.at[pair_rows(k)]
        remote(mine, crecv.at[slot, pair_rows(k)], rs_s.at[l, op, 0, k], rs_r.at[l, op, 0, k], core_id).start()

        def own_tile(j, carry):
            cols = pl.ds(pl.multiple_of(j * COLS, COLS), COLS)
            at = pl.ds(pl.multiple_of(4 * off + c * 2 * n, 16), 2 * n)
            part[pair_rows(k), cols] = product(at, cols)
            return carry

        lax.fori_loop(0, D // COLS, own_tile, 0)
        arrived(mine, rs_r.at[l, op, 0, k])
        other = pl.ds(pl.multiple_of(2 * off + (1 - y) * n, 16), n)
        ysend[own_rows(k)] = (part[other] + crecv[slot, other].astype(F32)).astype(BF)
        remote(
            ysend.at[own_rows(k)], yrecv.at[slot, own_rows(k)], rs_s.at[l, op, 1, k], rs_r.at[l, op, 1, k], y_id
        ).start()

    def scatter_finish(l, op, k):
        slot = op % 2
        off, n = CH[k]
        mine = pl.ds(pl.multiple_of(2 * off + y * n, 16), n)
        arrived(sendbuf.at[pair_rows(k)], rs_s.at[l, op, 0, k])
        arrived(ysend.at[own_rows(k)], rs_s.at[l, op, 1, k])
        arrived(ysend.at[own_rows(k)], rs_r.at[l, op, 1, k])
        return part[mine] + crecv[slot, mine].astype(F32) + yrecv[slot, own_rows(k)].astype(F32)

    FD, UP, OUT = 0, FF, FF + D
    QKV = OUT + HD
    KS = grads.shape[1] // SUB
    HALF = SUB // 2
    middle = (b == 1) | (b == 2)
    end = jnp.logical_not(middle)
    inner_id = (s, jnp.where(b == 0, 1, 2), t)
    outer_id = (s, jnp.where(b == 1, 0, 3), t)
    partner_id = (s, jnp.where(b == 1, 2, 1), t)
    mine_at = jnp.where(b == 1, 0, HALF)
    other_at = HALF - mine_at

    def sub_rows(k):
        return pl.ds(pl.multiple_of(k * SUB, 16), SUB)

    def half_rows(k, at):
        return pl.ds(pl.multiple_of(k * SUB + at, 16), HALF)

    def send_grads(l, lo, hi):
        if not chain:
            return

        @pl.when(l != s)
        def _():
            def one(k, carry):
                rows = sub_rows(k)
                remote(grads.at[l, rows], gx.at[rows], gx_s.at[k], gx_r.at[k], x_id).start()
                return carry

            lax.fori_loop(lo, hi, one, 0)

    def step1(k, carry):
        rows = sub_rows(k)
        arrived(gx.at[rows], gx_r.at[k])
        grads[s, rows] = (grads[s, rows].astype(F32) + gx[rows].astype(F32)).astype(BF)

        @pl.when(end)
        def _():
            remote(grads.at[s, rows], gz.at[rows], gz_s.at[0, k], gz_r.at[0, k], inner_id).start()

        return carry

    def step2(k, carry):
        @pl.when(middle)
        def _():
            rows = sub_rows(k)
            arrived(gz.at[rows], gz_r.at[0, k])
            grads[s, rows] = (grads[s, rows].astype(F32) + gz[rows].astype(F32)).astype(BF)
            other = grads.at[s, half_rows(k, other_at)]
            remote(other, gpart.at[k], gz_s.at[0, k], gz_r.at[1, k], partner_id).start()

        return carry

    def step3(k, carry):
        @pl.when(middle)
        def _():
            rows = half_rows(k, mine_at)
            arrived(gpart.at[k], gz_r.at[1, k])
            grads[s, rows] = (grads[s, rows].astype(F32) + gpart[k].astype(F32)).astype(BF)
            done = grads.at[s, rows]
            remote(done, gfin.at[k], gz_s.at[1, k], gz_r.at[2, k], partner_id).start()
            remote(done, gz.at[rows], gz_s.at[2, k], gz_r.at[0, k], outer_id).start()
            pltpu.make_async_copy(done, g_out.at[rows], g_loc.at[0, k]).start()

        return carry

    def step4(k, carry):
        @pl.when(middle)
        def _():
            rows = half_rows(k, other_at)
            arrived(gfin.at[k], gz_r.at[2, k])
            remote(gfin.at[k], gz.at[rows], gz_s.at[3, k], gz_r.at[1, k], outer_id).start()
            pltpu.make_async_copy(gfin.at[k], g_out.at[rows], g_loc.at[1, k]).start()

        return carry

    def step5(k, carry):
        @pl.when(end)
        def _():
            rows = sub_rows(k)
            arrived(gz.at[half_rows(k, 0)], gz_r.at[0, k])
            arrived(gz.at[half_rows(k, HALF)], gz_r.at[1, k])
            pltpu.make_async_copy(gz.at[rows], g_out.at[rows], g_loc.at[0, k]).start()

        return carry

    steps = (step1, step2, step3, step4, step5)
    last_point = len(TAKEN[0]) + len(steps) - 1

    def progress(point, live):
        if not chain:
            return

        def taken(p):
            if p < 0:
                return 0
            p = min(p, len(TAKEN[0]) - 1)
            return jnp.where(live, jnp.where(s == 0, TAKEN[0][p], TAKEN[1][p]), 0)

        for i, step in enumerate(steps):
            lax.fori_loop(taken(point - i - 1), taken(point - i), step, 0)

    def finish_grads():
        def one(k, carry):
            rows = sub_rows(k)
            half = grads.at[1 - s, half_rows(k, 0)]
            arrived(grads.at[1 - s, rows], gx_s.at[k])

            @pl.when(end)
            def _():
                arrived(grads.at[s, rows], gz_s.at[0, k])
                arrived(g_out.at[rows], g_loc.at[0, k])

            @pl.when(middle)
            def _():
                for j in range(4):
                    arrived(half, gz_s.at[j, k])
                for j in range(2):
                    arrived(g_out.at[half_rows(k, 0)], g_loc.at[j, k])

            return carry

        lax.fori_loop(0, KS, one, 0)

    def q_rows(h):
        return pl.ds(pl.multiple_of(h * HEAD, HEAD), HEAD)

    def attention_input(l, k):
        xh, r = normed(xres[own_rows(k)])
        xh1[l, own_rows(k)] = xh
        r1[l, own_rows(k)] = r
        a_all[l, block_rows(k, pos)] = (xh * sml[l, 0:1]).astype(BF)
        gather_start(a_all, l, l, 0, k)

    def project(l, k):
        off, n = CH[k]
        rows, lanes = slice(4 * off, 4 * (off + n)), slice(4 * off, 4 * (off + n))

        def query_key(i, carry):
            at = pl.ds(pl.multiple_of(i * HD, HEAD), HD)
            v = mm_nt(wq[l, at], a_all[l, rows])
            for h in range(NH):
                u = v[h * HEAD : (h + 1) * HEAD]
                u = u - jnp.mean(u, axis=0, keepdims=True)
                rr = lax.rsqrt(jnp.mean(u * u, axis=0, keepdims=True) + EPS)
                u = u * rr
                at = pl.ds(pl.multiple_of(i * HD + h * HEAD, HEAD), HEAD)
                qkh[l, at, lanes] = u
                qkr[l, i, pl.ds(h, 1), lanes] = rr
                scale = jnp.where(i == 0, HEAD**-0.5, 1.0).astype(F32)
                gain = jnp.where(i == 0, qkg[l, :, h : h + 1], qkg[l, :, NH + h : NH + h + 1])
                qkvb[l, at, lanes] = ((u * gain).astype(BF).astype(F32) * scale).astype(BF)
            return carry

        lax.fori_loop(0, 2, query_key, 0)
        qkvb[l, 2 * HD :, lanes] = mm_nt(wq[l, 2 * HD :], a_all[l, rows]).astype(BF)

    def attention(l):
        def head(h, carry):
            q_t = qkvb[l, q_rows(h)]
            v_t = qkvb[l, q_rows(2 * NH + h)]
            rows_buf[0, :, :HEAD] = qkvb[l, q_rows(NH + h)].astype(F32).T.astype(BF)

            def block(i, total):
                at = pl.ds(pl.multiple_of(i * KEY_BLOCK, KEY_BLOCK), KEY_BLOCK)
                sc = mm(rows_buf[0, at, :HEAD], q_t)
                e = jnp.where(segc_ref[at] == segr_ref[...], jnp.exp(sc), 0.0)
                e_buf[at] = e.astype(BF)
                return total + jnp.sum(e, axis=0, keepdims=True)

            total = lax.fori_loop(0, NB, block, jnp.zeros((1, N), F32))
            lse[l, pl.ds(h, 1)] = jnp.log(total)
            o_t[l, q_rows(h)] = (mm(v_t, e_buf[...]) * (1.0 / total)).astype(BF)
            return carry

        lax.fori_loop(0, NH, head, 0)
        rows_buf[1, :, :HD] = o_t[l].astype(F32).T.astype(BF)

    def hidden(l, k):
        off, n = CH[k]

        def tile(i, carry):
            rows = pl.ds(pl.multiple_of(4 * off + lax.rem(i, 2) * 2 * n, 16), 2 * n)
            cols = pl.ds(pl.multiple_of((i // 2) * COLS, COLS), COLS)
            u = mm(b_all[l, rows], wu[l, :, cols])
            cdf = 0.5 * (1.0 + lax.erf(u * 0.7071067811865476))
            pdf = jnp.exp(-0.5 * u * u) * 0.3989422804014327
            g_all[l, rows, cols] = (u * cdf).astype(BF)
            gp_all[l, rows, cols] = (cdf + u * pdf).astype(BF)
            return carry

        lax.fori_loop(0, 2 * (FF // COLS), tile, 0)

    def hidden_back(l, k):
        off, n = CH[k]

        def tile(i, carry):
            rows = pl.ds(pl.multiple_of(4 * off + lax.rem(i, 2) * 2 * n, 16), 2 * n)
            cols = pl.ds(pl.multiple_of((i // 2) * COLS, COLS), COLS)
            dg = mm_nt(dm_all[0, rows], wd[l, cols])
            gp_all[l, rows, cols] = (dg * gp_all[l, rows, cols].astype(F32)).astype(BF)
            return carry

        lax.fori_loop(0, 2 * (FF // COLS), tile, 0)

    def down_grad(l):
        def tile(i, carry):
            cols = pl.ds(pl.multiple_of(i * COLS, COLS), COLS)
            at = pl.ds(pl.multiple_of(FD + i * COLS, COLS), COLS)
            grads[l, at] = mm_tn(g_all[l, :, cols], dm_all[0]).astype(BF)
            return carry

        lax.fori_loop(0, FF // COLS, tile, 0)
        send_grads(l, 0, UP // SUB)

    def up_grad(l):
        def tile(i, carry):
            cols = pl.ds(pl.multiple_of(i * COLS, COLS), COLS)
            at = pl.ds(pl.multiple_of(UP + i * COLS, COLS), COLS)
            grads[l, at] = mm_tn(b_all[l, :, cols], gp_all[l]).astype(BF)
            return carry

        lax.fori_loop(0, D // COLS, tile, 0)
        send_grads(l, UP // SUB, OUT // SUB)

    def gains_of(l, i, h):
        out = qkg[l, :, i * NH : i * NH + 1]
        for k in range(1, NH):
            out = jnp.where(h == k, qkg[l, :, i * NH + k : i * NH + k + 1], out)
        return out

    def attention_back(l):
        def head(h, carry):
            q_t = qkvb[l, q_rows(h)]
            k_t = qkvb[l, q_rows(NH + h)]
            v_t = qkvb[l, q_rows(2 * NH + h)]
            rows_buf[0, :, :HEAD] = k_t.astype(F32).T.astype(BF)
            rows_buf[1, :, :HEAD] = v_t.astype(F32).T.astype(BF)
            do_t = dot_buf[q_rows(h)]
            delta = jnp.sum(do_t.astype(F32) * o_t[l, q_rows(h)].astype(F32), axis=0, keepdims=True)
            log_total = lse[l, pl.ds(h, 1)]

            def block(i, carry):
                at = pl.ds(pl.multiple_of(i * KEY_BLOCK, KEY_BLOCK), KEY_BLOCK)
                sc = mm(rows_buf[0, at, :HEAD], q_t)
                p = jnp.where(segc_ref[at] == segr_ref[...], jnp.exp(sc - log_total), 0.0)
                dp = mm(rows_buf[1, at, :HEAD], do_t)
                e_buf[at] = p.astype(BF)
                d_buf[at] = (p * (dp - delta)).astype(BF)
                return carry

            lax.fori_loop(0, NB, block, 0)
            dqkv_t[q_rows(2 * NH + h)] = mm_nt(do_t, e_buf[...]).astype(BF)
            dk = mm_nt(q_t, d_buf[...])
            dq = mm(k_t, d_buf[...]) * (HEAD**-0.5)
            for i, dv in ((0, dq), (1, dk)):
                at = q_rows(i * NH + h)
                dv = dv.astype(BF).astype(F32)
                uh = qkh[l, at]
                lanes = lax.broadcasted_iota(jnp.int32, (HEAD, 128), 1) == i * NH + h
                hgains[l] = jnp.where(lanes, jnp.sum(dv * uh, axis=1, keepdims=True), hgains[l])
                g = dv * gains_of(l, i, h)
                back = g - jnp.mean(g, axis=0, keepdims=True) - uh * jnp.mean(g * uh, axis=0, keepdims=True)
                dqkv_t[at] = (qkr[l, i, pl.ds(h, 1)] * back).astype(BF)
            return carry

        hgains[l] = jnp.zeros((HEAD, 128), F32)
        lax.fori_loop(0, NH, head, 0)
        rows_buf[0] = dqkv_t[...].astype(F32).T.astype(BF)

    each = range(len(CH))
    gains[...] = jnp.zeros_like(gains)

    for l in range(2):
        if l == 0:
            weights_here(l, 0)
            weights_here(l, 1)
            for k in each:
                xres[own_rows(k)] = x_ref[own_rows(k)].astype(F32)
                attention_input(l, k)
                dm_all[0, block_rows(k, pos)] = ct_ref[own_rows(k)]
            forward_blocks(0, 3)
        else:
            weights_here(l, 1)
        weights_here(l, 2)
        for k in each:
            gather_pass(a_all, l, l, 0, k)
        for k in each:
            gather_finish(a_all, l, l, 0, k)
            project(l, k)
        if l == 0:
            for k in each:
                gather_start(dm_all, 0, 1, 2, k)
            forward_blocks(3, 4)
        attention(l)
        if l == 0:
            forward_blocks(4, 6)
            for k in each:
                gather_pass(dm_all, 0, 1, 2, k)
        weights_here(l, 3)
        for k in each:
            scatter_start(lambda at, cols: mm(rows_buf[1, at, :HD], wo[l, :, cols]), l, 0, k)
        for k in each:
            residual = xres[own_rows(k)] + scatter_finish(l, 0, k)
            xres[own_rows(k)] = residual
            xh, r = normed(residual)
            xh2[l, own_rows(k)] = xh
            r2[l, own_rows(k)] = r
            b_all[l, block_rows(k, pos)] = (xh * sml[l, 1:2]).astype(BF)
            gather_start(b_all, l, l, 1, k)
        if l == 0:
            forward_blocks(6, len(blocks))
        weights_here(l, 4)
        weights_here(l, 5)
        gather_pass(b_all, l, l, 1, 0)
        for k in each:
            gather_finish(b_all, l, l, 1, k)
            hidden(l, k)
            if k + 1 < len(CH):
                gather_pass(b_all, l, l, 1, k + 1)
            scatter_start(lambda at, cols: mm(g_all[l, at], wd[l, :, cols]), l, 1, k)
        if l == 0:
            for k in each:
                rounded = (xres[own_rows(k)] + scatter_finish(l, 1, k)).astype(BF)
                ybuf[l, own_rows(k)] = rounded
                xres[own_rows(k)] = rounded.astype(F32)
                if k == 0:
                    weights_here(1, 0)
                attention_input(1, k)

    for l in (1, 0):
        if l == 1:
            for k in each:
                gather_finish(dm_all, 0, l, 2, k)
                hidden_back(l, k)
            down_grad(l)
            for k in each:
                ybuf[l, own_rows(k)] = (xres[own_rows(k)] + scatter_finish(l, 1, k)).astype(BF)
                xres[own_rows(k)] = ct_ref[own_rows(k)].astype(F32)
            y_move = remote(ybuf.at[1 - s], ylo, x_s.at[0], x_r.at[0], x_id)
            y_move.start()
            for k in each:
                scatter_start(lambda at, cols: mm_nt(gp_all[l, at], wu[l, cols]), l, 2, k)
        else:
            progress(0, True)
            gather_pass(dm_all, 0, l, 2, 0)
            for k in each:
                gather_finish(dm_all, 0, l, 2, k)
                hidden_back(l, k)
                if k + 1 < len(CH):
                    gather_pass(dm_all, 0, l, 2, k + 1)
                scatter_start(lambda at, cols: mm_nt(gp_all[l, at], wu[l, cols]), l, 2, k)
            down_grad(l)
            progress(1, True)
        up_grad(l)
        if l == 0:
            progress(2, True)
        for k in each:
            db = scatter_finish(l, 2, k)
            xh = xh2[l, own_rows(k)]
            gains[l, 1:2] = gains[l, 1:2] + jnp.sum(db * xh, axis=0, keepdims=True)
            dh = xres[own_rows(k)] + normed_back(db, sml[l, 1:2], xh, r2[l, own_rows(k)])
            xres[own_rows(k)] = dh
            da_all[0, block_rows(k, pos)] = dh.astype(BF)
            gather_start(da_all, 0, l, 3, k)
        if l == 0:
            progress(3, True)
        for k in each:
            gather_pass(da_all, 0, l, 3, k)
        for k in each:
            gather_finish(da_all, 0, l, 3, k)
        dot_buf[...] = mm_nt(wo[l], da_all[0]).astype(BF)
        grads[l, OUT:QKV] = mm(o_t[l], da_all[0]).astype(BF)
        send_grads(l, OUT // SUB, QKV // SUB)
        if l == 0:
            progress(4, True)
        attention_back(l)
        if l == 0:
            progress(5, True)
        for k in each:
            scatter_start(lambda at, cols: mm(rows_buf[0, at], wq[l, :, cols]), l, 3, k)
        grads[l, QKV:] = mm(dqkv_t[...], a_all[l]).astype(BF)
        send_grads(l, QKV // SUB, KS)
        if l == 0:
            progress(6, True)
        for k in each:
            da = scatter_finish(l, 3, k)
            xh = xh1[l, own_rows(k)]
            gains[l, 0:1] = gains[l, 0:1] + jnp.sum(da * xh, axis=0, keepdims=True)
            dx = xres[own_rows(k)] + normed_back(da, sml[l, 0:1], xh, r1[l, own_rows(k)])
            rounded = dx.astype(BF)
            dxbuf[l, own_rows(k)] = rounded
            if l == 1:
                xres[own_rows(k)] = rounded.astype(F32)
                dm_all[0, block_rows(k, pos)] = rounded
                gather_start(dm_all, 0, 0, 2, k)
            else:
                xres[own_rows(k)] = dx

        @pl.when(l == s)
        def _():
            ig_out[s] = dxbuf[1].astype(F32) if l == 1 else xres[...]

        @pl.when(l != s)
        def _():
            remote(dxbuf.at[1 - s], dxlo, x_s.at[1], x_r.at[1], x_id).start()
            if chain:
                remote(gains.at[1 - s], gains_x, sm_s.at[0], sm_r.at[0], x_id).start()
                remote(hgains.at[1 - s], hgains_x, sm_s.at[1], sm_r.at[1], x_id).start()

    progress(LAYER_POINTS, True)
    if chain:
        arrived(gains_x, sm_r.at[0])
        arrived(hgains_x, sm_r.at[1])
        gains_z[b] = gains[s] + gains_x[...]
        hgains_z[b] = hgains[s] + hgains_x[...]
        for i, peer in enumerate(z_ids):
            remote(gains_z.at[b], gains_z.at[b], sm_s.at[2 + i], sm_r.at[2 + i], peer).start()
            remote(hgains_z.at[b], hgains_z.at[b], sm_s.at[5 + i], sm_r.at[5 + i], peer).start()
        progress(LAYER_POINTS + 1, True)
        for i in range(3):
            arrived(gains_x, sm_r.at[2 + i])
            arrived(hgains_x, sm_r.at[5 + i])
        gh_out[...] = hgains_z[0] + hgains_z[1] + hgains_z[2] + hgains_z[3]
        gains_t[t] = gains_z[0] + gains_z[1] + gains_z[2] + gains_z[3]
        for i, peer in enumerate((core_id, y_id, diag_id)):
            remote(gains_t.at[t], gains_t.at[t], sm_s.at[8 + i], sm_r.at[8 + i], peer).start()
        progress(LAYER_POINTS + 2, True)
        for i in range(3):
            arrived(gains_x, sm_r.at[8 + i])
        gg_out[...] = gains_t[0] + gains_t[1] + gains_t[2] + gains_t[3]
        for point in range(LAYER_POINTS + 3, last_point):
            progress(point, True)
    else:
        g_out[...] = grads[...]
        gg_out[...] = gains[...]
        gh_out[...] = hgains[...]
    y_move.wait()
    y_out[s] = ybuf[s]
    y_out[1 - s] = ylo[...]
    finish_weights()
    arrived(dxlo, x_s.at[1])
    arrived(dxlo, x_r.at[1])
    ig_out[1 - s] = dxlo[...].astype(F32)
    if chain:
        finish_grads()
        for i in range(2, 5):
            arrived(gains_x, sm_s.at[i])
            arrived(hgains_x, sm_s.at[3 + i])
            arrived(gains_x, sm_s.at[6 + i])
        arrived(gains_x, sm_s.at[0])
        arrived(hgains_x, sm_s.at[1])


def fused(chain, x, ct, segc, segr, small, qk_gain, wq, wo, wu, wd):
    R, D = x.shape
    N = 4 * R
    QD, HD, FF = wq.shape[0], wo.shape[0], wu.shape[1]
    NH = HD // HEAD
    CH = len(chunks_of(R))
    vmem = pl.BlockSpec(memory_space=pltpu.VMEM)
    hbm = pl.BlockSpec(memory_space=pl.ANY)
    shape = jax.ShapeDtypeStruct
    V = pltpu.VMEM
    dma = pltpu.SemaphoreType.DMA
    G = FF + D + HD + QD
    KS = G // SUB
    ahead = () if chain else (2,)
    extra = [
        V((G, D), BF), V((G, D), BF), V((KS, SUB // 2, D), BF), V((KS, SUB // 2, D), BF),
        V((8, D), F32), V((HEAD, 128), F32), V((4, 8, D), F32), V((4, HEAD, 128), F32), V((4, 8, D), F32),
        dma((KS,)), dma((KS,)), dma((4, KS)), dma((3, KS)), dma((2, KS)), dma((11,)), dma((11,)),
    ]
    if not chain:
        extra = [V((8, 128), F32)] * 9 + [dma((1,))] * 7
    return pl.pallas_call(
        functools.partial(body, chain),
        out_shape=(
            shape((2, R, D), BF),
            shape((2, R, D), F32),
            shape(ahead + (G, D), BF),
            shape(ahead + (8, D), F32),
            shape(ahead + (HEAD, 128), F32),
        ),
        in_specs=[vmem] * 4 + [hbm] * 6,
        out_specs=(vmem, vmem, hbm if chain else vmem, vmem, vmem),
        scratch_shapes=[
            V((2, QD, D), BF), V((2, HD, D), BF), V((2, D, FF), BF), V((2, FF, D), BF),
            V((2, 8, D), F32), V((2, HEAD, 128), F32),
            V((R, D), F32), V((2, R, D), F32), V((2, R, 1), F32), V((2, R, D), F32), V((2, R, 1), F32),
            V((2, N, D), BF), V((2, N, D), BF), V((1, N, D), BF), V((1, N, D), BF),
            V((2, 2 * HD, N), F32), V((2, 2, 8, N), F32), V((2, QD, N), BF), V((2, 8, N), F32),
            V((2, HD, N), BF), V((2, N, FF), BF), V((2, N, FF), BF),
            V((2, N, QD), BF), V((2 * R, D), F32), V((2 * R, D), BF), V((R, D), BF),
            V((2, 2 * R, D), BF), V((2, R, D), BF),
            V((N, N), BF), V((N, N), BF), V((HD, N), BF), V((QD, N), BF),
            V((2, R, D), BF), V((2, R, D), BF), V((R, D), BF), V((R, D), BF),
            V((2, G, D), BF), V((2, 8, D), F32), V((2, HEAD, 128), F32),
            dma((6,)), dma((16,)), dma((16,)), dma((16,)), dma((16,)),
            dma((2, 4, 3, CH)), dma((2, 4, 3, CH)), dma((2, 4, 2, CH)), dma((2, 4, 2, CH)), dma((2,)), dma((2,)),
        ] + extra,
        name="layers",
        compiler_params=pltpu.CompilerParams(
            collective_id=0, has_side_effects=True, vmem_limit_bytes=63 * 2**20
        ),
    )(x, ct, segc, segr, small, qk_gain, wq, wo, wu, wd)


def shards(
    patches, cotangent, image_lengths, attn_gain, qkv_weight, query_gain, key_gain, out_weight,
    mlp_gain, up_weight, down_weight,
):
    s = lax.axis_index("section")
    _, own, D = patches.shape
    seq_len = 4 * own
    R = ceil_to(own, 16)
    N = 4 * R
    HD = out_weight.shape[1]
    NH = HD // HEAD
    pad = ((0, R - own), (0, 0))
    x = jnp.pad(lax.dynamic_index_in_dim(patches, s, 0, keepdims=False), pad)
    ct = jnp.pad(lax.dynamic_index_in_dim(cotangent, s, 0, keepdims=False), pad)
    lengths = lax.dynamic_index_in_dim(image_lengths, s, 0, keepdims=False)[0]
    bounds = jnp.cumsum(lengths, dtype=jnp.int32)
    places = jnp.arange(seq_len, dtype=jnp.int32)
    seg = jnp.sum((places[:, None] >= bounds[None, :]).astype(jnp.int32), axis=-1)
    seg = seg.reshape(2, 2, own).transpose(1, 0, 2).reshape(4, own)
    seg = jnp.pad(seg, ((0, 0), (0, R - own)), constant_values=-1)
    seg = jnp.concatenate([seg[:, a : a + n].reshape(4 * n) for a, n in chunks_of(R)])
    small = jnp.zeros((8, D), F32).at[0].set(attn_gain[0].astype(F32)).at[1].set(mlp_gain[0].astype(F32))
    qk_gain = jnp.concatenate([query_gain[0], key_gain[0]], axis=0).astype(F32).T
    qk_gain = jnp.pad(qk_gain, ((0, 0), (0, 128 - 2 * NH)))
    wq = qkv_weight[0].reshape(D, 3 * HD).T
    chain = lax.axis_size("batch") == 4
    y, ig, g, gg, gh = fused(
        chain, x, ct, seg[:, None], seg[None, :], small, qk_gain, wq, out_weight[0], up_weight[0],
        down_weight[0],
    )
    if not chain:
        theirs = lax.ppermute(g[1 - s], "section", [(0, 1), (1, 0)])
        g = lax.psum((g[s].astype(F32) + theirs.astype(F32)).astype(BF), "batch")
        gg = lax.psum(gg, ("section", "batch", "tensor"))[s]
        gh = lax.psum(gh, ("section", "batch"))[s]
    FF = up_weight.shape[2]
    gd, gu, go, gq = (g[:FF], g[FF : FF + D], g[FF + D : FF + D + HD], g[FF + D + HD :])
    gh = gh[:, : 2 * NH].T.reshape(2, NH, HEAD)
    return (
        y[:, :own][None],
        ig[:, :own][None],
        gg[0][None],
        gq.astype(F32).T.reshape(D, 3, HD)[None],
        gh[0][None],
        gh[1][None],
        go.astype(F32)[None],
        gg[1][None],
        gu.astype(F32)[None],
        gd.astype(F32)[None],
    )


def solution(mesh):
    return jax.shard_map(
        shards,
        mesh=mesh,
        in_specs=(
            P(None, ("batch", "tensor"), None),
            P(None, ("batch", "tensor"), None),
            P(None, "batch", None),
            P("section", None),
            P("section", None, None, "tensor"),
            P("section", "tensor", None),
            P("section", "tensor", None),
            P("section", "tensor", None),
            P("section", None),
            P("section", None, "tensor"),
            P("section", "tensor", None),
        ),
        out_specs=(
            P("section", None, ("batch", "tensor"), None),
            P("section", None, ("batch", "tensor"), None),
            P("section", None),
            P("section", None, None, "tensor"),
            P("section", "tensor", None),
            P("section", "tensor", None),
            P("section", "tensor", None),
            P("section", None),
            P("section", None, "tensor"),
            P("section", "tensor", None),
        ),
        check_vma=False,
    )
```

```python
import functools

import jax
import jax.numpy as jnp
from jax import lax
from jax.experimental import pallas as pl
from jax.experimental.pallas import tpu as pltpu
from jax.sharding import PartitionSpec as P

HEAD = 64
EPS = 1e-06
MESH = pl.DeviceIdType.MESH
BF = jnp.bfloat16
F32 = jnp.float32
KEY_BLOCK = 64
COLS = 256
SUB = 192
CHUNKS = 2
TAKEN = (
    (0, 0, 0, 0, 0, 0, 0, 0, 0, 0, 1, 1, 2, 3, 4, 5) + tuple(range(6, 13)),
    (0, 0, 0, 0, 1, 1, 2, 3, 4, 5, 5, 6, 6, 7, 8, 9) + tuple(range(10, 13)),
)
LAGS = (0, 2, 3, 4, 5)
LAYER_POINTS = 8


def ceil_to(n, m):
    return -(-n // m) * m


def chunks_of(rows):
    step = max(32, rows // CHUNKS // 32 * 32)
    starts = [i * step for i in range(CHUNKS) if i * step < rows]
    return [(a, b - a) for a, b in zip(starts, starts[1:] + [rows])]


def mm(a, b):
    return lax.dot_general(a, b, (((1,), (0,)), ((), ())), preferred_element_type=F32)


def mm_nt(a, b):
    return lax.dot_general(a, b, (((1,), (1,)), ((), ())), preferred_element_type=F32)


def mm_tn(a, b):
    return lax.dot_general(a, b, (((0,), (0,)), ((), ())), preferred_element_type=F32)


def normed(v):
    centre = v - jnp.mean(v, axis=-1, keepdims=True)
    r = lax.rsqrt(jnp.mean(centre * centre, axis=-1, keepdims=True) + EPS)
    return centre * r, r


def normed_back(dv, gain, xh, r):
    g = dv * gain
    return r * (g - jnp.mean(g, axis=-1, keepdims=True) - xh * jnp.mean(g * xh, axis=-1, keepdims=True))


def body(
    chain,
    x_ref, ct_ref, segc_ref, segr_ref, sml_in, qkg_in, wq_in, wo_in, wu_in, wd_in,
    y_out, ig_out, g_out, gg_out, gh_out,
    wq, wo, wu, wd, sml, qkg,
    xres, xh1, r1, xh2, r2,
    a_all, b_all, dm_all, da_all,
    qkh, qkr, qkvb, lse, o_t, g_all, gp_all,
    rows_buf, part, sendbuf, ysend, crecv, yrecv,
    e_buf, d_buf, dot_buf, dqkv_t,
    ybuf, dxbuf, ylo, dxlo,
    grads, gains, hgains,
    w_loc, w_send, w_recv, wz_s, wz_r, ag_s, ag_r, rs_s, rs_r, x_s, x_r,
    gx, gz, gpart, gfin, gains_x, hgains_x, gains_z, hgains_z, gains_t,
    gx_s, gx_r, gz_s, gz_r, g_loc, sm_s, sm_r,
):
    s, b, t = lax.axis_index("section"), lax.axis_index("batch"), lax.axis_index("tensor")
    y, c = t // 2, lax.rem(t, 2)
    core_id = (s, b, y * 2 + 1 - c)
    y_id = (s, b, (1 - y) * 2 + c)
    x_id = (1 - s, b, t)
    R, D = x_ref.shape
    N = 4 * R
    FF = wu.shape[2]
    HD = wo.shape[1]
    NH = HD // HEAD
    NB = N // KEY_BLOCK
    pos = c * 2 + y
    ypos = c * 2 + 1 - y
    CH = chunks_of(R)

    def block_rows(k, at):
        off, n = CH[k]
        return pl.ds(pl.multiple_of(4 * off + at * n, 16), n)

    def own_rows(k):
        return pl.ds(CH[k][0], CH[k][1])

    diag_id = (s, b, (1 - y) * 2 + 1 - c)
    z_ids = [(s, lax.rem(b + k, 4), t) for k in (1, 2, 3)] if chain else []
    barrier = pltpu.get_barrier_semaphore()
    for peer in [core_id, y_id, diag_id, x_id] + z_ids:
        pl.semaphore_signal(barrier, inc=1, device_id=peer, device_id_type=MESH)
    pl.semaphore_wait(barrier, 4 + len(z_ids))

    def remote(src, dst, ss, rs, peer):
        return pltpu.make_async_remote_copy(
            src_ref=src, dst_ref=dst, send_sem=ss, recv_sem=rs, device_id=peer, device_id_type=MESH
        )

    def arrived(ref, sem):
        pltpu.make_async_copy(ref, ref, sem).wait()

    moves = ((sml_in, sml), (qkg_in, qkg), (wq_in, wq), (wo_in, wo), (wu_in, wu), (wd_in, wd))
    pair_id = (s, b + 1 - 2 * lax.rem(b, 2), t)
    near = lax.rem(b, 2)
    blocks = []
    for i in range(2, 6):
        rows = moves[i][0].shape[0]
        step = min(rows, 2 * SUB if i > 3 else SUB)
        blocks += [(i, at, step) for at in range(0, rows, step)]

    def half_block(ref, j, h):
        _, at, n = blocks[j]
        return ref.at[pl.ds(pl.multiple_of(at + h * (n // 2), 16), n // 2)]

    def send_block(j):
        src, dst = moves[blocks[j][0]]
        if chain:
            remote(half_block(src, j, near), half_block(dst.at[s], j, near), w_send.at[j], w_recv.at[j], x_id).start()
        else:
            _, at, n = blocks[j]
            remote(src.at[at : at + n], dst.at[s, at : at + n], w_send.at[j], w_recv.at[j], x_id).start()

    def forward_blocks(lo, hi):
        if chain:
            for j in range(lo, hi):
                got = half_block(moves[blocks[j][0]][1].at[1 - s], j, near)
                arrived(got, w_recv.at[j])
                remote(got, got, wz_s.at[j], wz_r.at[j], pair_id).start()

    for i, (src, dst) in enumerate(moves):
        if i < 2:
            remote(src, dst.at[s], w_send.at[len(blocks) + i], w_recv.at[len(blocks) + i], x_id).start()
        else:
            for j in range(len(blocks)):
                if blocks[j][0] == i:
                    send_block(j)
        pltpu.make_async_copy(src, dst.at[s], w_loc.at[i]).start()

    def weights_here(l, i):
        src, dst = moves[i]

        @pl.when(l == s)
        def _():
            pltpu.make_async_copy(src, dst.at[s], w_loc.at[i]).wait()

        @pl.when(l != s)
        def _():
            if i < 2:
                arrived(dst.at[1 - s], w_recv.at[len(blocks) + i])
            for j in range(len(blocks)):
                if blocks[j][0] == i:
                    if chain:
                        arrived(half_block(dst.at[1 - s], j, 1 - near), wz_r.at[j])
                    else:
                        _, at, n = blocks[j]
                        arrived(dst.at[1 - s, at : at + n], w_recv.at[j])

    def finish_weights():
        for i in range(2):
            arrived(moves[i][1].at[s], w_send.at[len(blocks) + i])
        for j in range(len(blocks)):
            i, at, n = blocks[j]
            if chain:
                arrived(half_block(moves[i][1].at[s], j, near), w_send.at[j])
                arrived(half_block(moves[i][1].at[1 - s], j, near), wz_s.at[j])
            else:
                arrived(moves[i][1].at[s, at : at + n], w_send.at[j])

    def gather_start(buf, slot, l, op, k):
        mine = buf.at[slot, block_rows(k, pos)]
        remote(mine, mine, ag_s.at[l, op, 0, k], ag_r.at[l, op, 0, k], core_id).start()
        remote(mine, mine, ag_s.at[l, op, 1, k], ag_r.at[l, op, 1, k], y_id).start()

    def gather_pass(buf, slot, l, op, k):
        theirs = buf.at[slot, block_rows(k, ypos)]
        arrived(theirs, ag_r.at[l, op, 1, k])
        remote(theirs, theirs, ag_s.at[l, op, 2, k], ag_r.at[l, op, 2, k], core_id).start()

    def gather_finish(buf, slot, l, op, k):
        mine = buf.at[slot, block_rows(k, pos)]
        arrived(mine, ag_r.at[l, op, 0, k])
        arrived(mine, ag_r.at[l, op, 2, k])
        arrived(mine, ag_s.at[l, op, 0, k])
        arrived(mine, ag_s.at[l, op, 1, k])
        arrived(mine, ag_s.at[l, op, 2, k])

    def pair_rows(k):
        return pl.ds(2 * CH[k][0], 2 * CH[k][1])

    def scatter_start(product, l, op, k):
        slot = op % 2
        off, n = CH[k]

        def send_tile(j, carry):
            cols = pl.ds(pl.multiple_of(j * COLS, COLS), COLS)
            at = pl.ds(pl.multiple_of(4 * off + (1 - c) * 2 * n, 16), 2 * n)
            sendbuf[pair_rows(k), cols] = product(at, cols).astype(BF)
            return carry

        lax.fori_loop(0, D // COLS, send_tile, 0)
        mine = sendbuf.at[pair_rows(k)]
        remote(mine, crecv.at[slot, pair_rows(k)], rs_s.at[l, op, 0, k], rs_r.at[l, op, 0, k], core_id).start()

        def own_tile(j, carry):
            cols = pl.ds(pl.multiple_of(j * COLS, COLS), COLS)
            at = pl.ds(pl.multiple_of(4 * off + c * 2 * n, 16), 2 * n)
            part[pair_rows(k), cols] = product(at, cols)
            return carry

        lax.fori_loop(0, D // COLS, own_tile, 0)
        arrived(mine, rs_r.at[l, op, 0, k])
        other = pl.ds(pl.multiple_of(2 * off + (1 - y) * n, 16), n)
        ysend[own_rows(k)] = (part[other] + crecv[slot, other].astype(F32)).astype(BF)
        remote(
            ysend.at[own_rows(k)], yrecv.at[slot, own_rows(k)], rs_s.at[l, op, 1, k], rs_r.at[l, op, 1, k], y_id
        ).start()

    def scatter_finish(l, op, k):
        slot = op % 2
        off, n = CH[k]
        mine = pl.ds(pl.multiple_of(2 * off + y * n, 16), n)
        arrived(sendbuf.at[pair_rows(k)], rs_s.at[l, op, 0, k])
        arrived(ysend.at[own_rows(k)], rs_s.at[l, op, 1, k])
        arrived(ysend.at[own_rows(k)], rs_r.at[l, op, 1, k])
        return part[mine] + crecv[slot, mine].astype(F32) + yrecv[slot, own_rows(k)].astype(F32)

    FD, UP, OUT = 0, FF, FF + D
    QKV = OUT + HD
    KS = grads.shape[1] // SUB
    HALF = SUB // 2
    middle = (b == 1) | (b == 2)
    end = jnp.logical_not(middle)
    inner_id = (s, jnp.where(b == 0, 1, 2), t)
    outer_id = (s, jnp.where(b == 1, 0, 3), t)
    partner_id = (s, jnp.where(b == 1, 2, 1), t)
    mine_at = jnp.where(b == 1, 0, HALF)
    other_at = HALF - mine_at

    def sub_rows(k):
        return pl.ds(pl.multiple_of(k * SUB, 16), SUB)

    def half_rows(k, at):
        return pl.ds(pl.multiple_of(k * SUB + at, 16), HALF)

    def send_grads(l, lo, hi):
        if not chain:
            return

        @pl.when(l != s)
        def _():
            def one(k, carry):
                rows = sub_rows(k)
                remote(grads.at[l, rows], gx.at[rows], gx_s.at[k], gx_r.at[k], x_id).start()
                return carry

            lax.fori_loop(lo, hi, one, 0)

    def step1(k, carry):
        rows = sub_rows(k)
        arrived(gx.at[rows], gx_r.at[k])
        grads[s, rows] = (grads[s, rows].astype(F32) + gx[rows].astype(F32)).astype(BF)

        @pl.when(end)
        def _():
            remote(grads.at[s, rows], gz.at[rows], gz_s.at[0, k], gz_r.at[0, k], inner_id).start()

        return carry

    def step2(k, carry):
        @pl.when(middle)
        def _():
            rows = sub_rows(k)
            arrived(gz.at[rows], gz_r.at[0, k])
            grads[s, rows] = (grads[s, rows].astype(F32) + gz[rows].astype(F32)).astype(BF)
            other = grads.at[s, half_rows(k, other_at)]
            remote(other, gpart.at[k], gz_s.at[0, k], gz_r.at[1, k], partner_id).start()

        return carry

    def step3(k, carry):
        @pl.when(middle)
        def _():
            rows = half_rows(k, mine_at)
            arrived(gpart.at[k], gz_r.at[1, k])
            grads[s, rows] = (grads[s, rows].astype(F32) + gpart[k].astype(F32)).astype(BF)
            done = grads.at[s, rows]
            remote(done, gfin.at[k], gz_s.at[1, k], gz_r.at[2, k], partner_id).start()
            remote(done, gz.at[rows], gz_s.at[2, k], gz_r.at[0, k], outer_id).start()
            pltpu.make_async_copy(done, g_out.at[rows], g_loc.at[0, k]).start()

        return carry

    def step4(k, carry):
        @pl.when(middle)
        def _():
            rows = half_rows(k, other_at)
            arrived(gfin.at[k], gz_r.at[2, k])
            remote(gfin.at[k], gz.at[rows], gz_s.at[3, k], gz_r.at[1, k], outer_id).start()
            pltpu.make_async_copy(gfin.at[k], g_out.at[rows], g_loc.at[1, k]).start()

        return carry

    def step5(k, carry):
        @pl.when(end)
        def _():
            rows = sub_rows(k)
            arrived(gz.at[half_rows(k, 0)], gz_r.at[0, k])
            arrived(gz.at[half_rows(k, HALF)], gz_r.at[1, k])
            pltpu.make_async_copy(gz.at[rows], g_out.at[rows], g_loc.at[0, k]).start()

        return carry

    steps = (step1, step2, step3, step4, step5)
    last_point = max(len(row) for row in TAKEN) + LAGS[-1]

    def progress(point):
        if not chain:
            return

        def taken(p):
            first, second = ((0 if p < 0 else row[min(p, len(row) - 1)]) for row in TAKEN)
            return first if first == second else jnp.where(s == 0, first, second)

        for step, lag in zip(steps, LAGS):
            lo, hi = taken(point - lag - 1), taken(point - lag)
            if not (isinstance(lo, int) and isinstance(hi, int) and lo == hi):
                lax.fori_loop(lo, hi, step, 0)

    def finish_grads():
        def one(k, carry):
            rows = sub_rows(k)
            half = grads.at[1 - s, half_rows(k, 0)]
            arrived(grads.at[1 - s, rows], gx_s.at[k])

            @pl.when(end)
            def _():
                arrived(grads.at[s, rows], gz_s.at[0, k])
                arrived(g_out.at[rows], g_loc.at[0, k])

            @pl.when(middle)
            def _():
                for j in range(4):
                    arrived(half, gz_s.at[j, k])
                for j in range(2):
                    arrived(g_out.at[half_rows(k, 0)], g_loc.at[j, k])

            return carry

        lax.fori_loop(0, KS, one, 0)

    def q_rows(h):
        return pl.ds(pl.multiple_of(h * HEAD, HEAD), HEAD)

    def attention_input(l, k):
        xh, r = normed(xres[own_rows(k)])
        xh1[l, own_rows(k)] = xh
        r1[l, own_rows(k)] = r
        a_all[l, block_rows(k, pos)] = (xh * sml[l, 0:1]).astype(BF)
        gather_start(a_all, l, l, 0, k)

    def project(l, k):
        off, n = CH[k]
        rows, lanes = slice(4 * off, 4 * (off + n)), slice(4 * off, 4 * (off + n))

        def query_key(i, carry):
            at = pl.ds(pl.multiple_of(i * HD, HEAD), HD)
            v = mm_nt(wq[l, at], a_all[l, rows])
            for h in range(NH):
                u = v[h * HEAD : (h + 1) * HEAD]
                u = u - jnp.mean(u, axis=0, keepdims=True)
                rr = lax.rsqrt(jnp.mean(u * u, axis=0, keepdims=True) + EPS)
                u = u * rr
                at = pl.ds(pl.multiple_of(i * HD + h * HEAD, HEAD), HEAD)
                qkh[l, at, lanes] = u
                qkr[l, i, pl.ds(h, 1), lanes] = rr
                scale = jnp.where(i == 0, HEAD**-0.5, 1.0).astype(F32)
                gain = jnp.where(i == 0, qkg[l, :, h : h + 1], qkg[l, :, NH + h : NH + h + 1])
                qkvb[l, at, lanes] = ((u * gain).astype(BF).astype(F32) * scale).astype(BF)
            return carry

        lax.fori_loop(0, 2, query_key, 0)
        qkvb[l, 2 * HD :, lanes] = mm_nt(wq[l, 2 * HD :], a_all[l, rows]).astype(BF)

    def attention(l):
        def head(h, carry):
            q_t = qkvb[l, q_rows(h)]
            v_t = qkvb[l, q_rows(2 * NH + h)]
            rows_buf[0, :, :HEAD] = qkvb[l, q_rows(NH + h)].astype(F32).T.astype(BF)

            def block(i, total):
                at = pl.ds(pl.multiple_of(i * KEY_BLOCK, KEY_BLOCK), KEY_BLOCK)
                sc = mm(rows_buf[0, at, :HEAD], q_t)
                e = jnp.where(segc_ref[at] == segr_ref[...], jnp.exp(sc), 0.0)
                e_buf[at] = e.astype(BF)
                return total + jnp.sum(e, axis=0, keepdims=True)

            total = lax.fori_loop(0, NB, block, jnp.zeros((1, N), F32))
            lse[l, pl.ds(h, 1)] = jnp.log(total)
            o_t[l, q_rows(h)] = (mm(v_t, e_buf[...]) * (1.0 / total)).astype(BF)
            return carry

        lax.fori_loop(0, NH, head, 0)
        rows_buf[1, :, :HD] = o_t[l].astype(F32).T.astype(BF)

    def hidden(l, k):
        off, n = CH[k]

        def tile(i, carry):
            rows = pl.ds(pl.multiple_of(4 * off + lax.rem(i, 2) * 2 * n, 16), 2 * n)
            cols = pl.ds(pl.multiple_of((i // 2) * COLS, COLS), COLS)
            u = mm(b_all[l, rows], wu[l, :, cols])
            cdf = 0.5 * (1.0 + lax.erf(u * 0.7071067811865476))
            pdf = jnp.exp(-0.5 * u * u) * 0.3989422804014327
            g_all[l, rows, cols] = (u * cdf).astype(BF)
            gp_all[l, rows, cols] = (cdf + u * pdf).astype(BF)
            return carry

        lax.fori_loop(0, 2 * (FF // COLS), tile, 0)

    def hidden_back(l, k):
        off, n = CH[k]

        def tile(i, carry):
            rows = pl.ds(pl.multiple_of(4 * off + lax.rem(i, 2) * 2 * n, 16), 2 * n)
            cols = pl.ds(pl.multiple_of((i // 2) * COLS, COLS), COLS)
            dg = mm_nt(dm_all[0, rows], wd[l, cols])
            gp_all[l, rows, cols] = (dg * gp_all[l, rows, cols].astype(F32)).astype(BF)
            return carry

        lax.fori_loop(0, 2 * (FF // COLS), tile, 0)

    def down_grad(l):
        def tile(i, carry):
            cols = pl.ds(pl.multiple_of(i * COLS, COLS), COLS)
            at = pl.ds(pl.multiple_of(FD + i * COLS, COLS), COLS)
            grads[l, at] = mm_tn(g_all[l, :, cols], dm_all[0]).astype(BF)
            return carry

        lax.fori_loop(0, FF // COLS, tile, 0)
        send_grads(l, 0, UP // SUB)

    def up_grad(l):
        def tile(i, carry):
            cols = pl.ds(pl.multiple_of(i * COLS, COLS), COLS)
            at = pl.ds(pl.multiple_of(UP + i * COLS, COLS), COLS)
            grads[l, at] = mm_tn(b_all[l, :, cols], gp_all[l]).astype(BF)
            return carry

        lax.fori_loop(0, D // COLS, tile, 0)
        send_grads(l, UP // SUB, OUT // SUB)

    def gains_of(l, i, h):
        out = qkg[l, :, i * NH : i * NH + 1]
        for k in range(1, NH):
            out = jnp.where(h == k, qkg[l, :, i * NH + k : i * NH + k + 1], out)
        return out

    def attention_back(l):
        def head(h, carry):
            q_t = qkvb[l, q_rows(h)]
            k_t = qkvb[l, q_rows(NH + h)]
            v_t = qkvb[l, q_rows(2 * NH + h)]
            rows_buf[0, :, :HEAD] = k_t.astype(F32).T.astype(BF)
            rows_buf[1, :, :HEAD] = v_t.astype(F32).T.astype(BF)
            do_t = dot_buf[q_rows(h)]
            delta = jnp.sum(do_t.astype(F32) * o_t[l, q_rows(h)].astype(F32), axis=0, keepdims=True)
            log_total = lse[l, pl.ds(h, 1)]

            def block(i, carry):
                at = pl.ds(pl.multiple_of(i * KEY_BLOCK, KEY_BLOCK), KEY_BLOCK)
                sc = mm(rows_buf[0, at, :HEAD], q_t)
                p = jnp.where(segc_ref[at] == segr_ref[...], jnp.exp(sc - log_total), 0.0)
                dp = mm(rows_buf[1, at, :HEAD], do_t)
                e_buf[at] = p.astype(BF)
                d_buf[at] = (p * (dp - delta)).astype(BF)
                return carry

            lax.fori_loop(0, NB, block, 0)
            dqkv_t[q_rows(2 * NH + h)] = mm_nt(do_t, e_buf[...]).astype(BF)
            dk = mm_nt(q_t, d_buf[...])
            dq = mm(k_t, d_buf[...]) * (HEAD**-0.5)
            for i, dv in ((0, dq), (1, dk)):
                at = q_rows(i * NH + h)
                dv = dv.astype(BF).astype(F32)
                uh = qkh[l, at]
                lanes = lax.broadcasted_iota(jnp.int32, (HEAD, 128), 1) == i * NH + h
                hgains[l] = jnp.where(lanes, jnp.sum(dv * uh, axis=1, keepdims=True), hgains[l])
                g = dv * gains_of(l, i, h)
                back = g - jnp.mean(g, axis=0, keepdims=True) - uh * jnp.mean(g * uh, axis=0, keepdims=True)
                dqkv_t[at] = (qkr[l, i, pl.ds(h, 1)] * back).astype(BF)
            return carry

        hgains[l] = jnp.zeros((HEAD, 128), F32)
        lax.fori_loop(0, NH, head, 0)
        rows_buf[0] = dqkv_t[...].astype(F32).T.astype(BF)

    each = range(len(CH))
    gains[...] = jnp.zeros_like(gains)

    for l in range(2):
        if l == 0:
            weights_here(l, 0)
            weights_here(l, 1)
            for k in each:
                xres[own_rows(k)] = x_ref[own_rows(k)].astype(F32)
                attention_input(l, k)
                dm_all[0, block_rows(k, pos)] = ct_ref[own_rows(k)]
            forward_blocks(0, 3)
        else:
            weights_here(l, 1)
        weights_here(l, 2)
        for k in each:
            gather_pass(a_all, l, l, 0, k)
        for k in each:
            gather_finish(a_all, l, l, 0, k)
            project(l, k)
        if l == 0:
            for k in each:
                gather_start(dm_all, 0, 1, 2, k)
            forward_blocks(3, 4)
        attention(l)
        if l == 0:
            forward_blocks(4, 6)
            for k in each:
                gather_pass(dm_all, 0, 1, 2, k)
        weights_here(l, 3)
        for k in each:
            scatter_start(lambda at, cols: mm(rows_buf[1, at, :HD], wo[l, :, cols]), l, 0, k)
        for k in each:
            residual = xres[own_rows(k)] + scatter_finish(l, 0, k)
            xres[own_rows(k)] = residual
            xh, r = normed(residual)
            xh2[l, own_rows(k)] = xh
            r2[l, own_rows(k)] = r
            b_all[l, block_rows(k, pos)] = (xh * sml[l, 1:2]).astype(BF)
            gather_start(b_all, l, l, 1, k)
        if l == 0:
            forward_blocks(6, len(blocks))
        weights_here(l, 4)
        weights_here(l, 5)
        gather_pass(b_all, l, l, 1, 0)
        for k in each:
            gather_finish(b_all, l, l, 1, k)
            hidden(l, k)
            if k + 1 < len(CH):
                gather_pass(b_all, l, l, 1, k + 1)
            scatter_start(lambda at, cols: mm(g_all[l, at], wd[l, :, cols]), l, 1, k)
        if l == 0:
            for k in each:
                rounded = (xres[own_rows(k)] + scatter_finish(l, 1, k)).astype(BF)
                ybuf[l, own_rows(k)] = rounded
                xres[own_rows(k)] = rounded.astype(F32)
                if k == 0:
                    weights_here(1, 0)
                attention_input(1, k)

    for l in (1, 0):
        base = LAYER_POINTS * (1 - l)
        progress(base)
        if l == 1:
            for k in each:
                gather_finish(dm_all, 0, l, 2, k)
                hidden_back(l, k)
            down_grad(l)
            for k in each:
                ybuf[l, own_rows(k)] = (xres[own_rows(k)] + scatter_finish(l, 1, k)).astype(BF)
                xres[own_rows(k)] = ct_ref[own_rows(k)].astype(F32)
            y_move = remote(ybuf.at[1 - s], ylo, x_s.at[0], x_r.at[0], x_id)
            y_move.start()
            for k in each:
                scatter_start(lambda at, cols: mm_nt(gp_all[l, at], wu[l, cols]), l, 2, k)
        else:
            for k in each:
                gather_pass(dm_all, 0, l, 2, k)
            for k in each:
                gather_finish(dm_all, 0, l, 2, k)
            down_grad(l)
            for k in each:
                hidden_back(l, k)
                scatter_start(lambda at, cols: mm_nt(gp_all[l, at], wu[l, cols]), l, 2, k)
        progress(base + 1)
        up_grad(l)
        progress(base + 2)
        for k in each:
            db = scatter_finish(l, 2, k)
            xh = xh2[l, own_rows(k)]
            gains[l, 1:2] = gains[l, 1:2] + jnp.sum(db * xh, axis=0, keepdims=True)
            dh = xres[own_rows(k)] + normed_back(db, sml[l, 1:2], xh, r2[l, own_rows(k)])
            xres[own_rows(k)] = dh
            da_all[0, block_rows(k, pos)] = dh.astype(BF)
            gather_start(da_all, 0, l, 3, k)
        progress(base + 3)
        for k in each:
            gather_pass(da_all, 0, l, 3, k)
        for k in each:
            gather_finish(da_all, 0, l, 3, k)
        dot_buf[...] = mm_nt(wo[l], da_all[0]).astype(BF)
        grads[l, OUT:QKV] = mm(o_t[l], da_all[0]).astype(BF)
        send_grads(l, OUT // SUB, QKV // SUB)
        progress(base + 4)
        attention_back(l)
        progress(base + 5)
        for k in each:
            scatter_start(lambda at, cols: mm(rows_buf[0, at], wq[l, :, cols]), l, 3, k)
        grads[l, QKV:] = mm(dqkv_t[...], a_all[l]).astype(BF)
        send_grads(l, QKV // SUB, KS)
        progress(base + 6)
        for k in each:
            da = scatter_finish(l, 3, k)
            xh = xh1[l, own_rows(k)]
            gains[l, 0:1] = gains[l, 0:1] + jnp.sum(da * xh, axis=0, keepdims=True)
            dx = xres[own_rows(k)] + normed_back(da, sml[l, 0:1], xh, r1[l, own_rows(k)])
            rounded = dx.astype(BF)
            dxbuf[l, own_rows(k)] = rounded
            if l == 1:
                xres[own_rows(k)] = rounded.astype(F32)
                dm_all[0, block_rows(k, pos)] = rounded
                gather_start(dm_all, 0, 0, 2, k)
            else:
                xres[own_rows(k)] = dx

        progress(base + 7)

        @pl.when(l == s)
        def _():
            ig_out[s] = dxbuf[1].astype(F32) if l == 1 else xres[...]

        @pl.when(l != s)
        def _():
            if chain:
                remote(gains.at[1 - s], gains_x, sm_s.at[0], sm_r.at[0], x_id).start()
                remote(hgains.at[1 - s], hgains_x, sm_s.at[1], sm_r.at[1], x_id).start()
            remote(dxbuf.at[1 - s], dxlo, x_s.at[1], x_r.at[1], x_id).start()

    taken_all = max(len(row) for row in TAKEN)
    for point in range(2 * LAYER_POINTS, taken_all):
        progress(point)
    if chain:
        arrived(gains_x, sm_r.at[0])
        arrived(hgains_x, sm_r.at[1])
        gains_z[b] = gains[s] + gains_x[...]
        hgains_z[b] = hgains[s] + hgains_x[...]
        for i, peer in enumerate(z_ids):
            remote(gains_z.at[b], gains_z.at[b], sm_s.at[2 + i], sm_r.at[2 + i], peer).start()
            remote(hgains_z.at[b], hgains_z.at[b], sm_s.at[5 + i], sm_r.at[5 + i], peer).start()
        progress(taken_all)
        for i in range(3):
            arrived(gains_x, sm_r.at[2 + i])
            arrived(hgains_x, sm_r.at[5 + i])
        gh_out[...] = hgains_z[0] + hgains_z[1] + hgains_z[2] + hgains_z[3]
        gains_t[t] = gains_z[0] + gains_z[1] + gains_z[2] + gains_z[3]
        for i, peer in enumerate((core_id, y_id, diag_id)):
            remote(gains_t.at[t], gains_t.at[t], sm_s.at[8 + i], sm_r.at[8 + i], peer).start()
        progress(taken_all + 1)
        for i in range(3):
            arrived(gains_x, sm_r.at[8 + i])
        gg_out[...] = gains_t[0] + gains_t[1] + gains_t[2] + gains_t[3]
        for point in range(taken_all + 2, last_point):
            progress(point)
    else:
        g_out[...] = grads[...]
        gg_out[...] = gains[...]
        gh_out[...] = hgains[...]
    y_move.wait()
    y_out[s] = ybuf[s]
    y_out[1 - s] = ylo[...]
    finish_weights()
    arrived(dxlo, x_s.at[1])
    arrived(dxlo, x_r.at[1])
    ig_out[1 - s] = dxlo[...].astype(F32)
    if chain:
        finish_grads()
        for i in range(2, 5):
            arrived(gains_x, sm_s.at[i])
            arrived(hgains_x, sm_s.at[3 + i])
            arrived(gains_x, sm_s.at[6 + i])
        arrived(gains_x, sm_s.at[0])
        arrived(hgains_x, sm_s.at[1])


def fused(chain, x, ct, segc, segr, small, qk_gain, wq, wo, wu, wd):
    R, D = x.shape
    N = 4 * R
    QD, HD, FF = wq.shape[0], wo.shape[0], wu.shape[1]
    NH = HD // HEAD
    CH = len(chunks_of(R))
    vmem = pl.BlockSpec(memory_space=pltpu.VMEM)
    hbm = pl.BlockSpec(memory_space=pl.ANY)
    shape = jax.ShapeDtypeStruct
    V = pltpu.VMEM
    dma = pltpu.SemaphoreType.DMA
    G = FF + D + HD + QD
    KS = G // SUB
    ahead = () if chain else (2,)
    extra = [
        V((G, D), BF), V((G, D), BF), V((KS, SUB // 2, D), BF), V((KS, SUB // 2, D), BF),
        V((8, D), F32), V((HEAD, 128), F32), V((4, 8, D), F32), V((4, HEAD, 128), F32), V((4, 8, D), F32),
        dma((KS,)), dma((KS,)), dma((4, KS)), dma((3, KS)), dma((2, KS)), dma((11,)), dma((11,)),
    ]
    if not chain:
        extra = [V((8, 128), F32)] * 9 + [dma((1,))] * 7
    return pl.pallas_call(
        functools.partial(body, chain),
        out_shape=(
            shape((2, R, D), BF),
            shape((2, R, D), F32),
            shape(ahead + (G, D), BF),
            shape(ahead + (8, D), F32),
            shape(ahead + (HEAD, 128), F32),
        ),
        in_specs=[vmem] * 4 + [hbm] * 6,
        out_specs=(vmem, vmem, hbm if chain else vmem, vmem, vmem),
        scratch_shapes=[
            V((2, QD, D), BF), V((2, HD, D), BF), V((2, D, FF), BF), V((2, FF, D), BF),
            V((2, 8, D), F32), V((2, HEAD, 128), F32),
            V((R, D), F32), V((2, R, D), F32), V((2, R, 1), F32), V((2, R, D), F32), V((2, R, 1), F32),
            V((2, N, D), BF), V((2, N, D), BF), V((1, N, D), BF), V((1, N, D), BF),
            V((2, 2 * HD, N), F32), V((2, 2, 8, N), F32), V((2, QD, N), BF), V((2, 8, N), F32),
            V((2, HD, N), BF), V((2, N, FF), BF), V((2, N, FF), BF),
            V((2, N, QD), BF), V((2 * R, D), F32), V((2 * R, D), BF), V((R, D), BF),
            V((2, 2 * R, D), BF), V((2, R, D), BF),
            V((N, N), BF), V((N, N), BF), V((HD, N), BF), V((QD, N), BF),
            V((2, R, D), BF), V((2, R, D), BF), V((R, D), BF), V((R, D), BF),
            V((2, G, D), BF), V((2, 8, D), F32), V((2, HEAD, 128), F32),
            dma((6,)), dma((16,)), dma((16,)), dma((16,)), dma((16,)),
            dma((2, 4, 3, CH)), dma((2, 4, 3, CH)), dma((2, 4, 2, CH)), dma((2, 4, 2, CH)), dma((2,)), dma((2,)),
        ] + extra,
        name="layers",
        compiler_params=pltpu.CompilerParams(
            collective_id=0, has_side_effects=True, vmem_limit_bytes=63 * 2**20
        ),
    )(x, ct, segc, segr, small, qk_gain, wq, wo, wu, wd)


def shards(
    patches, cotangent, image_lengths, attn_gain, qkv_weight, query_gain, key_gain, out_weight,
    mlp_gain, up_weight, down_weight,
):
    s = lax.axis_index("section")
    _, own, D = patches.shape
    seq_len = 4 * own
    R = ceil_to(own, 16)
    N = 4 * R
    HD = out_weight.shape[1]
    NH = HD // HEAD
    pad = ((0, R - own), (0, 0))
    x = jnp.pad(lax.dynamic_index_in_dim(patches, s, 0, keepdims=False), pad)
    ct = jnp.pad(lax.dynamic_index_in_dim(cotangent, s, 0, keepdims=False), pad)
    lengths = lax.dynamic_index_in_dim(image_lengths, s, 0, keepdims=False)[0]
    bounds = jnp.cumsum(lengths, dtype=jnp.int32)
    places = jnp.arange(seq_len, dtype=jnp.int32)
    seg = jnp.sum((places[:, None] >= bounds[None, :]).astype(jnp.int32), axis=-1)
    seg = seg.reshape(2, 2, own).transpose(1, 0, 2).reshape(4, own)
    seg = jnp.pad(seg, ((0, 0), (0, R - own)), constant_values=-1)
    seg = jnp.concatenate([seg[:, a : a + n].reshape(4 * n) for a, n in chunks_of(R)])
    small = jnp.zeros((8, D), F32).at[0].set(attn_gain[0].astype(F32)).at[1].set(mlp_gain[0].astype(F32))
    qk_gain = jnp.concatenate([query_gain[0], key_gain[0]], axis=0).astype(F32).T
    qk_gain = jnp.pad(qk_gain, ((0, 0), (0, 128 - 2 * NH)))
    wq = qkv_weight[0].reshape(D, 3 * HD).T
    chain = lax.axis_size("batch") == 4
    y, ig, g, gg, gh = fused(
        chain, x, ct, seg[:, None], seg[None, :], small, qk_gain, wq, out_weight[0], up_weight[0],
        down_weight[0],
    )
    if not chain:
        theirs = lax.ppermute(g[1 - s], "section", [(0, 1), (1, 0)])
        g = lax.psum((g[s].astype(F32) + theirs.astype(F32)).astype(BF), "batch")
        gg = lax.psum(gg, ("section", "batch", "tensor"))[s]
        gh = lax.psum(gh, ("section", "batch"))[s]
    FF = up_weight.shape[2]
    gd, gu, go, gq = (g[:FF], g[FF : FF + D], g[FF + D : FF + D + HD], g[FF + D + HD :])
    gh = gh[:, : 2 * NH].T.reshape(2, NH, HEAD)
    return (
        y[:, :own][None],
        ig[:, :own][None],
        gg[0][None],
        gq.astype(F32).T.reshape(D, 3, HD)[None],
        gh[0][None],
        gh[1][None],
        go.astype(F32)[None],
        gg[1][None],
        gu.astype(F32)[None],
        gd.astype(F32)[None],
    )


def solution(mesh):
    return jax.shard_map(
        shards,
        mesh=mesh,
        in_specs=(
            P(None, ("batch", "tensor"), None),
            P(None, ("batch", "tensor"), None),
            P(None, "batch", None),
            P("section", None),
            P("section", None, None, "tensor"),
            P("section", "tensor", None),
            P("section", "tensor", None),
            P("section", "tensor", None),
            P("section", None),
            P("section", None, "tensor"),
            P("section", "tensor", None),
        ),
        out_specs=(
            P("section", None, ("batch", "tensor"), None),
            P("section", None, ("batch", "tensor"), None),
            P("section", None),
            P("section", None, None, "tensor"),
            P("section", "tensor", None),
            P("section", "tensor", None),
            P("section", "tensor", None),
            P("section", None),
            P("section", None, "tensor"),
            P("section", "tensor", None),
        ),
        check_vma=False,
    )
```

```python
import functools

import jax
import jax.numpy as jnp
from jax import lax
from jax.experimental import pallas as pl
from jax.experimental.pallas import tpu as pltpu
from jax.sharding import PartitionSpec as P

HEAD = 64
EPS = 1e-06
MESH = pl.DeviceIdType.MESH
BF = jnp.bfloat16
F32 = jnp.float32
KEY_BLOCK = 64
COLS = 256
SUB = 192
CHUNKS = 2
TAKEN = (
    (0, 0, 0, 0, 0, 0, 0, 0, 0, 0, 1, 1, 2, 3, 4, 5) + tuple(range(6, 13)),
    (0, 0, 0, 0, 1, 1, 2, 3, 4, 5, 5, 6, 6, 7, 8, 9) + tuple(range(10, 13)),
)
LAGS = (0, 2, 3, 4, 5)
LAYER_POINTS = 8


def ceil_to(n, m):
    return -(-n // m) * m


def chunks_of(rows):
    step = max(32, rows // CHUNKS // 32 * 32)
    starts = [i * step for i in range(CHUNKS) if i * step < rows]
    return [(a, b - a) for a, b in zip(starts, starts[1:] + [rows])]


def mm(a, b):
    return lax.dot_general(a, b, (((1,), (0,)), ((), ())), preferred_element_type=F32)


def mm_nt(a, b):
    return lax.dot_general(a, b, (((1,), (1,)), ((), ())), preferred_element_type=F32)


def mm_tn(a, b):
    return lax.dot_general(a, b, (((0,), (0,)), ((), ())), preferred_element_type=F32)


def normed(v):
    centre = v - jnp.mean(v, axis=-1, keepdims=True)
    r = lax.rsqrt(jnp.mean(centre * centre, axis=-1, keepdims=True) + EPS)
    return centre * r, r


def normed_back(dv, gain, xh, r):
    g = dv * gain
    return r * (g - jnp.mean(g, axis=-1, keepdims=True) - xh * jnp.mean(g * xh, axis=-1, keepdims=True))


def body(
    chain,
    x_ref, ct_ref, len_ref, again_ref, mgain_ref, qgain_ref, kgain_ref, wq_in, wo_in, wu_in, wd_in,
    y_out, ig_out, g_out, gg_out, gh_out,
    wq, wo, wu, wd, sml, qkg, segc_ref, segr_ref, square,
    xres, xh1, r1, xh2, r2,
    a_all, b_all, dm_all, da_all,
    qkh, qkr, qkvb, lse, o_t, g_all, gp_all,
    rows_buf, part, sendbuf, ysend, crecv, yrecv,
    e_buf, d_buf, dot_buf, dqkv_t,
    ybuf, dxbuf, ylo, dxlo,
    grads, gains, hgains,
    w_loc, w_send, w_recv, wz_s, wz_r, ag_s, ag_r, rs_s, rs_r, x_s, x_r,
    gx, gz, gpart, gfin, gains_x, hgains_x, gains_z, hgains_z, gains_t,
    gx_s, gx_r, gz_s, gz_r, g_loc, sm_s, sm_r,
):
    s, b, t = lax.axis_index("section"), lax.axis_index("batch"), lax.axis_index("tensor")
    y, c = t // 2, lax.rem(t, 2)
    core_id = (s, b, y * 2 + 1 - c)
    y_id = (s, b, (1 - y) * 2 + c)
    x_id = (1 - s, b, t)
    own, D = x_ref.shape[1:]
    R = ceil_to(own, 16)
    N = 4 * R
    FF = wu.shape[2]
    HD = wo.shape[1]
    NH = HD // HEAD
    NB = N // KEY_BLOCK
    pos = c * 2 + y
    ypos = c * 2 + 1 - y
    CH = chunks_of(R)

    def block_rows(k, at):
        off, n = CH[k]
        return pl.ds(pl.multiple_of(4 * off + at * n, 16), n)

    def own_rows(k):
        return pl.ds(CH[k][0], CH[k][1])

    diag_id = (s, b, (1 - y) * 2 + 1 - c)
    z_ids = [(s, lax.rem(b + k, 4), t) for k in (1, 2, 3)] if chain else []
    barrier = pltpu.get_barrier_semaphore()
    for peer in [core_id, y_id, diag_id, x_id] + z_ids:
        pl.semaphore_signal(barrier, inc=1, device_id=peer, device_id_type=MESH)
    pl.semaphore_wait(barrier, 4 + len(z_ids))

    def remote(src, dst, ss, rs, peer):
        return pltpu.make_async_remote_copy(
            src_ref=src, dst_ref=dst, send_sem=ss, recv_sem=rs, device_id=peer, device_id_type=MESH
        )

    def arrived(ref, sem):
        pltpu.make_async_copy(ref, ref, sem).wait()

    sml[s] = jnp.zeros(sml.shape[1:], F32)
    sml[s, 0:1] = again_ref[...].astype(F32)
    sml[s, 1:2] = mgain_ref[...].astype(F32)
    square[...] = jnp.zeros_like(square)
    square[0:NH, 0:HEAD] = qgain_ref[0].astype(F32)
    square[NH : 2 * NH, 0:HEAD] = kgain_ref[0].astype(F32)
    qkg[s] = square[...].T[0:HEAD]
    moves = ((sml.at[s], sml), (qkg.at[s], qkg), (wq_in, wq), (wo_in, wo), (wu_in, wu), (wd_in, wd))
    pair_id = (s, b + 1 - 2 * lax.rem(b, 2), t)
    near = lax.rem(b, 2)
    blocks = []
    for i in range(2, 6):
        rows = moves[i][0].shape[0]
        step = min(rows, 2 * SUB if i > 3 else SUB)
        blocks += [(i, at, step) for at in range(0, rows, step)]

    def half_block(ref, j, h):
        _, at, n = blocks[j]
        return ref.at[pl.ds(pl.multiple_of(at + h * (n // 2), 16), n // 2)]

    def send_block(j):
        src, dst = moves[blocks[j][0]]
        if chain:
            remote(half_block(src, j, near), half_block(dst.at[s], j, near), w_send.at[j], w_recv.at[j], x_id).start()
        else:
            _, at, n = blocks[j]
            remote(src.at[at : at + n], dst.at[s, at : at + n], w_send.at[j], w_recv.at[j], x_id).start()

    def forward_blocks(lo, hi):
        if chain:
            for j in range(lo, hi):
                got = half_block(moves[blocks[j][0]][1].at[1 - s], j, near)
                arrived(got, w_recv.at[j])
                remote(got, got, wz_s.at[j], wz_r.at[j], pair_id).start()

    for i, (src, dst) in enumerate(moves):
        if i < 2:
            remote(src, dst.at[s], w_send.at[len(blocks) + i], w_recv.at[len(blocks) + i], x_id).start()
        else:
            for j in range(len(blocks)):
                if blocks[j][0] == i:
                    send_block(j)
            pltpu.make_async_copy(src, dst.at[s], w_loc.at[i]).start()

    def weights_here(l, i):
        src, dst = moves[i]

        if i > 1:

            @pl.when(l == s)
            def _():
                pltpu.make_async_copy(src, dst.at[s], w_loc.at[i]).wait()

        @pl.when(l != s)
        def _():
            if i < 2:
                arrived(dst.at[1 - s], w_recv.at[len(blocks) + i])
            for j in range(len(blocks)):
                if blocks[j][0] == i:
                    if chain:
                        arrived(half_block(dst.at[1 - s], j, 1 - near), wz_r.at[j])
                    else:
                        _, at, n = blocks[j]
                        arrived(dst.at[1 - s, at : at + n], w_recv.at[j])

    def finish_weights():
        for i in range(2):
            arrived(moves[i][1].at[s], w_send.at[len(blocks) + i])
        for j in range(len(blocks)):
            i, at, n = blocks[j]
            if chain:
                arrived(half_block(moves[i][1].at[s], j, near), w_send.at[j])
                arrived(half_block(moves[i][1].at[1 - s], j, near), wz_s.at[j])
            else:
                arrived(moves[i][1].at[s, at : at + n], w_send.at[j])

    def gather_start(buf, slot, l, op, k):
        mine = buf.at[slot, block_rows(k, pos)]
        remote(mine, mine, ag_s.at[l, op, 0, k], ag_r.at[l, op, 0, k], core_id).start()
        remote(mine, mine, ag_s.at[l, op, 1, k], ag_r.at[l, op, 1, k], y_id).start()

    def gather_pass(buf, slot, l, op, k):
        theirs = buf.at[slot, block_rows(k, ypos)]
        arrived(theirs, ag_r.at[l, op, 1, k])
        remote(theirs, theirs, ag_s.at[l, op, 2, k], ag_r.at[l, op, 2, k], core_id).start()

    def gather_finish(buf, slot, l, op, k):
        mine = buf.at[slot, block_rows(k, pos)]
        arrived(mine, ag_r.at[l, op, 0, k])
        arrived(mine, ag_r.at[l, op, 2, k])
        arrived(mine, ag_s.at[l, op, 0, k])
        arrived(mine, ag_s.at[l, op, 1, k])
        arrived(mine, ag_s.at[l, op, 2, k])

    def pair_rows(k):
        return pl.ds(2 * CH[k][0], 2 * CH[k][1])

    def scatter_start(product, l, op, k):
        slot = op % 2
        off, n = CH[k]

        def send_tile(j, carry):
            cols = pl.ds(pl.multiple_of(j * COLS, COLS), COLS)
            at = pl.ds(pl.multiple_of(4 * off + (1 - c) * 2 * n, 16), 2 * n)
            sendbuf[pair_rows(k), cols] = product(at, cols).astype(BF)
            return carry

        lax.fori_loop(0, D // COLS, send_tile, 0)
        mine = sendbuf.at[pair_rows(k)]
        remote(mine, crecv.at[slot, pair_rows(k)], rs_s.at[l, op, 0, k], rs_r.at[l, op, 0, k], core_id).start()

        def own_tile(j, carry):
            cols = pl.ds(pl.multiple_of(j * COLS, COLS), COLS)
            at = pl.ds(pl.multiple_of(4 * off + c * 2 * n, 16), 2 * n)
            part[pair_rows(k), cols] = product(at, cols)
            return carry

        lax.fori_loop(0, D // COLS, own_tile, 0)
        arrived(mine, rs_r.at[l, op, 0, k])
        other = pl.ds(pl.multiple_of(2 * off + (1 - y) * n, 16), n)
        ysend[own_rows(k)] = (part[other] + crecv[slot, other].astype(F32)).astype(BF)
        remote(
            ysend.at[own_rows(k)], yrecv.at[slot, own_rows(k)], rs_s.at[l, op, 1, k], rs_r.at[l, op, 1, k], y_id
        ).start()

    def scatter_finish(l, op, k):
        slot = op % 2
        off, n = CH[k]
        mine = pl.ds(pl.multiple_of(2 * off + y * n, 16), n)
        arrived(sendbuf.at[pair_rows(k)], rs_s.at[l, op, 0, k])
        arrived(ysend.at[own_rows(k)], rs_s.at[l, op, 1, k])
        arrived(ysend.at[own_rows(k)], rs_r.at[l, op, 1, k])
        return part[mine] + crecv[slot, mine].astype(F32) + yrecv[slot, own_rows(k)].astype(F32)

    FD, UP, OUT = 0, FF, FF + D
    QKV = OUT + HD
    KS = grads.shape[1] // SUB
    HALF = SUB // 2
    middle = (b == 1) | (b == 2)
    end = jnp.logical_not(middle)
    inner_id = (s, jnp.where(b == 0, 1, 2), t)
    outer_id = (s, jnp.where(b == 1, 0, 3), t)
    partner_id = (s, jnp.where(b == 1, 2, 1), t)
    mine_at = jnp.where(b == 1, 0, HALF)
    other_at = HALF - mine_at

    def sub_rows(k):
        return pl.ds(pl.multiple_of(k * SUB, 16), SUB)

    def half_rows(k, at):
        return pl.ds(pl.multiple_of(k * SUB + at, 16), HALF)

    def send_grads(l, lo, hi):
        if not chain:
            return

        @pl.when(l != s)
        def _():
            def one(k, carry):
                rows = sub_rows(k)
                remote(grads.at[l, rows], gx.at[rows], gx_s.at[k], gx_r.at[k], x_id).start()
                return carry

            lax.fori_loop(lo, hi, one, 0)

    def step1(k, carry):
        rows = sub_rows(k)
        arrived(gx.at[rows], gx_r.at[k])
        grads[s, rows] = (grads[s, rows].astype(F32) + gx[rows].astype(F32)).astype(BF)

        @pl.when(end)
        def _():
            remote(grads.at[s, rows], gz.at[rows], gz_s.at[0, k], gz_r.at[0, k], inner_id).start()

        return carry

    def step2(k, carry):
        @pl.when(middle)
        def _():
            rows = sub_rows(k)
            arrived(gz.at[rows], gz_r.at[0, k])
            grads[s, rows] = (grads[s, rows].astype(F32) + gz[rows].astype(F32)).astype(BF)
            other = grads.at[s, half_rows(k, other_at)]
            remote(other, gpart.at[k], gz_s.at[0, k], gz_r.at[1, k], partner_id).start()

        return carry

    def step3(k, carry):
        @pl.when(middle)
        def _():
            rows = half_rows(k, mine_at)
            arrived(gpart.at[k], gz_r.at[1, k])
            grads[s, rows] = (grads[s, rows].astype(F32) + gpart[k].astype(F32)).astype(BF)
            done = grads.at[s, rows]
            remote(done, gfin.at[k], gz_s.at[1, k], gz_r.at[2, k], partner_id).start()
            remote(done, gz.at[rows], gz_s.at[2, k], gz_r.at[0, k], outer_id).start()
            pltpu.make_async_copy(done, g_out.at[rows], g_loc.at[0, k]).start()

        return carry

    def step4(k, carry):
        @pl.when(middle)
        def _():
            rows = half_rows(k, other_at)
            arrived(gfin.at[k], gz_r.at[2, k])
            remote(gfin.at[k], gz.at[rows], gz_s.at[3, k], gz_r.at[1, k], outer_id).start()
            pltpu.make_async_copy(gfin.at[k], g_out.at[rows], g_loc.at[1, k]).start()

        return carry

    def step5(k, carry):
        @pl.when(end)
        def _():
            rows = sub_rows(k)
            arrived(gz.at[half_rows(k, 0)], gz_r.at[0, k])
            arrived(gz.at[half_rows(k, HALF)], gz_r.at[1, k])
            pltpu.make_async_copy(gz.at[rows], g_out.at[rows], g_loc.at[0, k]).start()

        return carry

    steps = (step1, step2, step3, step4, step5)
    last_point = max(len(row) for row in TAKEN) + LAGS[-1]

    def progress(point):
        if not chain:
            return

        def taken(p):
            first, second = ((0 if p < 0 else row[min(p, len(row) - 1)]) for row in TAKEN)
            return first if first == second else jnp.where(s == 0, first, second)

        for step, lag in zip(steps, LAGS):
            lo, hi = taken(point - lag - 1), taken(point - lag)
            if not (isinstance(lo, int) and isinstance(hi, int) and lo == hi):
                lax.fori_loop(lo, hi, step, 0)

    def finish_grads():
        def one(k, carry):
            rows = sub_rows(k)
            half = grads.at[1 - s, half_rows(k, 0)]
            arrived(grads.at[1 - s, rows], gx_s.at[k])

            @pl.when(end)
            def _():
                arrived(grads.at[s, rows], gz_s.at[0, k])
                arrived(g_out.at[rows], g_loc.at[0, k])

            @pl.when(middle)
            def _():
                for j in range(4):
                    arrived(half, gz_s.at[j, k])
                for j in range(2):
                    arrived(g_out.at[half_rows(k, 0)], g_loc.at[j, k])

            return carry

        lax.fori_loop(0, KS, one, 0)

    def q_rows(h):
        return pl.ds(pl.multiple_of(h * HEAD, HEAD), HEAD)

    def segments():
        wide = lax.broadcasted_iota(jnp.int32, (128, 128), 1)
        tall = lax.broadcasted_iota(jnp.int32, (128, 128), 0)
        slots = len_ref.shape[2]
        square[...] = jnp.zeros_like(square)
        square[0:1, 0:slots] = len_ref[s].astype(F32)
        row = jnp.broadcast_to(square[0:1], (128, 128))
        column = row.T
        column_sums = jnp.sum(jnp.where(wide <= tall, row, 0.0), axis=1, keepdims=True)
        row_sums = jnp.sum(jnp.where(tall <= wide, column, 0.0), axis=0, keepdims=True)
        used = (lax.broadcasted_iota(jnp.int32, (128, 1), 0) < slots).astype(F32)
        used_row = (lax.broadcasted_iota(jnp.int32, (1, 128), 1) < slots).astype(F32)
        lane = lax.broadcasted_iota(jnp.int32, (1, N), 1)
        place = lane
        padding = jnp.zeros((1, N), F32)
        for off, n in CH:
            for at in range(4):
                start = 4 * off + at * n
                device = at % 2 * 2 + at // 2
                here = lane >= start
                place = jnp.where(here, lane - start + device * own + off, place)
                padding = jnp.where(here, jnp.where(lane - start + off >= own, 1.0, 0.0), padding)
                r = lax.broadcasted_iota(jnp.int32, (n, 1), 0) + off
                after = jnp.where((r + device * own).astype(F32) >= row_sums, used_row, 0.0)
                seg = jnp.sum(after, axis=1, keepdims=True)
                segc_ref[start : start + n] = jnp.where(r >= own, -1.0, seg)
        seg = jnp.sum(jnp.where(place.astype(F32) >= column_sums, used, 0.0), axis=0, keepdims=True)
        segr_ref[...] = jnp.where(padding > 0, -1.0, seg)

    def padded_rows(ref, k):
        off, n = CH[k]
        v = ref[s, off : min(off + n, own)].astype(F32)
        if off + n > own:
            v = jnp.concatenate([v, jnp.zeros((off + n - own, D), F32)], axis=0)
        return v

    def attention_input(l, k):
        xh, r = normed(xres[own_rows(k)])
        xh1[l, own_rows(k)] = xh
        r1[l, own_rows(k)] = r
        a_all[l, block_rows(k, pos)] = (xh * sml[l, 0:1]).astype(BF)
        gather_start(a_all, l, l, 0, k)

    def project(l, k):
        off, n = CH[k]
        rows, lanes = slice(4 * off, 4 * (off + n)), slice(4 * off, 4 * (off + n))

        def query_key(i, carry):
            at = pl.ds(pl.multiple_of(i * HD, HEAD), HD)
            v = mm_nt(wq[l, at], a_all[l, rows])
            for h in range(NH):
                u = v[h * HEAD : (h + 1) * HEAD]
                u = u - jnp.mean(u, axis=0, keepdims=True)
                rr = lax.rsqrt(jnp.mean(u * u, axis=0, keepdims=True) + EPS)
                u = u * rr
                at = pl.ds(pl.multiple_of(i * HD + h * HEAD, HEAD), HEAD)
                qkh[l, at, lanes] = u
                qkr[l, i, pl.ds(h, 1), lanes] = rr
                scale = jnp.where(i == 0, HEAD**-0.5, 1.0).astype(F32)
                gain = jnp.where(i == 0, qkg[l, :, h : h + 1], qkg[l, :, NH + h : NH + h + 1])
                qkvb[l, at, lanes] = ((u * gain).astype(BF).astype(F32) * scale).astype(BF)
            return carry

        lax.fori_loop(0, 2, query_key, 0)
        qkvb[l, 2 * HD :, lanes] = mm_nt(wq[l, 2 * HD :], a_all[l, rows]).astype(BF)

    def attention(l):
        def head(h, carry):
            q_t = qkvb[l, q_rows(h)]
            v_t = qkvb[l, q_rows(2 * NH + h)]
            rows_buf[0, :, :HEAD] = qkvb[l, q_rows(NH + h)].astype(F32).T.astype(BF)

            def block(i, total):
                at = pl.ds(pl.multiple_of(i * KEY_BLOCK, KEY_BLOCK), KEY_BLOCK)
                sc = mm(rows_buf[0, at, :HEAD], q_t)
                e = jnp.where(segc_ref[at] == segr_ref[...], jnp.exp(sc), 0.0)
                e_buf[at] = e.astype(BF)
                return total + jnp.sum(e, axis=0, keepdims=True)

            total = lax.fori_loop(0, NB, block, jnp.zeros((1, N), F32))
            lse[l, pl.ds(h, 1)] = jnp.log(total)
            o_t[l, q_rows(h)] = (mm(v_t, e_buf[...]) * (1.0 / total)).astype(BF)
            return carry

        lax.fori_loop(0, NH, head, 0)
        rows_buf[1, :, :HD] = o_t[l].astype(F32).T.astype(BF)

    def hidden(l, k):
        off, n = CH[k]

        def tile(i, carry):
            rows = pl.ds(pl.multiple_of(4 * off + lax.rem(i, 2) * 2 * n, 16), 2 * n)
            cols = pl.ds(pl.multiple_of((i // 2) * COLS, COLS), COLS)
            u = mm(b_all[l, rows], wu[l, :, cols])
            cdf = 0.5 * (1.0 + lax.erf(u * 0.7071067811865476))
            pdf = jnp.exp(-0.5 * u * u) * 0.3989422804014327
            g_all[l, rows, cols] = (u * cdf).astype(BF)
            gp_all[l, rows, cols] = (cdf + u * pdf).astype(BF)
            return carry

        lax.fori_loop(0, 2 * (FF // COLS), tile, 0)

    def hidden_back(l, k):
        off, n = CH[k]

        def tile(i, carry):
            rows = pl.ds(pl.multiple_of(4 * off + lax.rem(i, 2) * 2 * n, 16), 2 * n)
            cols = pl.ds(pl.multiple_of((i // 2) * COLS, COLS), COLS)
            dg = mm_nt(dm_all[0, rows], wd[l, cols])
            gp_all[l, rows, cols] = (dg * gp_all[l, rows, cols].astype(F32)).astype(BF)
            return carry

        lax.fori_loop(0, 2 * (FF // COLS), tile, 0)

    def down_grad(l):
        def tile(i, carry):
            cols = pl.ds(pl.multiple_of(i * COLS, COLS), COLS)
            at = pl.ds(pl.multiple_of(FD + i * COLS, COLS), COLS)
            grads[l, at] = mm_tn(g_all[l, :, cols], dm_all[0]).astype(BF)
            return carry

        lax.fori_loop(0, FF // COLS, tile, 0)
        send_grads(l, 0, UP // SUB)

    def up_grad(l):
        def tile(i, carry):
            cols = pl.ds(pl.multiple_of(i * COLS, COLS), COLS)
            at = pl.ds(pl.multiple_of(UP + i * COLS, COLS), COLS)
            grads[l, at] = mm_tn(b_all[l, :, cols], gp_all[l]).astype(BF)
            return carry

        lax.fori_loop(0, D // COLS, tile, 0)
        send_grads(l, UP // SUB, OUT // SUB)

    def gains_of(l, i, h):
        out = qkg[l, :, i * NH : i * NH + 1]
        for k in range(1, NH):
            out = jnp.where(h == k, qkg[l, :, i * NH + k : i * NH + k + 1], out)
        return out

    def attention_back(l):
        def head(h, carry):
            q_t = qkvb[l, q_rows(h)]
            k_t = qkvb[l, q_rows(NH + h)]
            v_t = qkvb[l, q_rows(2 * NH + h)]
            rows_buf[0, :, :HEAD] = k_t.astype(F32).T.astype(BF)
            rows_buf[1, :, :HEAD] = v_t.astype(F32).T.astype(BF)
            do_t = dot_buf[q_rows(h)]
            delta = jnp.sum(do_t.astype(F32) * o_t[l, q_rows(h)].astype(F32), axis=0, keepdims=True)
            log_total = lse[l, pl.ds(h, 1)]

            def block(i, carry):
                at = pl.ds(pl.multiple_of(i * KEY_BLOCK, KEY_BLOCK), KEY_BLOCK)
                sc = mm(rows_buf[0, at, :HEAD], q_t)
                p = jnp.where(segc_ref[at] == segr_ref[...], jnp.exp(sc - log_total), 0.0)
                dp = mm(rows_buf[1, at, :HEAD], do_t)
                e_buf[at] = p.astype(BF)
                d_buf[at] = (p * (dp - delta)).astype(BF)
                return carry

            lax.fori_loop(0, NB, block, 0)
            dqkv_t[q_rows(2 * NH + h)] = mm_nt(do_t, e_buf[...]).astype(BF)
            dk = mm_nt(q_t, d_buf[...])
            dq = mm(k_t, d_buf[...]) * (HEAD**-0.5)
            for i, dv in ((0, dq), (1, dk)):
                at = q_rows(i * NH + h)
                dv = dv.astype(BF).astype(F32)
                uh = qkh[l, at]
                lanes = lax.broadcasted_iota(jnp.int32, (HEAD, 128), 1) == i * NH + h
                hgains[l] = jnp.where(lanes, jnp.sum(dv * uh, axis=1, keepdims=True), hgains[l])
                g = dv * gains_of(l, i, h)
                back = g - jnp.mean(g, axis=0, keepdims=True) - uh * jnp.mean(g * uh, axis=0, keepdims=True)
                dqkv_t[at] = (qkr[l, i, pl.ds(h, 1)] * back).astype(BF)
            return carry

        hgains[l] = jnp.zeros((HEAD, 128), F32)
        lax.fori_loop(0, NH, head, 0)
        rows_buf[0] = dqkv_t[...].astype(F32).T.astype(BF)

    each = range(len(CH))
    gains[...] = jnp.zeros_like(gains)

    for l in range(2):
        if l == 0:
            weights_here(l, 0)
            weights_here(l, 1)
            for k in each:
                xres[own_rows(k)] = padded_rows(x_ref, k)
                attention_input(l, k)
                dm_all[0, block_rows(k, pos)] = padded_rows(ct_ref, k).astype(BF)
            segments()
            forward_blocks(0, 3)
        else:
            weights_here(l, 1)
        weights_here(l, 2)
        for k in each:
            gather_pass(a_all, l, l, 0, k)
        for k in each:
            gather_finish(a_all, l, l, 0, k)
            project(l, k)
        if l == 0:
            for k in each:
                gather_start(dm_all, 0, 1, 2, k)
            forward_blocks(3, 4)
        attention(l)
        if l == 0:
            forward_blocks(4, 6)
            for k in each:
                gather_pass(dm_all, 0, 1, 2, k)
        weights_here(l, 3)
        for k in each:
            scatter_start(lambda at, cols: mm(rows_buf[1, at, :HD], wo[l, :, cols]), l, 0, k)
        if l == 0:
            forward_blocks(6, 7)
        for k in each:
            residual = xres[own_rows(k)] + scatter_finish(l, 0, k)
            xres[own_rows(k)] = residual
            xh, r = normed(residual)
            xh2[l, own_rows(k)] = xh
            r2[l, own_rows(k)] = r
            b_all[l, block_rows(k, pos)] = (xh * sml[l, 1:2]).astype(BF)
            gather_start(b_all, l, l, 1, k)
        if l == 0:
            forward_blocks(7, len(blocks))
        weights_here(l, 4)
        gather_pass(b_all, l, l, 1, 0)
        for k in each:
            gather_finish(b_all, l, l, 1, k)
            hidden(l, k)
            if k + 1 < len(CH):
                gather_pass(b_all, l, l, 1, k + 1)
            if k == 0:
                weights_here(l, 5)
            scatter_start(lambda at, cols: mm(g_all[l, at], wd[l, :, cols]), l, 1, k)
        if l == 0:
            for k in each:
                rounded = (xres[own_rows(k)] + scatter_finish(l, 1, k)).astype(BF)
                ybuf[l, own_rows(k)] = rounded
                xres[own_rows(k)] = rounded.astype(F32)
                if k == 0:
                    weights_here(1, 0)
                attention_input(1, k)

    for l in (1, 0):
        base = LAYER_POINTS * (1 - l)
        progress(base)
        if l == 1:
            for k in each:
                gather_finish(dm_all, 0, l, 2, k)
                hidden_back(l, k)
            down_grad(l)
            for k in each:
                ybuf[l, own_rows(k)] = (xres[own_rows(k)] + scatter_finish(l, 1, k)).astype(BF)
                xres[own_rows(k)] = padded_rows(ct_ref, k)
            y_move = remote(ybuf.at[1 - s], ylo, x_s.at[0], x_r.at[0], x_id)
            y_move.start()
            for k in each:
                scatter_start(lambda at, cols: mm_nt(gp_all[l, at], wu[l, cols]), l, 2, k)
        else:
            for k in each:
                gather_pass(dm_all, 0, l, 2, k)
            for k in each:
                gather_finish(dm_all, 0, l, 2, k)
            down_grad(l)
            for k in each:
                hidden_back(l, k)
                scatter_start(lambda at, cols: mm_nt(gp_all[l, at], wu[l, cols]), l, 2, k)
        progress(base + 1)
        up_grad(l)
        progress(base + 2)
        for k in each:
            db = scatter_finish(l, 2, k)
            xh = xh2[l, own_rows(k)]
            gains[l, 1:2] = gains[l, 1:2] + jnp.sum(db * xh, axis=0, keepdims=True)
            dh = xres[own_rows(k)] + normed_back(db, sml[l, 1:2], xh, r2[l, own_rows(k)])
            xres[own_rows(k)] = dh
            da_all[0, block_rows(k, pos)] = dh.astype(BF)
            gather_start(da_all, 0, l, 3, k)
        progress(base + 3)
        for k in each:
            gather_pass(da_all, 0, l, 3, k)
        for k in each:
            gather_finish(da_all, 0, l, 3, k)
        dot_buf[...] = mm_nt(wo[l], da_all[0]).astype(BF)
        grads[l, OUT:QKV] = mm(o_t[l], da_all[0]).astype(BF)
        send_grads(l, OUT // SUB, QKV // SUB)
        progress(base + 4)
        attention_back(l)
        progress(base + 5)
        for k in each:
            scatter_start(lambda at, cols: mm(rows_buf[0, at], wq[l, :, cols]), l, 3, k)
        grads[l, QKV:] = mm(dqkv_t[...], a_all[l]).astype(BF)
        send_grads(l, QKV // SUB, KS)
        progress(base + 6)
        for k in each:
            da = scatter_finish(l, 3, k)
            xh = xh1[l, own_rows(k)]
            gains[l, 0:1] = gains[l, 0:1] + jnp.sum(da * xh, axis=0, keepdims=True)
            dx = xres[own_rows(k)] + normed_back(da, sml[l, 0:1], xh, r1[l, own_rows(k)])
            rounded = dx.astype(BF)
            dxbuf[l, own_rows(k)] = rounded
            if l == 1:
                xres[own_rows(k)] = rounded.astype(F32)
                dm_all[0, block_rows(k, pos)] = rounded
                gather_start(dm_all, 0, 0, 2, k)
            else:
                xres[own_rows(k)] = dx

        progress(base + 7)

        @pl.when(l == s)
        def _():
            ig_out[s] = dxbuf[1, 0:own].astype(F32) if l == 1 else xres[0:own]

        @pl.when(l != s)
        def _():
            if chain:
                remote(gains.at[1 - s], gains_x, sm_s.at[0], sm_r.at[0], x_id).start()
                remote(hgains.at[1 - s], hgains_x, sm_s.at[1], sm_r.at[1], x_id).start()
            remote(dxbuf.at[1 - s], dxlo, x_s.at[1], x_r.at[1], x_id).start()

    taken_all = max(len(row) for row in TAKEN)
    for point in range(2 * LAYER_POINTS, taken_all):
        progress(point)
    if chain:
        arrived(gains_x, sm_r.at[0])
        arrived(hgains_x, sm_r.at[1])
        gains_z[b] = gains[s] + gains_x[...]
        hgains_z[b] = hgains[s] + hgains_x[...]
        for i, peer in enumerate(z_ids):
            remote(gains_z.at[b], gains_z.at[b], sm_s.at[2 + i], sm_r.at[2 + i], peer).start()
            remote(hgains_z.at[b], hgains_z.at[b], sm_s.at[5 + i], sm_r.at[5 + i], peer).start()
        progress(taken_all)
        for i in range(3):
            arrived(gains_x, sm_r.at[2 + i])
            arrived(hgains_x, sm_r.at[5 + i])
        gh_out[...] = hgains_z[0] + hgains_z[1] + hgains_z[2] + hgains_z[3]
        gains_t[t] = gains_z[0] + gains_z[1] + gains_z[2] + gains_z[3]
        for i, peer in enumerate((core_id, y_id, diag_id)):
            remote(gains_t.at[t], gains_t.at[t], sm_s.at[8 + i], sm_r.at[8 + i], peer).start()
        progress(taken_all + 1)
        for i in range(3):
            arrived(gains_x, sm_r.at[8 + i])
        gg_out[...] = gains_t[0] + gains_t[1] + gains_t[2] + gains_t[3]
        for point in range(taken_all + 2, last_point):
            progress(point)
    else:
        g_out[...] = grads[...]
        gg_out[...] = gains[...]
        gh_out[...] = hgains[...]
    y_move.wait()
    y_out[s] = ybuf[s, 0:own]
    y_out[1 - s] = ylo[0:own]
    finish_weights()
    arrived(dxlo, x_s.at[1])
    arrived(dxlo, x_r.at[1])
    ig_out[1 - s] = dxlo[0:own].astype(F32)
    if chain:
        finish_grads()
        for i in range(2, 5):
            arrived(gains_x, sm_s.at[i])
            arrived(hgains_x, sm_s.at[3 + i])
            arrived(gains_x, sm_s.at[6 + i])
        arrived(gains_x, sm_s.at[0])
        arrived(hgains_x, sm_s.at[1])


def fused(chain, x, ct, lengths, again, mgain, qgain, kgain, wq, wo, wu, wd):
    own, D = x.shape[1:]
    R = ceil_to(own, 16)
    N = 4 * R
    QD, HD, FF = wq.shape[0], wo.shape[0], wu.shape[1]
    NH = HD // HEAD
    CH = len(chunks_of(R))
    vmem = pl.BlockSpec(memory_space=pltpu.VMEM)
    hbm = pl.BlockSpec(memory_space=pl.ANY)
    shape = jax.ShapeDtypeStruct
    V = pltpu.VMEM
    dma = pltpu.SemaphoreType.DMA
    G = FF + D + HD + QD
    KS = G // SUB
    ahead = () if chain else (2,)
    extra = [
        V((G, D), BF), V((G, D), BF), V((KS, SUB // 2, D), BF), V((KS, SUB // 2, D), BF),
        V((8, D), F32), V((HEAD, 128), F32), V((4, 8, D), F32), V((4, HEAD, 128), F32), V((4, 8, D), F32),
        dma((KS,)), dma((KS,)), dma((4, KS)), dma((3, KS)), dma((2, KS)), dma((11,)), dma((11,)),
    ]
    if not chain:
        extra = [V((8, 128), F32)] * 9 + [dma((1,))] * 7
    return pl.pallas_call(
        functools.partial(body, chain),
        out_shape=(
            shape((2, own, D), BF),
            shape((2, own, D), F32),
            shape(ahead + (G, D), BF),
            shape(ahead + (8, D), F32),
            shape(ahead + (HEAD, 128), F32),
        ),
        in_specs=[vmem] * 7 + [hbm] * 4,
        out_specs=(vmem, vmem, hbm if chain else vmem, vmem, vmem),
        scratch_shapes=[
            V((2, QD, D), BF), V((2, HD, D), BF), V((2, D, FF), BF), V((2, FF, D), BF),
            V((2, 8, D), F32), V((2, HEAD, 128), F32), V((N, 1), F32), V((1, N), F32), V((128, 128), F32),
            V((R, D), F32), V((2, R, D), F32), V((2, R, 1), F32), V((2, R, D), F32), V((2, R, 1), F32),
            V((2, N, D), BF), V((2, N, D), BF), V((1, N, D), BF), V((1, N, D), BF),
            V((2, 2 * HD, N), F32), V((2, 2, 8, N), F32), V((2, QD, N), BF), V((2, 8, N), F32),
            V((2, HD, N), BF), V((2, N, FF), BF), V((2, N, FF), BF),
            V((2, N, QD), BF), V((2 * R, D), F32), V((2 * R, D), BF), V((R, D), BF),
            V((2, 2 * R, D), BF), V((2, R, D), BF),
            V((N, N), BF), V((N, N), BF), V((HD, N), BF), V((QD, N), BF),
            V((2, R, D), BF), V((2, R, D), BF), V((R, D), BF), V((R, D), BF),
            V((2, G, D), BF), V((2, 8, D), F32), V((2, HEAD, 128), F32),
            dma((6,)), dma((16,)), dma((16,)), dma((16,)), dma((16,)),
            dma((2, 4, 3, CH)), dma((2, 4, 3, CH)), dma((2, 4, 2, CH)), dma((2, 4, 2, CH)), dma((2,)), dma((2,)),
        ] + extra,
        name="layers",
        compiler_params=pltpu.CompilerParams(
            collective_id=0, has_side_effects=True, vmem_limit_bytes=63 * 2**20
        ),
    )(x, ct, lengths, again, mgain, qgain, kgain, wq, wo, wu, wd)


def widen(
    y_in, ig_in, g_in, gg_ref, gh_ref,
    y_out, ig_out, gd_out, gu_out, go_out, gq_out, gattn_out, gmlp_out, gqg_out, gkg_out,
    low, wide, y_buf, ig_buf, in_sem, out_sem, move_sem,
):
    fetch = [
        pltpu.make_async_copy(y_in, y_buf, move_sem.at[0]),
        pltpu.make_async_copy(ig_in, ig_buf, move_sem.at[1]),
    ]
    put = [
        pltpu.make_async_copy(y_buf, y_out, move_sem.at[2]),
        pltpu.make_async_copy(ig_buf, ig_out, move_sem.at[3]),
    ]
    pieces = []
    at = 0
    for out in (gd_out, gu_out, go_out, gq_out):
        for row in range(0, out.shape[0], SUB):
            pieces.append((at, row, out))
            at += SUB
    loads = [pltpu.make_async_copy(g_in.at[a : a + SUB], low.at[a : a + SUB], in_sem.at[i]) for i, (a, _, _) in enumerate(pieces)]
    stores = [
        pltpu.make_async_copy(wide.at[a : a + SUB], out.at[row : row + SUB], out_sem.at[i])
        for i, (a, row, out) in enumerate(pieces)
    ]
    for copy in fetch + loads:
        copy.start()
    gattn_out[...] = gg_ref[0:1]
    gmlp_out[...] = gg_ref[1:2]
    heads = gqg_out.shape[0]
    by_head = gh_ref[...].T
    for h in range(heads):
        gqg_out[h] = by_head[h : h + 1]
        gkg_out[h] = by_head[heads + h : heads + h + 1]
    for i in range(2):
        fetch[i].wait()
        put[i].start()
    for i, (a, _, _) in enumerate(pieces):
        loads[i].wait()
        wide[a : a + SUB] = low[a : a + SUB].astype(F32)
        stores[i].start()
    for copy in stores + put:
        copy.wait()


def final(y, ig, g, gg, gh, FF, D, HD):
    G = g.shape[0]
    NH = HD // HEAD
    vmem = pl.BlockSpec(memory_space=pltpu.VMEM)
    hbm = pl.BlockSpec(memory_space=pl.ANY)
    shape = jax.ShapeDtypeStruct
    dma = pltpu.SemaphoreType.DMA
    return pl.pallas_call(
        widen,
        out_shape=(
            shape(y.shape, BF), shape(ig.shape, F32), shape((FF, D), F32), shape((D, FF), F32), shape((HD, D), F32),
            shape((3 * HD, D), F32), shape((1, D), F32), shape((1, D), F32), shape((NH, 1, HEAD), F32),
            shape((NH, 1, HEAD), F32),
        ),
        in_specs=[hbm] * 3 + [vmem] * 2,
        out_specs=(hbm,) * 6 + (vmem,) * 4,
        scratch_shapes=[
            pltpu.VMEM((G, D), BF), pltpu.VMEM((G, D), F32), pltpu.VMEM(y.shape, BF),
            pltpu.VMEM(ig.shape, F32), dma((G // SUB,)), dma((G // SUB,)), dma((4,)),
        ],
        name="widen",
        compiler_params=pltpu.CompilerParams(vmem_limit_bytes=60 * 2**20),
    )(y, ig, g, gg, gh)


def shards(
    patches, cotangent, image_lengths, attn_gain, qkv_weight, query_gain, key_gain, out_weight,
    mlp_gain, up_weight, down_weight,
):
    s = lax.axis_index("section")
    own, D = patches.shape[1:]
    HD = out_weight.shape[1]
    NH = HD // HEAD
    wq = qkv_weight[0].reshape(D, 3 * HD).T
    chain = lax.axis_size("batch") == 4
    y, ig, g, gg, gh = fused(
        chain, patches, cotangent, image_lengths, attn_gain, mlp_gain, query_gain, key_gain, wq,
        out_weight[0], up_weight[0], down_weight[0],
    )
    if not chain:
        theirs = lax.ppermute(g[1 - s], "section", [(0, 1), (1, 0)])
        g = lax.psum((g[s].astype(F32) + theirs.astype(F32)).astype(BF), "batch")
        gg = lax.psum(gg, ("section", "batch", "tensor"))[s]
        gh = lax.psum(gh, ("section", "batch"))[s]
    y, ig, gd, gu, go, gq, gattn, gmlp, gqg, gkg = final(y, ig, g, gg, gh, up_weight.shape[2], D, HD)
    return (
        y[None],
        ig[None],
        gattn,
        gq.T.reshape(D, 3, HD)[None],
        gqg.reshape(1, NH, HEAD),
        gkg.reshape(1, NH, HEAD),
        go[None],
        gmlp,
        gu[None],
        gd[None],
    )


def solution(mesh):
    return jax.shard_map(
        shards,
        mesh=mesh,
        in_specs=(
            P(None, ("batch", "tensor"), None),
            P(None, ("batch", "tensor"), None),
            P(None, "batch", None),
            P("section", None),
            P("section", None, None, "tensor"),
            P("section", "tensor", None),
            P("section", "tensor", None),
            P("section", "tensor", None),
            P("section", None),
            P("section", None, "tensor"),
            P("section", "tensor", None),
        ),
        out_specs=(
            P("section", None, ("batch", "tensor"), None),
            P("section", None, ("batch", "tensor"), None),
            P("section", None),
            P("section", None, None, "tensor"),
            P("section", "tensor", None),
            P("section", "tensor", None),
            P("section", "tensor", None),
            P("section", None),
            P("section", None, "tensor"),
            P("section", "tensor", None),
        ),
        check_vma=False,
    )
```

```python
import functools

import jax
import jax.numpy as jnp
from jax import lax
from jax.experimental import pallas as pl
from jax.experimental.pallas import tpu as pltpu
from jax.sharding import PartitionSpec as P

HEAD = 64
EPS = 1e-06
MESH = pl.DeviceIdType.MESH
BF = jnp.bfloat16
F32 = jnp.float32
KEY_BLOCK = 208
COLS = 384
SUB = 192
CHUNKS = 2
TAKEN = (
    (0, 0, 0, 0, 0, 0, 0, 0, 0, 0, 1, 1, 2, 3, 4, 5) + tuple(range(6, 13)),
    (0, 0, 0, 0, 1, 1, 2, 3, 4, 5, 5, 6, 6, 7, 8, 9) + tuple(range(10, 13)),
)
LAGS = (0, 2, 3, 4, 5)
LAYER_POINTS = 8


def ceil_to(n, m):
    return -(-n // m) * m


def chunks_of(rows):
    step = max(32, rows // CHUNKS // 32 * 32)
    starts = [i * step for i in range(CHUNKS) if i * step < rows]
    return [(a, b - a) for a, b in zip(starts, starts[1:] + [rows])]


def mm(a, b):
    return lax.dot_general(a, b, (((1,), (0,)), ((), ())), preferred_element_type=F32)


def mm_nt(a, b):
    return lax.dot_general(a, b, (((1,), (1,)), ((), ())), preferred_element_type=F32)


def mm_tn(a, b):
    return lax.dot_general(a, b, (((0,), (0,)), ((), ())), preferred_element_type=F32)


def normed(v):
    centre = v - jnp.mean(v, axis=-1, keepdims=True)
    r = lax.rsqrt(jnp.mean(centre * centre, axis=-1, keepdims=True) + EPS)
    return centre * r, r


def normed_back(dv, gain, xh, r):
    g = dv * gain
    return r * (g - jnp.mean(g, axis=-1, keepdims=True) - xh * jnp.mean(g * xh, axis=-1, keepdims=True))


def body(
    chain,
    x_ref, ct_ref, len_ref, again_ref, mgain_ref, qgain_ref, kgain_ref, wq_in, wo_in, wu_in, wd_in,
    y_out, ig_out, g_out, gg_out, gh_out,
    wq, wo, wu, wd, sml, qkg, segc_ref, segr_ref, square,
    xres, xh1, r1, xh2, r2,
    a_all, b_all, dm_all, da_all,
    qkh, qkr, qkvb, lse, o_t, g_all, gp_all,
    rows_buf, rows_two, part, sendbuf, ysend, crecv, yrecv,
    e_buf, d_buf, dot_buf, dqkv_t,
    ybuf, dxbuf, ylo, dxlo,
    grads, gains, hgains,
    w_loc, w_send, w_recv, wz_s, wz_r, ag_s, ag_r, rs_s, rs_r, x_s, x_r,
    gx, gz, gpart, gains_x, hgains_x, gains_z, hgains_z, gains_t,
    gx_s, gx_r, gz_s, gz_r, g_loc, sm_s, sm_r,
):
    s, b, t = lax.axis_index("section"), lax.axis_index("batch"), lax.axis_index("tensor")
    y, c = t // 2, lax.rem(t, 2)
    core_id = (s, b, y * 2 + 1 - c)
    y_id = (s, b, (1 - y) * 2 + c)
    x_id = (1 - s, b, t)
    own, D = x_ref.shape[1:]
    R = ceil_to(own, 16)
    N = 4 * R
    FF = wu.shape[2]
    HD = wo.shape[1]
    NH = HD // HEAD
    NB = N // KEY_BLOCK
    pos = c * 2 + y
    ypos = c * 2 + 1 - y
    CH = chunks_of(R)

    def block_rows(k, at):
        off, n = CH[k]
        return pl.ds(pl.multiple_of(4 * off + at * n, 16), n)

    def own_rows(k):
        return pl.ds(CH[k][0], CH[k][1])

    diag_id = (s, b, (1 - y) * 2 + 1 - c)
    z_ids = [(s, lax.rem(b + k, 4), t) for k in (1, 2, 3)] if chain else []
    barrier = pltpu.get_barrier_semaphore()
    for peer in [core_id, y_id, diag_id, x_id] + z_ids:
        pl.semaphore_signal(barrier, inc=1, device_id=peer, device_id_type=MESH)
    pl.semaphore_wait(barrier, 4 + len(z_ids))

    def remote(src, dst, ss, rs, peer):
        return pltpu.make_async_remote_copy(
            src_ref=src, dst_ref=dst, send_sem=ss, recv_sem=rs, device_id=peer, device_id_type=MESH
        )

    def arrived(ref, sem):
        pltpu.make_async_copy(ref, ref, sem).wait()

    sml[s] = jnp.zeros(sml.shape[1:], F32)
    sml[s, 0:1] = again_ref[...].astype(F32)
    sml[s, 1:2] = mgain_ref[...].astype(F32)
    square[...] = jnp.zeros_like(square)
    square[0:NH, 0:HEAD] = qgain_ref[0].astype(F32)
    square[NH : 2 * NH, 0:HEAD] = kgain_ref[0].astype(F32)
    qkg[s] = square[...].T[0:HEAD]
    moves = ((sml.at[s], sml), (qkg.at[s], qkg), (wq_in, wq), (wo_in, wo), (wu_in, wu), (wd_in, wd))
    pair_id = (s, b + 1 - 2 * lax.rem(b, 2), t)
    near = lax.rem(b, 2)
    blocks = []
    for i in range(2, 6):
        rows = moves[i][0].shape[0]
        step = min(rows, 2 * SUB if i > 3 else SUB)
        blocks += [(i, at, step) for at in range(0, rows, step)]

    def half_block(ref, j, h):
        _, at, n = blocks[j]
        return ref.at[pl.ds(pl.multiple_of(at + h * (n // 2), 16), n // 2)]

    def send_block(j):
        src, dst = moves[blocks[j][0]]
        if chain:
            remote(half_block(src, j, near), half_block(dst.at[s], j, near), w_send.at[j], w_recv.at[j], x_id).start()
        else:
            _, at, n = blocks[j]
            remote(src.at[at : at + n], dst.at[s, at : at + n], w_send.at[j], w_recv.at[j], x_id).start()

    def forward_blocks(lo, hi):
        if chain:
            for j in range(lo, hi):
                got = half_block(moves[blocks[j][0]][1].at[1 - s], j, near)
                arrived(got, w_recv.at[j])
                remote(got, got, wz_s.at[j], wz_r.at[j], pair_id).start()

    for i, (src, dst) in enumerate(moves):
        if i < 2:
            remote(src, dst.at[s], w_send.at[len(blocks) + i], w_recv.at[len(blocks) + i], x_id).start()
        else:
            for j in range(len(blocks)):
                if blocks[j][0] == i:
                    send_block(j)
            pltpu.make_async_copy(src, dst.at[s], w_loc.at[i]).start()

    def weights_here(l, i):
        src, dst = moves[i]

        if i > 1:

            @pl.when(l == s)
            def _():
                pltpu.make_async_copy(src, dst.at[s], w_loc.at[i]).wait()

        @pl.when(l != s)
        def _():
            if i < 2:
                arrived(dst.at[1 - s], w_recv.at[len(blocks) + i])
            for j in range(len(blocks)):
                if blocks[j][0] == i:
                    if chain:
                        arrived(half_block(dst.at[1 - s], j, 1 - near), wz_r.at[j])
                    else:
                        _, at, n = blocks[j]
                        arrived(dst.at[1 - s, at : at + n], w_recv.at[j])

    def finish_weights():
        for i in range(2):
            arrived(moves[i][1].at[s], w_send.at[len(blocks) + i])
        for j in range(len(blocks)):
            i, at, n = blocks[j]
            if chain:
                arrived(half_block(moves[i][1].at[s], j, near), w_send.at[j])
                arrived(half_block(moves[i][1].at[1 - s], j, near), wz_s.at[j])
            else:
                arrived(moves[i][1].at[s, at : at + n], w_send.at[j])

    def gather_start(buf, slot, l, op, k):
        mine = buf.at[slot, block_rows(k, pos)]
        remote(mine, mine, ag_s.at[l, op, 0, k], ag_r.at[l, op, 0, k], core_id).start()
        remote(mine, mine, ag_s.at[l, op, 1, k], ag_r.at[l, op, 1, k], y_id).start()

    def gather_pass(buf, slot, l, op, k):
        theirs = buf.at[slot, block_rows(k, ypos)]
        arrived(theirs, ag_r.at[l, op, 1, k])
        remote(theirs, theirs, ag_s.at[l, op, 2, k], ag_r.at[l, op, 2, k], core_id).start()

    def gather_finish(buf, slot, l, op, k):
        mine = buf.at[slot, block_rows(k, pos)]
        arrived(mine, ag_r.at[l, op, 0, k])
        arrived(mine, ag_r.at[l, op, 2, k])
        arrived(mine, ag_s.at[l, op, 0, k])
        arrived(mine, ag_s.at[l, op, 1, k])
        arrived(mine, ag_s.at[l, op, 2, k])

    def pair_rows(k):
        return pl.ds(2 * CH[k][0], 2 * CH[k][1])

    def scatter_start(product, l, op, k):
        slot = op % 2
        off, n = CH[k]

        def send_tile(j, carry):
            cols = pl.ds(pl.multiple_of(j * COLS, COLS), COLS)
            at = pl.ds(pl.multiple_of(4 * off + (1 - c) * 2 * n, 16), 2 * n)
            sendbuf[pair_rows(k), cols] = product(at, cols).astype(BF)
            return carry

        lax.fori_loop(0, D // COLS, send_tile, 0)
        mine = sendbuf.at[pair_rows(k)]
        remote(mine, crecv.at[slot, pair_rows(k)], rs_s.at[l, op, 0, k], rs_r.at[l, op, 0, k], core_id).start()

        def own_tile(j, carry):
            cols = pl.ds(pl.multiple_of(j * COLS, COLS), COLS)
            at = pl.ds(pl.multiple_of(4 * off + c * 2 * n, 16), 2 * n)
            part[pair_rows(k), cols] = product(at, cols)
            return carry

        lax.fori_loop(0, D // COLS, own_tile, 0)
        arrived(mine, rs_r.at[l, op, 0, k])
        other = pl.ds(pl.multiple_of(2 * off + (1 - y) * n, 16), n)
        ysend[own_rows(k)] = (part[other] + crecv[slot, other].astype(F32)).astype(BF)
        remote(
            ysend.at[own_rows(k)], yrecv.at[slot, own_rows(k)], rs_s.at[l, op, 1, k], rs_r.at[l, op, 1, k], y_id
        ).start()

    def scatter_finish(l, op, k):
        slot = op % 2
        off, n = CH[k]
        mine = pl.ds(pl.multiple_of(2 * off + y * n, 16), n)
        arrived(sendbuf.at[pair_rows(k)], rs_s.at[l, op, 0, k])
        arrived(ysend.at[own_rows(k)], rs_s.at[l, op, 1, k])
        arrived(ysend.at[own_rows(k)], rs_r.at[l, op, 1, k])
        return part[mine] + crecv[slot, mine].astype(F32) + yrecv[slot, own_rows(k)].astype(F32)

    FD, UP, OUT = 0, FF, FF + D
    QKV = OUT + HD
    KS = grads.shape[1] // SUB
    HALF = SUB // 2
    middle = (b == 1) | (b == 2)
    end = jnp.logical_not(middle)
    inner_id = (s, jnp.where(b == 0, 1, 2), t)
    outer_id = (s, jnp.where(b == 1, 0, 3), t)
    partner_id = (s, jnp.where(b == 1, 2, 1), t)
    mine_at = jnp.where(b == 1, 0, HALF)
    other_at = HALF - mine_at

    def sub_rows(k):
        return pl.ds(pl.multiple_of(k * SUB, 16), SUB)

    def half_rows(k, at):
        return pl.ds(pl.multiple_of(k * SUB + at, 16), HALF)

    def send_grads(l, lo, hi):
        if not chain:
            return

        @pl.when(l != s)
        def _():
            def one(k, carry):
                rows = sub_rows(k)
                remote(grads.at[l, rows], gx.at[rows], gx_s.at[k], gx_r.at[k], x_id).start()
                return carry

            lax.fori_loop(lo, hi, one, 0)

    def step1(k, carry):
        rows = sub_rows(k)
        arrived(gx.at[rows], gx_r.at[k])
        grads[s, rows] = (grads[s, rows].astype(F32) + gx[rows].astype(F32)).astype(BF)

        @pl.when(end)
        def _():
            remote(grads.at[s, rows], gz.at[rows], gz_s.at[0, k], gz_r.at[0, k], inner_id).start()

        return carry

    def step2(k, carry):
        @pl.when(middle)
        def _():
            rows = sub_rows(k)
            arrived(gz.at[rows], gz_r.at[0, k])
            grads[s, rows] = (grads[s, rows].astype(F32) + gz[rows].astype(F32)).astype(BF)
            other = grads.at[s, half_rows(k, other_at)]
            remote(other, gpart.at[k], gz_s.at[0, k], gz_r.at[1, k], partner_id).start()

        return carry

    def step3(k, carry):
        @pl.when(middle)
        def _():
            rows = half_rows(k, mine_at)
            arrived(gpart.at[k], gz_r.at[1, k])
            grads[s, rows] = (grads[s, rows].astype(F32) + gpart[k].astype(F32)).astype(BF)
            done = grads.at[s, rows]
            remote(done, gz.at[rows], gz_s.at[1, k], gz_r.at[2, k], partner_id).start()
            remote(done, gz.at[rows], gz_s.at[2, k], gz_r.at[0, k], outer_id).start()
            pltpu.make_async_copy(done, g_out.at[rows], g_loc.at[0, k]).start()

        return carry

    def step4(k, carry):
        @pl.when(middle)
        def _():
            rows = half_rows(k, other_at)
            done = gz.at[rows]
            arrived(done, gz_r.at[2, k])
            remote(done, done, gz_s.at[3, k], gz_r.at[1, k], outer_id).start()
            pltpu.make_async_copy(done, g_out.at[rows], g_loc.at[1, k]).start()

        return carry

    def step5(k, carry):
        @pl.when(end)
        def _():
            rows = sub_rows(k)
            arrived(gz.at[half_rows(k, 0)], gz_r.at[0, k])
            arrived(gz.at[half_rows(k, HALF)], gz_r.at[1, k])
            pltpu.make_async_copy(gz.at[rows], g_out.at[rows], g_loc.at[0, k]).start()

        return carry

    steps = (step1, step2, step3, step4, step5)
    last_point = max(len(row) for row in TAKEN) + LAGS[-1]

    def progress(point):
        if not chain:
            return

        def taken(p):
            first, second = ((0 if p < 0 else row[min(p, len(row) - 1)]) for row in TAKEN)
            return first if first == second else jnp.where(s == 0, first, second)

        for step, lag in zip(steps, LAGS):
            lo, hi = taken(point - lag - 1), taken(point - lag)
            if not (isinstance(lo, int) and isinstance(hi, int) and lo == hi):
                lax.fori_loop(lo, hi, step, 0)

    def finish_grads():
        def one(k, carry):
            rows = sub_rows(k)
            half = grads.at[1 - s, half_rows(k, 0)]
            arrived(grads.at[1 - s, rows], gx_s.at[k])

            @pl.when(end)
            def _():
                arrived(grads.at[s, rows], gz_s.at[0, k])
                arrived(g_out.at[rows], g_loc.at[0, k])

            @pl.when(middle)
            def _():
                for j in range(4):
                    arrived(half, gz_s.at[j, k])
                for j in range(2):
                    arrived(g_out.at[half_rows(k, 0)], g_loc.at[j, k])

            return carry

        lax.fori_loop(0, KS, one, 0)

    def q_rows(h):
        return pl.ds(pl.multiple_of(h * HEAD, HEAD), HEAD)

    def segments():
        wide = lax.broadcasted_iota(jnp.int32, (128, 128), 1)
        tall = lax.broadcasted_iota(jnp.int32, (128, 128), 0)
        slots = len_ref.shape[2]
        square[...] = jnp.zeros_like(square)
        square[0:1, 0:slots] = len_ref[s].astype(F32)
        row = jnp.broadcast_to(square[0:1], (128, 128))
        column = row.T
        column_sums = jnp.sum(jnp.where(wide <= tall, row, 0.0), axis=1, keepdims=True)
        row_sums = jnp.sum(jnp.where(tall <= wide, column, 0.0), axis=0, keepdims=True)
        used = (lax.broadcasted_iota(jnp.int32, (128, 1), 0) < slots).astype(F32)
        used_row = (lax.broadcasted_iota(jnp.int32, (1, 128), 1) < slots).astype(F32)
        lane = lax.broadcasted_iota(jnp.int32, (1, N), 1)
        place = lane
        padding = jnp.zeros((1, N), F32)
        for off, n in CH:
            for at in range(4):
                start = 4 * off + at * n
                device = at % 2 * 2 + at // 2
                here = lane >= start
                place = jnp.where(here, lane - start + device * own + off, place)
                padding = jnp.where(here, jnp.where(lane - start + off >= own, 1.0, 0.0), padding)
                r = lax.broadcasted_iota(jnp.int32, (n, 1), 0) + off
                after = jnp.where((r + device * own).astype(F32) >= row_sums, used_row, 0.0)
                seg = jnp.sum(after, axis=1, keepdims=True)
                segc_ref[start : start + n] = jnp.where(r >= own, -1.0, seg)
        seg = jnp.sum(jnp.where(place.astype(F32) >= column_sums, used, 0.0), axis=0, keepdims=True)
        segr_ref[...] = jnp.where(padding > 0, -1.0, seg)

    def padded_rows(ref, k):
        off, n = CH[k]
        v = ref[s, off : min(off + n, own)].astype(F32)
        if off + n > own:
            v = jnp.concatenate([v, jnp.zeros((off + n - own, D), F32)], axis=0)
        return v

    def attention_input(l, k):
        xh, r = normed(xres[own_rows(k)])
        xh1[l, own_rows(k)] = xh
        r1[l, own_rows(k)] = r
        a_all[l, block_rows(k, pos)] = (xh * sml[l, 0:1]).astype(BF)
        gather_start(a_all, l, l, 0, k)

    def project(l, k):
        off, n = CH[k]
        rows, lanes = slice(4 * off, 4 * (off + n)), slice(4 * off, 4 * (off + n))

        def query_key(i, carry):
            at = pl.ds(pl.multiple_of(i * HD, HEAD), HD)
            v = mm_nt(wq[l, at], a_all[l, rows])
            for h in range(NH):
                u = v[h * HEAD : (h + 1) * HEAD]
                u = u - jnp.mean(u, axis=0, keepdims=True)
                rr = lax.rsqrt(jnp.mean(u * u, axis=0, keepdims=True) + EPS)
                u = u * rr
                at = pl.ds(pl.multiple_of(i * HD + h * HEAD, HEAD), HEAD)
                qkh[l, at, lanes] = u
                qkr[l, i, pl.ds(h, 1), lanes] = rr
                scale = jnp.where(i == 0, HEAD**-0.5, 1.0).astype(F32)
                gain = jnp.where(i == 0, qkg[l, :, h : h + 1], qkg[l, :, NH + h : NH + h + 1])
                qkvb[l, at, lanes] = ((u * gain).astype(BF).astype(F32) * scale).astype(BF)
            return carry

        lax.fori_loop(0, 2, query_key, 0)
        qkvb[l, 2 * HD :, lanes] = mm_nt(wq[l, 2 * HD :], a_all[l, rows]).astype(BF)

    def attention(l):
        def head(h, carry):
            q_t = qkvb[l, q_rows(h)]
            v_t = qkvb[l, q_rows(2 * NH + h)]
            rows_buf[:, :HEAD] = qkvb[l, q_rows(NH + h)].astype(F32).T.astype(BF)

            def block(i, total):
                at = pl.ds(pl.multiple_of(i * KEY_BLOCK, KEY_BLOCK), KEY_BLOCK)
                sc = mm(rows_buf[at, :HEAD], q_t)
                e = jnp.where(segc_ref[at] == segr_ref[...], jnp.exp(sc), 0.0)
                e_buf[at] = e.astype(BF)
                return total + jnp.sum(e, axis=0, keepdims=True)

            total = lax.fori_loop(0, NB, block, jnp.zeros((1, N), F32), unroll=True)
            lse[l, pl.ds(h, 1)] = jnp.log(total)
            o_t[l, q_rows(h)] = (mm(v_t, e_buf[...]) * (1.0 / total)).astype(BF)
            return carry

        lax.fori_loop(0, NH, head, 0)
        rows_two[:, :HD] = o_t[l].astype(F32).T.astype(BF)

    def hidden(l, k):
        off, n = CH[k]

        def tile(i, carry):
            rows = pl.ds(pl.multiple_of(4 * off + lax.rem(i, 2) * 2 * n, 16), 2 * n)
            cols = pl.ds(pl.multiple_of((i // 2) * COLS, COLS), COLS)
            u = mm(b_all[l, rows], wu[l, :, cols])
            cdf = 0.5 * (1.0 + lax.erf(u * 0.7071067811865476))
            pdf = jnp.exp(-0.5 * u * u) * 0.3989422804014327
            g_all[l, rows, cols] = (u * cdf).astype(BF)
            gp_all[l, rows, cols] = (cdf + u * pdf).astype(BF)
            return carry

        lax.fori_loop(0, 2 * (FF // COLS), tile, 0)

    def hidden_back(l, k):
        off, n = CH[k]

        def tile(i, carry):
            rows = pl.ds(pl.multiple_of(4 * off + lax.rem(i, 2) * 2 * n, 16), 2 * n)
            cols = pl.ds(pl.multiple_of((i // 2) * COLS, COLS), COLS)
            dg = mm_nt(dm_all[0, rows], wd[l, cols])
            gp_all[l, rows, cols] = (dg * gp_all[l, rows, cols].astype(F32)).astype(BF)
            return carry

        lax.fori_loop(0, 2 * (FF // COLS), tile, 0)

    def down_grad(l):
        def tile(i, carry):
            cols = pl.ds(pl.multiple_of(i * COLS, COLS), COLS)
            at = pl.ds(pl.multiple_of(FD + i * COLS, COLS), COLS)
            grads[l, at] = mm_tn(g_all[l, :, cols], dm_all[0]).astype(BF)
            return carry

        lax.fori_loop(0, FF // COLS, tile, 0)
        send_grads(l, 0, UP // SUB)

    def up_grad(l):
        def tile(i, carry):
            cols = pl.ds(pl.multiple_of(i * COLS, COLS), COLS)
            at = pl.ds(pl.multiple_of(UP + i * COLS, COLS), COLS)
            grads[l, at] = mm_tn(b_all[l, :, cols], gp_all[l]).astype(BF)
            return carry

        lax.fori_loop(0, D // COLS, tile, 0)
        send_grads(l, UP // SUB, OUT // SUB)

    def gains_of(l, i, h):
        out = qkg[l, :, i * NH : i * NH + 1]
        for k in range(1, NH):
            out = jnp.where(h == k, qkg[l, :, i * NH + k : i * NH + k + 1], out)
        return out

    def attention_back(l):
        def head(h, carry):
            q_t = qkvb[l, q_rows(h)]
            k_t = qkvb[l, q_rows(NH + h)]
            v_t = qkvb[l, q_rows(2 * NH + h)]
            rows_buf[:, :HEAD] = k_t.astype(F32).T.astype(BF)
            rows_two[:, :HEAD] = v_t.astype(F32).T.astype(BF)
            do_t = dot_buf[q_rows(h)]
            delta = jnp.sum(do_t.astype(F32) * o_t[l, q_rows(h)].astype(F32), axis=0, keepdims=True)
            log_total = lse[l, pl.ds(h, 1)]

            def block(i, carry):
                at = pl.ds(pl.multiple_of(i * KEY_BLOCK, KEY_BLOCK), KEY_BLOCK)
                sc = mm(rows_buf[at, :HEAD], q_t)
                p = jnp.where(segc_ref[at] == segr_ref[...], jnp.exp(sc - log_total), 0.0)
                dp = mm(rows_two[at, :HEAD], do_t)
                e_buf[at] = p.astype(BF)
                d_buf[at] = (p * (dp - delta)).astype(BF)
                return carry

            lax.fori_loop(0, NB, block, 0, unroll=True)
            dqkv_t[q_rows(2 * NH + h)] = mm_nt(do_t, e_buf[...]).astype(BF)
            dk = mm_nt(q_t, d_buf[...])
            dq = mm(k_t, d_buf[...]) * (HEAD**-0.5)
            for i, dv in ((0, dq), (1, dk)):
                at = q_rows(i * NH + h)
                dv = dv.astype(BF).astype(F32)
                uh = qkh[l, at]
                lanes = lax.broadcasted_iota(jnp.int32, (HEAD, 128), 1) == i * NH + h
                hgains[l] = jnp.where(lanes, jnp.sum(dv * uh, axis=1, keepdims=True), hgains[l])
                g = dv * gains_of(l, i, h)
                back = g - jnp.mean(g, axis=0, keepdims=True) - uh * jnp.mean(g * uh, axis=0, keepdims=True)
                dqkv_t[at] = (qkr[l, i, pl.ds(h, 1)] * back).astype(BF)
            return carry

        hgains[l] = jnp.zeros((HEAD, 128), F32)
        lax.fori_loop(0, NH, head, 0)
        rows_buf[...] = dqkv_t[...].astype(F32).T.astype(BF)

    each = range(len(CH))
    gains[...] = jnp.zeros_like(gains)

    for l in range(2):
        if l == 0:
            weights_here(l, 0)
            weights_here(l, 1)
            for k in each:
                xres[own_rows(k)] = padded_rows(x_ref, k)
                attention_input(l, k)
                dm_all[0, block_rows(k, pos)] = padded_rows(ct_ref, k).astype(BF)
            segments()
            forward_blocks(0, 3)
        else:
            weights_here(l, 1)
        weights_here(l, 2)
        for k in each:
            gather_pass(a_all, l, l, 0, k)
        for k in each:
            gather_finish(a_all, l, l, 0, k)
            project(l, k)
        if l == 0:
            for k in each:
                gather_start(dm_all, 0, 1, 2, k)
            forward_blocks(3, 4)
        attention(l)
        if l == 0:
            forward_blocks(4, 6)
            for k in each:
                gather_pass(dm_all, 0, 1, 2, k)
        weights_here(l, 3)
        for k in each:
            scatter_start(lambda at, cols: mm(rows_two[at, :HD], wo[l, :, cols]), l, 0, k)
        if l == 0:
            forward_blocks(6, 7)
        for k in each:
            residual = xres[own_rows(k)] + scatter_finish(l, 0, k)
            xres[own_rows(k)] = residual
            xh, r = normed(residual)
            xh2[l, own_rows(k)] = xh
            r2[l, own_rows(k)] = r
            b_all[l, block_rows(k, pos)] = (xh * sml[l, 1:2]).astype(BF)
            gather_start(b_all, l, l, 1, k)
        if l == 0:
            forward_blocks(7, len(blocks))
        weights_here(l, 4)
        gather_pass(b_all, l, l, 1, 0)
        for k in each:
            gather_finish(b_all, l, l, 1, k)
            hidden(l, k)
            if k + 1 < len(CH):
                gather_pass(b_all, l, l, 1, k + 1)
            if k == 0:
                weights_here(l, 5)
            scatter_start(lambda at, cols: mm(g_all[l, at], wd[l, :, cols]), l, 1, k)
        if l == 0:
            for k in each:
                rounded = (xres[own_rows(k)] + scatter_finish(l, 1, k)).astype(BF)
                ybuf[l, own_rows(k)] = rounded
                xres[own_rows(k)] = rounded.astype(F32)
                if k == 0:
                    weights_here(1, 0)
                attention_input(1, k)

    for l in (1, 0):
        base = LAYER_POINTS * (1 - l)
        progress(base)
        if l == 1:
            for k in each:
                gather_finish(dm_all, 0, l, 2, k)
                hidden_back(l, k)
            down_grad(l)
            for k in each:
                ybuf[l, own_rows(k)] = (xres[own_rows(k)] + scatter_finish(l, 1, k)).astype(BF)
                xres[own_rows(k)] = padded_rows(ct_ref, k)
            y_move = remote(ybuf.at[1 - s], ylo, x_s.at[0], x_r.at[0], x_id)
            y_move.start()
            for k in each:
                scatter_start(lambda at, cols: mm_nt(gp_all[l, at], wu[l, cols]), l, 2, k)
        else:
            for k in each:
                gather_pass(dm_all, 0, l, 2, k)
            for k in each:
                gather_finish(dm_all, 0, l, 2, k)
            down_grad(l)
            for k in each:
                hidden_back(l, k)
                scatter_start(lambda at, cols: mm_nt(gp_all[l, at], wu[l, cols]), l, 2, k)
        progress(base + 1)
        up_grad(l)
        progress(base + 2)
        for k in each:
            db = scatter_finish(l, 2, k)
            xh = xh2[l, own_rows(k)]
            gains[l, 1:2] = gains[l, 1:2] + jnp.sum(db * xh, axis=0, keepdims=True)
            dh = xres[own_rows(k)] + normed_back(db, sml[l, 1:2], xh, r2[l, own_rows(k)])
            xres[own_rows(k)] = dh
            da_all[0, block_rows(k, pos)] = dh.astype(BF)
            gather_start(da_all, 0, l, 3, k)
        progress(base + 3)
        for k in each:
            gather_pass(da_all, 0, l, 3, k)
        for k in each:
            gather_finish(da_all, 0, l, 3, k)
        dot_buf[...] = mm_nt(wo[l], da_all[0]).astype(BF)
        progress(base + 4)
        attention_back(l)
        progress(base + 5)
        for k in each:
            scatter_start(lambda at, cols: mm(rows_buf[at], wq[l, :, cols]), l, 3, k)
        grads[l, OUT:QKV] = mm(o_t[l], da_all[0]).astype(BF)
        send_grads(l, OUT // SUB, QKV // SUB)
        grads[l, QKV:] = mm(dqkv_t[...], a_all[l]).astype(BF)
        send_grads(l, QKV // SUB, KS)
        progress(base + 6)
        for k in each:
            da = scatter_finish(l, 3, k)
            xh = xh1[l, own_rows(k)]
            gains[l, 0:1] = gains[l, 0:1] + jnp.sum(da * xh, axis=0, keepdims=True)
            dx = xres[own_rows(k)] + normed_back(da, sml[l, 0:1], xh, r1[l, own_rows(k)])
            rounded = dx.astype(BF)
            dxbuf[l, own_rows(k)] = rounded
            if l == 1:
                xres[own_rows(k)] = rounded.astype(F32)
                dm_all[0, block_rows(k, pos)] = rounded
                gather_start(dm_all, 0, 0, 2, k)
            else:
                xres[own_rows(k)] = dx

        progress(base + 7)

        @pl.when(l == s)
        def _():
            ig_out[s] = dxbuf[1, 0:own].astype(F32) if l == 1 else xres[0:own]

        @pl.when(l != s)
        def _():
            if chain:
                remote(gains.at[1 - s], gains_x, sm_s.at[0], sm_r.at[0], x_id).start()
                remote(hgains.at[1 - s], hgains_x, sm_s.at[1], sm_r.at[1], x_id).start()
            remote(dxbuf.at[1 - s], dxlo, x_s.at[1], x_r.at[1], x_id).start()

    taken_all = max(len(row) for row in TAKEN)
    for point in range(2 * LAYER_POINTS, taken_all):
        progress(point)
    if chain:
        arrived(gains_x, sm_r.at[0])
        arrived(hgains_x, sm_r.at[1])
        gains_z[b] = gains[s] + gains_x[...]
        hgains_z[b] = hgains[s] + hgains_x[...]
        for i, peer in enumerate(z_ids):
            remote(gains_z.at[b], gains_z.at[b], sm_s.at[2 + i], sm_r.at[2 + i], peer).start()
            remote(hgains_z.at[b], hgains_z.at[b], sm_s.at[5 + i], sm_r.at[5 + i], peer).start()
        progress(taken_all)
        progress(taken_all + 1)
        for i in range(3):
            arrived(gains_x, sm_r.at[2 + i])
            arrived(hgains_x, sm_r.at[5 + i])
        gh_out[...] = hgains_z[0] + hgains_z[1] + hgains_z[2] + hgains_z[3]
        gains_t[t] = gains_z[0] + gains_z[1] + gains_z[2] + gains_z[3]
        for i, peer in enumerate((core_id, y_id, diag_id)):
            remote(gains_t.at[t], gains_t.at[t], sm_s.at[8 + i], sm_r.at[8 + i], peer).start()
        for point in range(taken_all + 2, last_point):
            progress(point)
        for i in range(3):
            arrived(gains_x, sm_r.at[8 + i])
        gg_out[...] = gains_t[0] + gains_t[1] + gains_t[2] + gains_t[3]
    else:
        g_out[...] = grads[...]
        gg_out[...] = gains[...]
        gh_out[...] = hgains[...]
    y_move.wait()
    y_out[s] = ybuf[s, 0:own]
    y_out[1 - s] = ylo[0:own]
    finish_weights()
    arrived(dxlo, x_s.at[1])
    arrived(dxlo, x_r.at[1])
    ig_out[1 - s] = dxlo[0:own].astype(F32)
    if chain:
        finish_grads()
        for i in range(2, 5):
            arrived(gains_x, sm_s.at[i])
            arrived(hgains_x, sm_s.at[3 + i])
            arrived(gains_x, sm_s.at[6 + i])
        arrived(gains_x, sm_s.at[0])
        arrived(hgains_x, sm_s.at[1])


def fused(chain, x, ct, lengths, again, mgain, qgain, kgain, wq, wo, wu, wd):
    own, D = x.shape[1:]
    R = ceil_to(own, 16)
    N = 4 * R
    QD, HD, FF = wq.shape[0], wo.shape[0], wu.shape[1]
    NH = HD // HEAD
    CH = len(chunks_of(R))
    vmem = pl.BlockSpec(memory_space=pltpu.VMEM)
    hbm = pl.BlockSpec(memory_space=pl.ANY)
    shape = jax.ShapeDtypeStruct
    V = pltpu.VMEM
    dma = pltpu.SemaphoreType.DMA
    G = FF + D + HD + QD
    KS = G // SUB
    ahead = () if chain else (2,)
    extra = [
        V((G, D), BF), V((G, D), BF), V((KS, SUB // 2, D), BF),
        V((8, D), F32), V((HEAD, 128), F32), V((4, 8, D), F32), V((4, HEAD, 128), F32), V((4, 8, D), F32),
        dma((KS,)), dma((KS,)), dma((4, KS)), dma((3, KS)), dma((2, KS)), dma((11,)), dma((11,)),
    ]
    if not chain:
        extra = [V((8, 128), F32)] * 8 + [dma((1,))] * 7
    return pl.pallas_call(
        functools.partial(body, chain),
        out_shape=(
            shape((2, own, D), BF),
            shape((2, own, D), F32),
            shape(ahead + (G, D), BF),
            shape(ahead + (8, D), F32),
            shape(ahead + (HEAD, 128), F32),
        ),
        in_specs=[vmem] * 7 + [hbm] * 4,
        out_specs=(vmem, vmem, hbm if chain else vmem, vmem, vmem),
        scratch_shapes=[
            V((2, QD, D), BF), V((2, HD, D), BF), V((2, D, FF), BF), V((2, FF, D), BF),
            V((2, 8, D), F32), V((2, HEAD, 128), F32), V((N, 1), F32), V((1, N), F32), V((128, 128), F32),
            V((R, D), F32), V((2, R, D), F32), V((2, R, 1), F32), V((2, R, D), F32), V((2, R, 1), F32),
            V((2, N, D), BF), V((2, N, D), BF), V((1, N, D), BF), V((1, N, D), BF),
            V((2, 2 * HD, N), F32), V((2, 2, 8, N), F32), V((2, QD, N), BF), V((2, 8, N), F32),
            V((2, HD, N), BF), V((2, N, FF), BF), V((2, N, FF), BF),
            V((N, QD), BF), V((N, HD), BF), V((2 * R, D), F32), V((2 * R, D), BF), V((R, D), BF),
            V((2, 2 * R, D), BF), V((2, R, D), BF),
            V((N, N), BF), V((N, N), BF), V((HD, N), BF), V((QD, N), BF),
            V((2, R, D), BF), V((2, R, D), BF), V((R, D), BF), V((R, D), BF),
            V((2, G, D), BF), V((2, 8, D), F32), V((2, HEAD, 128), F32),
            dma((6,)), dma((16,)), dma((16,)), dma((16,)), dma((16,)),
            dma((2, 4, 3, CH)), dma((2, 4, 3, CH)), dma((2, 4, 2, CH)), dma((2, 4, 2, CH)), dma((2,)), dma((2,)),
        ] + extra,
        name="layers",
        compiler_params=pltpu.CompilerParams(
            collective_id=0, has_side_effects=True, vmem_limit_bytes=63 * 2**20
        ),
    )(x, ct, lengths, again, mgain, qgain, kgain, wq, wo, wu, wd)


def widen(
    y_in, ig_in, g_in, gg_ref, gh_ref,
    y_out, ig_out, gd_out, gu_out, go_out, gq_out, gattn_out, gmlp_out, gqg_out, gkg_out,
    low, wide, y_buf, ig_buf, in_sem, out_sem, move_sem,
):
    fetch = [
        pltpu.make_async_copy(y_in, y_buf, move_sem.at[0]),
        pltpu.make_async_copy(ig_in, ig_buf, move_sem.at[1]),
    ]
    put = [
        pltpu.make_async_copy(y_buf, y_out, move_sem.at[2]),
        pltpu.make_async_copy(ig_buf, ig_out, move_sem.at[3]),
    ]
    pieces = []
    at = 0
    for out in (gd_out, gu_out, go_out, gq_out):
        for row in range(0, out.shape[0], SUB):
            pieces.append((at, row, out))
            at += SUB
    loads = [pltpu.make_async_copy(g_in.at[a : a + SUB], low.at[a : a + SUB], in_sem.at[i]) for i, (a, _, _) in enumerate(pieces)]
    stores = [
        pltpu.make_async_copy(wide.at[a : a + SUB], out.at[row : row + SUB], out_sem.at[i])
        for i, (a, row, out) in enumerate(pieces)
    ]
    for copy in fetch + loads:
        copy.start()
    gattn_out[...] = gg_ref[0:1]
    gmlp_out[...] = gg_ref[1:2]
    heads = gqg_out.shape[0]
    by_head = gh_ref[...].T
    for h in range(heads):
        gqg_out[h] = by_head[h : h + 1]
        gkg_out[h] = by_head[heads + h : heads + h + 1]
    for i in range(2):
        fetch[i].wait()
        put[i].start()
    for i, (a, _, _) in enumerate(pieces):
        loads[i].wait()
        wide[a : a + SUB] = low[a : a + SUB].astype(F32)
        stores[i].start()
    for copy in stores + put:
        copy.wait()


def final(y, ig, g, gg, gh, FF, D, HD):
    G = g.shape[0]
    NH = HD // HEAD
    vmem = pl.BlockSpec(memory_space=pltpu.VMEM)
    hbm = pl.BlockSpec(memory_space=pl.ANY)
    shape = jax.ShapeDtypeStruct
    dma = pltpu.SemaphoreType.DMA
    return pl.pallas_call(
        widen,
        out_shape=(
            shape(y.shape, BF), shape(ig.shape, F32), shape((FF, D), F32), shape((D, FF), F32), shape((HD, D), F32),
            shape((3 * HD, D), F32), shape((1, D), F32), shape((1, D), F32), shape((NH, 1, HEAD), F32),
            shape((NH, 1, HEAD), F32),
        ),
        in_specs=[hbm] * 3 + [vmem] * 2,
        out_specs=(hbm,) * 6 + (vmem,) * 4,
        scratch_shapes=[
            pltpu.VMEM((G, D), BF), pltpu.VMEM((G, D), F32), pltpu.VMEM(y.shape, BF),
            pltpu.VMEM(ig.shape, F32), dma((G // SUB,)), dma((G // SUB,)), dma((4,)),
        ],
        name="widen",
        compiler_params=pltpu.CompilerParams(vmem_limit_bytes=60 * 2**20),
    )(y, ig, g, gg, gh)


def shards(
    patches, cotangent, image_lengths, attn_gain, qkv_weight, query_gain, key_gain, out_weight,
    mlp_gain, up_weight, down_weight,
):
    s = lax.axis_index("section")
    own, D = patches.shape[1:]
    HD = out_weight.shape[1]
    NH = HD // HEAD
    wq = qkv_weight[0].reshape(D, 3 * HD).T
    chain = lax.axis_size("batch") == 4
    y, ig, g, gg, gh = fused(
        chain, patches, cotangent, image_lengths, attn_gain, mlp_gain, query_gain, key_gain, wq,
        out_weight[0], up_weight[0], down_weight[0],
    )
    if not chain:
        theirs = lax.ppermute(g[1 - s], "section", [(0, 1), (1, 0)])
        g = lax.psum((g[s].astype(F32) + theirs.astype(F32)).astype(BF), "batch")
        gg = lax.psum(gg, ("section", "batch", "tensor"))[s]
        gh = lax.psum(gh, ("section", "batch"))[s]
    y, ig, gd, gu, go, gq, gattn, gmlp, gqg, gkg = final(y, ig, g, gg, gh, up_weight.shape[2], D, HD)
    return (
        y[None],
        ig[None],
        gattn,
        gq.T.reshape(D, 3, HD)[None],
        gqg.reshape(1, NH, HEAD),
        gkg.reshape(1, NH, HEAD),
        go[None],
        gmlp,
        gu[None],
        gd[None],
    )


def solution(mesh):
    return jax.shard_map(
        shards,
        mesh=mesh,
        in_specs=(
            P(None, ("batch", "tensor"), None),
            P(None, ("batch", "tensor"), None),
            P(None, "batch", None),
            P("section", None),
            P("section", None, None, "tensor"),
            P("section", "tensor", None),
            P("section", "tensor", None),
            P("section", "tensor", None),
            P("section", None),
            P("section", None, "tensor"),
            P("section", "tensor", None),
        ),
        out_specs=(
            P("section", None, ("batch", "tensor"), None),
            P("section", None, ("batch", "tensor"), None),
            P("section", None),
            P("section", None, None, "tensor"),
            P("section", "tensor", None),
            P("section", "tensor", None),
            P("section", "tensor", None),
            P("section", None),
            P("section", None, "tensor"),
            P("section", "tensor", None),
        ),
        check_vma=False,
    )
```

```python
import functools

import jax
import jax.numpy as jnp
from jax import lax
from jax.experimental import pallas as pl
from jax.experimental.pallas import tpu as pltpu
from jax.sharding import PartitionSpec as P

HEAD = 64
EPS = 1e-06
MESH = pl.DeviceIdType.MESH
BF = jnp.bfloat16
F32 = jnp.float32
KEY_BLOCK = 208
COLS = 384
SUB = 192
CHUNKS = 2
TAKEN = (
    (0, 0, 0, 0, 0, 0, 0, 0, 0, 1, 1, 2, 3, 4, 5, 6) + tuple(range(7, 13)),
    (0, 0, 0, 0, 1, 1, 2, 3, 4, 5, 5, 6, 6, 7, 8, 9) + tuple(range(10, 13)),
)
LAGS = (0, 2, 3, 4, 5)
LAYER_POINTS = 8


def ceil_to(n, m):
    return -(-n // m) * m


def chunks_of(rows):
    step = max(32, rows // CHUNKS // 32 * 32)
    starts = [i * step for i in range(CHUNKS) if i * step < rows]
    return [(a, b - a) for a, b in zip(starts, starts[1:] + [rows])]


def mm(a, b):
    return lax.dot_general(a, b, (((1,), (0,)), ((), ())), preferred_element_type=F32)


def mm_nt(a, b):
    return lax.dot_general(a, b, (((1,), (1,)), ((), ())), preferred_element_type=F32)


def mm_tn(a, b):
    return lax.dot_general(a, b, (((0,), (0,)), ((), ())), preferred_element_type=F32)


def normed(v):
    centre = v - jnp.mean(v, axis=-1, keepdims=True)
    r = lax.rsqrt(jnp.mean(centre * centre, axis=-1, keepdims=True) + EPS)
    return centre * r, r


def normed_back(dv, gain, xh, r):
    g = dv * gain
    return r * (g - jnp.mean(g, axis=-1, keepdims=True) - xh * jnp.mean(g * xh, axis=-1, keepdims=True))


def body(
    chain,
    x_ref, ct_ref, len_ref, again_ref, mgain_ref, qgain_ref, kgain_ref, wq_in, wo_in, wu_in, wd_in,
    y_out, ig_out, g_out, gg_out, gh_out,
    wq, wo, wu, wd, sml, qkg, segc_ref, segr_ref, square,
    xres, xh1, r1, xh2, r2,
    a_all, b_all, dm_all, da_all,
    qkh, qkr, qkvb, lse, o_t, g_all, gp_all,
    rows_buf, rows_two, part, sendbuf, ysend, crecv, yrecv,
    e_buf, d_buf, dot_buf, dqkv_t,
    ybuf, dxbuf, ylo, dxlo,
    grads, gains, hgains,
    w_loc, w_send, w_recv, wz_s, wz_r, ag_s, ag_r, rs_s, rs_r, x_s, x_r,
    gx, gz, gpart, gains_x, hgains_x, gains_z, hgains_z, gains_t,
    gx_s, gx_r, gz_s, gz_r, g_loc, sm_s, sm_r,
):
    s, b, t = lax.axis_index("section"), lax.axis_index("batch"), lax.axis_index("tensor")
    y, c = t // 2, lax.rem(t, 2)
    core_id = (s, b, y * 2 + 1 - c)
    y_id = (s, b, (1 - y) * 2 + c)
    x_id = (1 - s, b, t)
    own, D = x_ref.shape[1:]
    R = ceil_to(own, 16)
    N = 4 * R
    FF = wu.shape[2]
    HD = wo.shape[1]
    NH = HD // HEAD
    NB = N // KEY_BLOCK
    pos = c * 2 + y
    ypos = c * 2 + 1 - y
    CH = chunks_of(R)

    def block_rows(k, at):
        off, n = CH[k]
        return pl.ds(pl.multiple_of(4 * off + at * n, 16), n)

    def own_rows(k):
        return pl.ds(CH[k][0], CH[k][1])

    diag_id = (s, b, (1 - y) * 2 + 1 - c)
    z_ids = [(s, lax.rem(b + k, 4), t) for k in (1, 2, 3)] if chain else []
    barrier = pltpu.get_barrier_semaphore()
    for peer in [core_id, y_id, diag_id, x_id] + z_ids:
        pl.semaphore_signal(barrier, inc=1, device_id=peer, device_id_type=MESH)
    pl.semaphore_wait(barrier, 4 + len(z_ids))

    def remote(src, dst, ss, rs, peer):
        return pltpu.make_async_remote_copy(
            src_ref=src, dst_ref=dst, send_sem=ss, recv_sem=rs, device_id=peer, device_id_type=MESH
        )

    def arrived(ref, sem):
        pltpu.make_async_copy(ref, ref, sem).wait()

    sml[s] = jnp.zeros(sml.shape[1:], F32)
    sml[s, 0:1] = again_ref[...].astype(F32)
    sml[s, 1:2] = mgain_ref[...].astype(F32)
    square[...] = jnp.zeros_like(square)
    square[0:NH, 0:HEAD] = qgain_ref[0].astype(F32)
    square[NH : 2 * NH, 0:HEAD] = kgain_ref[0].astype(F32)
    qkg[s] = square[...].T[0:HEAD]
    moves = ((sml.at[s], sml), (qkg.at[s], qkg), (wq_in, wq), (wo_in, wo), (wu_in, wu), (wd_in, wd))
    pair_id = (s, b + 1 - 2 * lax.rem(b, 2), t)
    near = lax.rem(b, 2)
    blocks = []
    for i in range(2, 6):
        rows = moves[i][0].shape[0]
        step = min(rows, 2 * SUB if i > 3 else SUB)
        blocks += [(i, at, step) for at in range(0, rows, step)]

    def half_block(ref, j, h):
        _, at, n = blocks[j]
        return ref.at[pl.ds(pl.multiple_of(at + h * (n // 2), 16), n // 2)]

    def send_block(j):
        src, dst = moves[blocks[j][0]]
        if chain:
            remote(half_block(src, j, near), half_block(dst.at[s], j, near), w_send.at[j], w_recv.at[j], x_id).start()
        else:
            _, at, n = blocks[j]
            remote(src.at[at : at + n], dst.at[s, at : at + n], w_send.at[j], w_recv.at[j], x_id).start()

    def forward_blocks(lo, hi):
        if chain:
            for j in range(lo, hi):
                got = half_block(moves[blocks[j][0]][1].at[1 - s], j, near)
                arrived(got, w_recv.at[j])
                remote(got, got, wz_s.at[j], wz_r.at[j], pair_id).start()

    for i, (src, dst) in enumerate(moves):
        if i < 2:
            remote(src, dst.at[s], w_send.at[len(blocks) + i], w_recv.at[len(blocks) + i], x_id).start()
        else:
            for j in range(len(blocks)):
                if blocks[j][0] == i:
                    send_block(j)
            pltpu.make_async_copy(src, dst.at[s], w_loc.at[i]).start()

    def weights_here(l, i):
        src, dst = moves[i]

        if i > 1:

            @pl.when(l == s)
            def _():
                pltpu.make_async_copy(src, dst.at[s], w_loc.at[i]).wait()

        @pl.when(l != s)
        def _():
            if i < 2:
                arrived(dst.at[1 - s], w_recv.at[len(blocks) + i])
            for j in range(len(blocks)):
                if blocks[j][0] == i:
                    if chain:
                        arrived(half_block(dst.at[1 - s], j, 1 - near), wz_r.at[j])
                    else:
                        _, at, n = blocks[j]
                        arrived(dst.at[1 - s, at : at + n], w_recv.at[j])

    def finish_weights():
        for i in range(2):
            arrived(moves[i][1].at[s], w_send.at[len(blocks) + i])
        for j in range(len(blocks)):
            i, at, n = blocks[j]
            if chain:
                arrived(half_block(moves[i][1].at[s], j, near), w_send.at[j])
                arrived(half_block(moves[i][1].at[1 - s], j, near), wz_s.at[j])
            else:
                arrived(moves[i][1].at[s, at : at + n], w_send.at[j])

    def gather_start(buf, slot, l, op, k):
        mine = buf.at[slot, block_rows(k, pos)]
        remote(mine, mine, ag_s.at[l, op, 0, k], ag_r.at[l, op, 0, k], core_id).start()
        remote(mine, mine, ag_s.at[l, op, 1, k], ag_r.at[l, op, 1, k], y_id).start()

    def gather_pass(buf, slot, l, op, k):
        theirs = buf.at[slot, block_rows(k, ypos)]
        arrived(theirs, ag_r.at[l, op, 1, k])
        remote(theirs, theirs, ag_s.at[l, op, 2, k], ag_r.at[l, op, 2, k], core_id).start()

    def gather_finish(buf, slot, l, op, k):
        mine = buf.at[slot, block_rows(k, pos)]
        arrived(mine, ag_r.at[l, op, 0, k])
        arrived(mine, ag_r.at[l, op, 2, k])
        arrived(mine, ag_s.at[l, op, 0, k])
        arrived(mine, ag_s.at[l, op, 1, k])
        arrived(mine, ag_s.at[l, op, 2, k])

    def pair_rows(k):
        return pl.ds(2 * CH[k][0], 2 * CH[k][1])

    def scatter_start(product, l, op, k):
        slot = op % 2
        off, n = CH[k]

        def send_tile(j, carry):
            cols = pl.ds(pl.multiple_of(j * COLS, COLS), COLS)
            at = pl.ds(pl.multiple_of(4 * off + (1 - c) * 2 * n, 16), 2 * n)
            sendbuf[pair_rows(k), cols] = product(at, cols).astype(BF)
            return carry

        lax.fori_loop(0, D // COLS, send_tile, 0)
        mine = sendbuf.at[pair_rows(k)]
        remote(mine, crecv.at[slot, pair_rows(k)], rs_s.at[l, op, 0, k], rs_r.at[l, op, 0, k], core_id).start()

        def own_tile(j, carry):
            cols = pl.ds(pl.multiple_of(j * COLS, COLS), COLS)
            at = pl.ds(pl.multiple_of(4 * off + c * 2 * n, 16), 2 * n)
            part[pair_rows(k), cols] = product(at, cols)
            return carry

        lax.fori_loop(0, D // COLS, own_tile, 0)
        arrived(mine, rs_r.at[l, op, 0, k])
        other = pl.ds(pl.multiple_of(2 * off + (1 - y) * n, 16), n)
        ysend[own_rows(k)] = (part[other] + crecv[slot, other].astype(F32)).astype(BF)
        remote(
            ysend.at[own_rows(k)], yrecv.at[slot, own_rows(k)], rs_s.at[l, op, 1, k], rs_r.at[l, op, 1, k], y_id
        ).start()

    def scatter_finish(l, op, k):
        slot = op % 2
        off, n = CH[k]
        mine = pl.ds(pl.multiple_of(2 * off + y * n, 16), n)
        arrived(sendbuf.at[pair_rows(k)], rs_s.at[l, op, 0, k])
        arrived(ysend.at[own_rows(k)], rs_s.at[l, op, 1, k])
        arrived(ysend.at[own_rows(k)], rs_r.at[l, op, 1, k])
        return part[mine] + crecv[slot, mine].astype(F32) + yrecv[slot, own_rows(k)].astype(F32)

    FD, UP, OUT = 0, FF, FF + D
    QKV = OUT + HD
    KS = grads.shape[1] // SUB
    HALF = SUB // 2
    middle = (b == 1) | (b == 2)
    end = jnp.logical_not(middle)
    inner_id = (s, jnp.where(b == 0, 1, 2), t)
    outer_id = (s, jnp.where(b == 1, 0, 3), t)
    partner_id = (s, jnp.where(b == 1, 2, 1), t)
    mine_at = jnp.where(b == 1, 0, HALF)
    other_at = HALF - mine_at

    def sub_rows(k):
        return pl.ds(pl.multiple_of(k * SUB, 16), SUB)

    def half_rows(k, at):
        return pl.ds(pl.multiple_of(k * SUB + at, 16), HALF)

    def send_grads(l, lo, hi):
        if not chain:
            return

        @pl.when(l != s)
        def _():
            def one(k, carry):
                rows = sub_rows(k)
                remote(grads.at[l, rows], gx.at[rows], gx_s.at[k], gx_r.at[k], x_id).start()
                return carry

            lax.fori_loop(lo, hi, one, 0)

    def step1(k, carry):
        rows = sub_rows(k)
        arrived(gx.at[rows], gx_r.at[k])
        grads[s, rows] = (grads[s, rows].astype(F32) + gx[rows].astype(F32)).astype(BF)

        @pl.when(end)
        def _():
            remote(grads.at[s, rows], gz.at[rows], gz_s.at[0, k], gz_r.at[0, k], inner_id).start()

        return carry

    def step2(k, carry):
        @pl.when(middle)
        def _():
            rows = sub_rows(k)
            arrived(gz.at[rows], gz_r.at[0, k])
            grads[s, rows] = (grads[s, rows].astype(F32) + gz[rows].astype(F32)).astype(BF)
            other = grads.at[s, half_rows(k, other_at)]
            remote(other, gpart.at[k], gz_s.at[0, k], gz_r.at[1, k], partner_id).start()

        return carry

    def step3(k, carry):
        @pl.when(middle)
        def _():
            rows = half_rows(k, mine_at)
            arrived(gpart.at[k], gz_r.at[1, k])
            grads[s, rows] = (grads[s, rows].astype(F32) + gpart[k].astype(F32)).astype(BF)
            done = grads.at[s, rows]
            remote(done, gz.at[rows], gz_s.at[1, k], gz_r.at[2, k], partner_id).start()
            remote(done, gz.at[rows], gz_s.at[2, k], gz_r.at[0, k], outer_id).start()
            pltpu.make_async_copy(done, g_out.at[rows], g_loc.at[0, k]).start()

        return carry

    def step4(k, carry):
        @pl.when(middle)
        def _():
            rows = half_rows(k, other_at)
            done = gz.at[rows]
            arrived(done, gz_r.at[2, k])
            remote(done, done, gz_s.at[3, k], gz_r.at[1, k], outer_id).start()
            pltpu.make_async_copy(done, g_out.at[rows], g_loc.at[1, k]).start()

        return carry

    def step5(k, carry):
        @pl.when(end)
        def _():
            rows = sub_rows(k)
            arrived(gz.at[half_rows(k, 0)], gz_r.at[0, k])
            arrived(gz.at[half_rows(k, HALF)], gz_r.at[1, k])
            pltpu.make_async_copy(gz.at[rows], g_out.at[rows], g_loc.at[0, k]).start()

        return carry

    steps = (step1, step2, step3, step4, step5)
    last_point = max(len(row) for row in TAKEN) + LAGS[-1]

    def progress(point):
        if not chain:
            return

        def taken(p):
            first, second = ((0 if p < 0 else row[min(p, len(row) - 1)]) for row in TAKEN)
            return first if first == second else jnp.where(s == 0, first, second)

        for step, lag in zip(steps, LAGS):
            lo, hi = taken(point - lag - 1), taken(point - lag)
            if not (isinstance(lo, int) and isinstance(hi, int) and lo == hi):
                lax.fori_loop(lo, hi, step, 0)

    def finish_grads():
        def one(k, carry):
            rows = sub_rows(k)
            half = grads.at[1 - s, half_rows(k, 0)]
            arrived(grads.at[1 - s, rows], gx_s.at[k])

            @pl.when(end)
            def _():
                arrived(grads.at[s, rows], gz_s.at[0, k])
                arrived(g_out.at[rows], g_loc.at[0, k])

            @pl.when(middle)
            def _():
                for j in range(4):
                    arrived(half, gz_s.at[j, k])
                for j in range(2):
                    arrived(g_out.at[half_rows(k, 0)], g_loc.at[j, k])

            return carry

        lax.fori_loop(0, KS, one, 0)

    def q_rows(h):
        return pl.ds(pl.multiple_of(h * HEAD, HEAD), HEAD)

    def segments():
        wide = lax.broadcasted_iota(jnp.int32, (128, 128), 1)
        tall = lax.broadcasted_iota(jnp.int32, (128, 128), 0)
        slots = len_ref.shape[2]
        square[...] = jnp.zeros_like(square)
        square[0:1, 0:slots] = len_ref[s].astype(F32)
        row = jnp.broadcast_to(square[0:1], (128, 128))
        column = row.T
        column_sums = jnp.sum(jnp.where(wide <= tall, row, 0.0), axis=1, keepdims=True)
        row_sums = jnp.sum(jnp.where(tall <= wide, column, 0.0), axis=0, keepdims=True)
        used = (lax.broadcasted_iota(jnp.int32, (128, 1), 0) < slots).astype(F32)
        used_row = (lax.broadcasted_iota(jnp.int32, (1, 128), 1) < slots).astype(F32)
        lane = lax.broadcasted_iota(jnp.int32, (1, N), 1)
        place = lane
        padding = jnp.zeros((1, N), F32)
        for off, n in CH:
            for at in range(4):
                start = 4 * off + at * n
                device = at % 2 * 2 + at // 2
                here = lane >= start
                place = jnp.where(here, lane - start + device * own + off, place)
                padding = jnp.where(here, jnp.where(lane - start + off >= own, 1.0, 0.0), padding)
                r = lax.broadcasted_iota(jnp.int32, (n, 1), 0) + off
                after = jnp.where((r + device * own).astype(F32) >= row_sums, used_row, 0.0)
                seg = jnp.sum(after, axis=1, keepdims=True)
                segc_ref[start : start + n] = jnp.where(r >= own, -1.0, seg)
        seg = jnp.sum(jnp.where(place.astype(F32) >= column_sums, used, 0.0), axis=0, keepdims=True)
        segr_ref[...] = jnp.where(padding > 0, -1.0, seg)

    def padded_rows(ref, k):
        off, n = CH[k]
        v = ref[s, off : min(off + n, own)].astype(F32)
        if off + n > own:
            v = jnp.concatenate([v, jnp.zeros((off + n - own, D), F32)], axis=0)
        return v

    def attention_input(l, k):
        xh, r = normed(xres[own_rows(k)])
        xh1[l, own_rows(k)] = xh
        r1[l, own_rows(k)] = r
        a_all[l, block_rows(k, pos)] = (xh * sml[l, 0:1]).astype(BF)
        gather_start(a_all, l, l, 0, k)

    def project(l, k):
        off, n = CH[k]
        rows, lanes = slice(4 * off, 4 * (off + n)), slice(4 * off, 4 * (off + n))

        def query_key(i, carry):
            at = pl.ds(pl.multiple_of(i * HD, HEAD), HD)
            v = mm_nt(wq[l, at], a_all[l, rows])
            for h in range(NH):
                u = v[h * HEAD : (h + 1) * HEAD]
                u = u - jnp.mean(u, axis=0, keepdims=True)
                rr = lax.rsqrt(jnp.mean(u * u, axis=0, keepdims=True) + EPS)
                u = u * rr
                at = pl.ds(pl.multiple_of(i * HD + h * HEAD, HEAD), HEAD)
                qkh[l, at, lanes] = u
                qkr[l, i, pl.ds(h, 1), lanes] = rr
                scale = jnp.where(i == 0, HEAD**-0.5, 1.0).astype(F32)
                gain = jnp.where(i == 0, qkg[l, :, h : h + 1], qkg[l, :, NH + h : NH + h + 1])
                qkvb[l, at, lanes] = ((u * gain).astype(BF).astype(F32) * scale).astype(BF)
            return carry

        lax.fori_loop(0, 2, query_key, 0)
        qkvb[l, 2 * HD :, lanes] = mm_nt(wq[l, 2 * HD :], a_all[l, rows]).astype(BF)

    def attention(l):
        def head(h, carry):
            q_t = qkvb[l, q_rows(h)]
            v_t = qkvb[l, q_rows(2 * NH + h)]
            rows_buf[:, :HEAD] = qkvb[l, q_rows(NH + h)].astype(F32).T.astype(BF)

            def block(i, total):
                at = pl.ds(pl.multiple_of(i * KEY_BLOCK, KEY_BLOCK), KEY_BLOCK)
                sc = mm(rows_buf[at, :HEAD], q_t)
                e = jnp.where(segc_ref[at] == segr_ref[...], jnp.exp(sc), 0.0)
                e_buf[at] = e.astype(BF)
                return total + jnp.sum(e, axis=0, keepdims=True)

            total = lax.fori_loop(0, NB, block, jnp.zeros((1, N), F32), unroll=True)
            lse[l, pl.ds(h, 1)] = jnp.log(total)
            o_t[l, q_rows(h)] = (mm(v_t, e_buf[...]) * (1.0 / total)).astype(BF)
            return carry

        lax.fori_loop(0, NH, head, 0)
        rows_two[:, :HD] = o_t[l].astype(F32).T.astype(BF)

    def hidden(l, k):
        off, n = CH[k]

        def tile(i, carry):
            rows = pl.ds(pl.multiple_of(4 * off + lax.rem(i, 2) * 2 * n, 16), 2 * n)
            cols = pl.ds(pl.multiple_of((i // 2) * COLS, COLS), COLS)
            u = mm(b_all[l, rows], wu[l, :, cols])
            cdf = 0.5 * (1.0 + lax.erf(u * 0.7071067811865476))
            pdf = jnp.exp(-0.5 * u * u) * 0.3989422804014327
            g_all[l, rows, cols] = (u * cdf).astype(BF)
            gp_all[l, rows, cols] = (cdf + u * pdf).astype(BF)
            return carry

        lax.fori_loop(0, 2 * (FF // COLS), tile, 0)

    def hidden_back(l, k):
        off, n = CH[k]

        def tile(i, carry):
            rows = pl.ds(pl.multiple_of(4 * off + lax.rem(i, 2) * 2 * n, 16), 2 * n)
            cols = pl.ds(pl.multiple_of((i // 2) * COLS, COLS), COLS)
            dg = mm_nt(dm_all[0, rows], wd[l, cols])
            gp_all[l, rows, cols] = (dg * gp_all[l, rows, cols].astype(F32)).astype(BF)
            return carry

        lax.fori_loop(0, 2 * (FF // COLS), tile, 0)

    def down_grad(l):
        def tile(i, carry):
            cols = pl.ds(pl.multiple_of(i * COLS, COLS), COLS)
            at = pl.ds(pl.multiple_of(FD + i * COLS, COLS), COLS)
            grads[l, at] = mm_tn(g_all[l, :, cols], dm_all[0]).astype(BF)
            send_grads(l, i * (COLS // SUB), (i + 1) * (COLS // SUB))
            return carry

        lax.fori_loop(0, FF // COLS, tile, 0)

    def up_grad(l):
        def tile(i, carry):
            cols = pl.ds(pl.multiple_of(i * COLS, COLS), COLS)
            at = pl.ds(pl.multiple_of(UP + i * COLS, COLS), COLS)
            grads[l, at] = mm_tn(b_all[l, :, cols], gp_all[l]).astype(BF)
            send_grads(l, UP // SUB + i * (COLS // SUB), UP // SUB + (i + 1) * (COLS // SUB))
            return carry

        lax.fori_loop(0, D // COLS, tile, 0)

    def gains_of(l, i, h):
        out = qkg[l, :, i * NH : i * NH + 1]
        for k in range(1, NH):
            out = jnp.where(h == k, qkg[l, :, i * NH + k : i * NH + k + 1], out)
        return out

    def attention_back(l):
        def head(h, carry):
            q_t = qkvb[l, q_rows(h)]
            k_t = qkvb[l, q_rows(NH + h)]
            v_t = qkvb[l, q_rows(2 * NH + h)]
            rows_buf[:, :HEAD] = k_t.astype(F32).T.astype(BF)
            rows_two[:, :HEAD] = v_t.astype(F32).T.astype(BF)
            do_t = dot_buf[q_rows(h)]
            delta = jnp.sum(do_t.astype(F32) * o_t[l, q_rows(h)].astype(F32), axis=0, keepdims=True)
            log_total = lse[l, pl.ds(h, 1)]

            def block(i, carry):
                at = pl.ds(pl.multiple_of(i * KEY_BLOCK, KEY_BLOCK), KEY_BLOCK)
                sc = mm(rows_buf[at, :HEAD], q_t)
                p = jnp.where(segc_ref[at] == segr_ref[...], jnp.exp(sc - log_total), 0.0)
                dp = mm(rows_two[at, :HEAD], do_t)
                e_buf[at] = p.astype(BF)
                d_buf[at] = (p * (dp - delta)).astype(BF)
                return carry

            lax.fori_loop(0, NB, block, 0, unroll=True)
            dqkv_t[q_rows(2 * NH + h)] = mm_nt(do_t, e_buf[...]).astype(BF)
            dk = mm_nt(q_t, d_buf[...])
            dq = mm(k_t, d_buf[...]) * (HEAD**-0.5)
            for i, dv in ((0, dq), (1, dk)):
                at = q_rows(i * NH + h)
                dv = dv.astype(BF).astype(F32)
                uh = qkh[l, at]
                lanes = lax.broadcasted_iota(jnp.int32, (HEAD, 128), 1) == i * NH + h
                hgains[l] = jnp.where(lanes, jnp.sum(dv * uh, axis=1, keepdims=True), hgains[l])
                g = dv * gains_of(l, i, h)
                back = g - jnp.mean(g, axis=0, keepdims=True) - uh * jnp.mean(g * uh, axis=0, keepdims=True)
                dqkv_t[at] = (qkr[l, i, pl.ds(h, 1)] * back).astype(BF)
            return carry

        hgains[l] = jnp.zeros((HEAD, 128), F32)
        lax.fori_loop(0, NH, head, 0)
        rows_buf[...] = dqkv_t[...].astype(F32).T.astype(BF)

    each = range(len(CH))
    gains[...] = jnp.zeros_like(gains)

    for l in range(2):
        if l == 0:
            weights_here(l, 0)
            weights_here(l, 1)
            for k in each:
                xres[own_rows(k)] = padded_rows(x_ref, k)
                attention_input(l, k)
                dm_all[0, block_rows(k, pos)] = padded_rows(ct_ref, k).astype(BF)
            segments()
            forward_blocks(0, 3)
        else:
            weights_here(l, 1)
        weights_here(l, 2)
        for k in each:
            gather_pass(a_all, l, l, 0, k)
        for k in each:
            gather_finish(a_all, l, l, 0, k)
            project(l, k)
        if l == 0:
            for k in each:
                gather_start(dm_all, 0, 1, 2, k)
            forward_blocks(3, 4)
        attention(l)
        if l == 0:
            forward_blocks(4, 6)
            for k in each:
                gather_pass(dm_all, 0, 1, 2, k)
        weights_here(l, 3)
        for k in each:
            scatter_start(lambda at, cols: mm(rows_two[at, :HD], wo[l, :, cols]), l, 0, k)
        if l == 0:
            forward_blocks(6, 7)
        for k in each:
            residual = xres[own_rows(k)] + scatter_finish(l, 0, k)
            xres[own_rows(k)] = residual
            xh, r = normed(residual)
            xh2[l, own_rows(k)] = xh
            r2[l, own_rows(k)] = r
            b_all[l, block_rows(k, pos)] = (xh * sml[l, 1:2]).astype(BF)
            gather_start(b_all, l, l, 1, k)
        if l == 0:
            forward_blocks(7, len(blocks))
        weights_here(l, 4)
        gather_pass(b_all, l, l, 1, 0)
        for k in each:
            gather_finish(b_all, l, l, 1, k)
            hidden(l, k)
            if k + 1 < len(CH):
                gather_pass(b_all, l, l, 1, k + 1)
            if k == 0:
                weights_here(l, 5)
            scatter_start(lambda at, cols: mm(g_all[l, at], wd[l, :, cols]), l, 1, k)
        if l == 0:
            for k in each:
                rounded = (xres[own_rows(k)] + scatter_finish(l, 1, k)).astype(BF)
                ybuf[l, own_rows(k)] = rounded
                xres[own_rows(k)] = rounded.astype(F32)
                if k == 0:
                    weights_here(1, 0)
                attention_input(1, k)

    for l in (1, 0):
        base = LAYER_POINTS * (1 - l)
        progress(base)
        if l == 1:
            for k in each:
                gather_finish(dm_all, 0, l, 2, k)
                hidden_back(l, k)
            down_grad(l)
            for k in each:
                ybuf[l, own_rows(k)] = (xres[own_rows(k)] + scatter_finish(l, 1, k)).astype(BF)
                xres[own_rows(k)] = padded_rows(ct_ref, k)
            y_move = remote(ybuf.at[1 - s], ylo, x_s.at[0], x_r.at[0], x_id)
            y_move.start()
            for k in each:
                scatter_start(lambda at, cols: mm_nt(gp_all[l, at], wu[l, cols]), l, 2, k)
        else:
            for k in each:
                gather_pass(dm_all, 0, l, 2, k)
            for k in each:
                gather_finish(dm_all, 0, l, 2, k)
            down_grad(l)
            for k in each:
                hidden_back(l, k)
                scatter_start(lambda at, cols: mm_nt(gp_all[l, at], wu[l, cols]), l, 2, k)
        progress(base + 1)
        up_grad(l)
        progress(base + 2)
        for k in each:
            db = scatter_finish(l, 2, k)
            xh = xh2[l, own_rows(k)]
            gains[l, 1:2] = gains[l, 1:2] + jnp.sum(db * xh, axis=0, keepdims=True)
            dh = xres[own_rows(k)] + normed_back(db, sml[l, 1:2], xh, r2[l, own_rows(k)])
            xres[own_rows(k)] = dh
            da_all[0, block_rows(k, pos)] = dh.astype(BF)
            gather_start(da_all, 0, l, 3, k)
        progress(base + 3)
        for k in each:
            gather_pass(da_all, 0, l, 3, k)
        for k in each:
            gather_finish(da_all, 0, l, 3, k)
        dot_buf[...] = mm_nt(wo[l], da_all[0]).astype(BF)
        progress(base + 4)
        attention_back(l)
        progress(base + 5)
        for k in each:
            scatter_start(lambda at, cols: mm(rows_buf[at], wq[l, :, cols]), l, 3, k)
        grads[l, OUT:QKV] = mm(o_t[l], da_all[0]).astype(BF)
        send_grads(l, OUT // SUB, QKV // SUB)
        grads[l, QKV:] = mm(dqkv_t[...], a_all[l]).astype(BF)
        send_grads(l, QKV // SUB, KS)
        progress(base + 6)
        for k in each:
            da = scatter_finish(l, 3, k)
            xh = xh1[l, own_rows(k)]
            gains[l, 0:1] = gains[l, 0:1] + jnp.sum(da * xh, axis=0, keepdims=True)
            dx = xres[own_rows(k)] + normed_back(da, sml[l, 0:1], xh, r1[l, own_rows(k)])
            rounded = dx.astype(BF)
            dxbuf[l, own_rows(k)] = rounded
            if l == 1:
                xres[own_rows(k)] = rounded.astype(F32)
                dm_all[0, block_rows(k, pos)] = rounded
                gather_start(dm_all, 0, 0, 2, k)
            else:
                xres[own_rows(k)] = dx

        progress(base + 7)

        @pl.when(l == s)
        def _():
            ig_out[s] = dxbuf[1, 0:own].astype(F32) if l == 1 else xres[0:own]

        @pl.when(l != s)
        def _():
            if chain:
                remote(gains.at[1 - s], gains_x, sm_s.at[0], sm_r.at[0], x_id).start()
                remote(hgains.at[1 - s], hgains_x, sm_s.at[1], sm_r.at[1], x_id).start()
            remote(dxbuf.at[1 - s], dxlo, x_s.at[1], x_r.at[1], x_id).start()

    y_move.wait()
    y_out[s] = ybuf[s, 0:own]
    y_out[1 - s] = ylo[0:own]
    finish_weights()

    def finish_inputs():
        arrived(dxlo, x_s.at[1])
        arrived(dxlo, x_r.at[1])
        ig_out[1 - s] = dxlo[0:own].astype(F32)

    taken_all = max(len(row) for row in TAKEN)
    for point in range(2 * LAYER_POINTS, taken_all):
        progress(point)
    if chain:
        arrived(gains_x, sm_r.at[0])
        arrived(hgains_x, sm_r.at[1])
        gains_z[b] = gains[s] + gains_x[...]
        hgains_z[b] = hgains[s] + hgains_x[...]
        for i, peer in enumerate(z_ids):
            remote(gains_z.at[b], gains_z.at[b], sm_s.at[2 + i], sm_r.at[2 + i], peer).start()
            remote(hgains_z.at[b], hgains_z.at[b], sm_s.at[5 + i], sm_r.at[5 + i], peer).start()
        progress(taken_all)
        progress(taken_all + 1)
        for i in range(3):
            arrived(gains_x, sm_r.at[2 + i])
            arrived(hgains_x, sm_r.at[5 + i])
        gh_out[...] = hgains_z[0] + hgains_z[1] + hgains_z[2] + hgains_z[3]
        gains_t[t] = gains_z[0] + gains_z[1] + gains_z[2] + gains_z[3]
        for i, peer in enumerate((core_id, y_id, diag_id)):
            remote(gains_t.at[t], gains_t.at[t], sm_s.at[8 + i], sm_r.at[8 + i], peer).start()
        for point in range(taken_all + 2, last_point):
            if point == last_point - 2:
                finish_inputs()
            progress(point)
        for i in range(3):
            arrived(gains_x, sm_r.at[8 + i])
        gg_out[...] = gains_t[0] + gains_t[1] + gains_t[2] + gains_t[3]
    else:
        g_out[...] = grads[...]
        gg_out[...] = gains[...]
        gh_out[...] = hgains[...]
    if not chain:
        finish_inputs()
    if chain:
        finish_grads()
        for i in range(2, 5):
            arrived(gains_x, sm_s.at[i])
            arrived(hgains_x, sm_s.at[3 + i])
            arrived(gains_x, sm_s.at[6 + i])
        arrived(gains_x, sm_s.at[0])
        arrived(hgains_x, sm_s.at[1])


def fused(chain, x, ct, lengths, again, mgain, qgain, kgain, wq, wo, wu, wd):
    own, D = x.shape[1:]
    R = ceil_to(own, 16)
    N = 4 * R
    QD, HD, FF = wq.shape[0], wo.shape[0], wu.shape[1]
    NH = HD // HEAD
    CH = len(chunks_of(R))
    vmem = pl.BlockSpec(memory_space=pltpu.VMEM)
    hbm = pl.BlockSpec(memory_space=pl.ANY)
    shape = jax.ShapeDtypeStruct
    V = pltpu.VMEM
    dma = pltpu.SemaphoreType.DMA
    G = FF + D + HD + QD
    KS = G // SUB
    ahead = () if chain else (2,)
    extra = [
        V((G, D), BF), V((G, D), BF), V((KS, SUB // 2, D), BF),
        V((8, D), F32), V((HEAD, 128), F32), V((4, 8, D), F32), V((4, HEAD, 128), F32), V((4, 8, D), F32),
        dma((KS,)), dma((KS,)), dma((4, KS)), dma((3, KS)), dma((2, KS)), dma((11,)), dma((11,)),
    ]
    if not chain:
        extra = [V((8, 128), F32)] * 8 + [dma((1,))] * 7
    return pl.pallas_call(
        functools.partial(body, chain),
        out_shape=(
            shape((2, own, D), BF),
            shape((2, own, D), F32),
            shape(ahead + (G, D), BF),
            shape(ahead + (8, D), F32),
            shape(ahead + (HEAD, 128), F32),
        ),
        in_specs=[vmem] * 7 + [hbm] * 4,
        out_specs=(vmem, vmem, hbm if chain else vmem, vmem, vmem),
        scratch_shapes=[
            V((2, QD, D), BF), V((2, HD, D), BF), V((2, D, FF), BF), V((2, FF, D), BF),
            V((2, 8, D), F32), V((2, HEAD, 128), F32), V((N, 1), F32), V((1, N), F32), V((128, 128), F32),
            V((R, D), F32), V((2, R, D), F32), V((2, R, 1), F32), V((2, R, D), F32), V((2, R, 1), F32),
            V((2, N, D), BF), V((2, N, D), BF), V((1, N, D), BF), V((1, N, D), BF),
            V((2, 2 * HD, N), F32), V((2, 2, 8, N), F32), V((2, QD, N), BF), V((2, 8, N), F32),
            V((2, HD, N), BF), V((2, N, FF), BF), V((2, N, FF), BF),
            V((N, QD), BF), V((N, HD), BF), V((2 * R, D), F32), V((2 * R, D), BF), V((R, D), BF),
            V((2, 2 * R, D), BF), V((2, R, D), BF),
            V((N, N), BF), V((N, N), BF), V((HD, N), BF), V((QD, N), BF),
            V((2, R, D), BF), V((2, R, D), BF), V((R, D), BF), V((R, D), BF),
            V((2, G, D), BF), V((2, 8, D), F32), V((2, HEAD, 128), F32),
            dma((6,)), dma((16,)), dma((16,)), dma((16,)), dma((16,)),
            dma((2, 4, 3, CH)), dma((2, 4, 3, CH)), dma((2, 4, 2, CH)), dma((2, 4, 2, CH)), dma((2,)), dma((2,)),
        ] + extra,
        name="layers",
        compiler_params=pltpu.CompilerParams(
            collective_id=0, has_side_effects=True, vmem_limit_bytes=63 * 2**20
        ),
    )(x, ct, lengths, again, mgain, qgain, kgain, wq, wo, wu, wd)


def widen(
    y_in, ig_in, g_in, gg_ref, gh_ref,
    y_out, ig_out, gd_out, gu_out, go_out, gq_out, gattn_out, gmlp_out, gqg_out, gkg_out,
    low, wide, y_buf, ig_buf, in_sem, out_sem, move_sem,
):
    fetch = [
        pltpu.make_async_copy(y_in, y_buf, move_sem.at[0]),
        pltpu.make_async_copy(ig_in, ig_buf, move_sem.at[1]),
    ]
    put = [
        pltpu.make_async_copy(y_buf, y_out, move_sem.at[2]),
        pltpu.make_async_copy(ig_buf, ig_out, move_sem.at[3]),
    ]
    pieces = []
    at = 0
    for out in (gd_out, gu_out, go_out, gq_out):
        for row in range(0, out.shape[0], SUB):
            pieces.append((at, row, out))
            at += SUB
    loads = [pltpu.make_async_copy(g_in.at[a : a + SUB], low.at[a : a + SUB], in_sem.at[i]) for i, (a, _, _) in enumerate(pieces)]
    stores = [
        pltpu.make_async_copy(wide.at[a : a + SUB], out.at[row : row + SUB], out_sem.at[i])
        for i, (a, row, out) in enumerate(pieces)
    ]
    for copy in fetch + loads:
        copy.start()
    gattn_out[...] = gg_ref[0:1]
    gmlp_out[...] = gg_ref[1:2]
    heads = gqg_out.shape[0]
    by_head = gh_ref[...].T
    for h in range(heads):
        gqg_out[h] = by_head[h : h + 1]
        gkg_out[h] = by_head[heads + h : heads + h + 1]
    for i in range(2):
        fetch[i].wait()
        put[i].start()
    for i, (a, _, _) in enumerate(pieces):
        loads[i].wait()
        wide[a : a + SUB] = low[a : a + SUB].astype(F32)
        stores[i].start()
    for copy in stores + put:
        copy.wait()


def final(y, ig, g, gg, gh, FF, D, HD):
    G = g.shape[0]
    NH = HD // HEAD
    vmem = pl.BlockSpec(memory_space=pltpu.VMEM)
    hbm = pl.BlockSpec(memory_space=pl.ANY)
    shape = jax.ShapeDtypeStruct
    dma = pltpu.SemaphoreType.DMA
    return pl.pallas_call(
        widen,
        out_shape=(
            shape(y.shape, BF), shape(ig.shape, F32), shape((FF, D), F32), shape((D, FF), F32), shape((HD, D), F32),
            shape((3 * HD, D), F32), shape((1, D), F32), shape((1, D), F32), shape((NH, 1, HEAD), F32),
            shape((NH, 1, HEAD), F32),
        ),
        in_specs=[hbm] * 3 + [vmem] * 2,
        out_specs=(hbm,) * 6 + (vmem,) * 4,
        scratch_shapes=[
            pltpu.VMEM((G, D), BF), pltpu.VMEM((G, D), F32), pltpu.VMEM(y.shape, BF),
            pltpu.VMEM(ig.shape, F32), dma((G // SUB,)), dma((G // SUB,)), dma((4,)),
        ],
        name="widen",
        compiler_params=pltpu.CompilerParams(vmem_limit_bytes=60 * 2**20),
    )(y, ig, g, gg, gh)


def shards(
    patches, cotangent, image_lengths, attn_gain, qkv_weight, query_gain, key_gain, out_weight,
    mlp_gain, up_weight, down_weight,
):
    s = lax.axis_index("section")
    own, D = patches.shape[1:]
    HD = out_weight.shape[1]
    NH = HD // HEAD
    wq = qkv_weight[0].reshape(D, 3 * HD).T
    chain = lax.axis_size("batch") == 4
    y, ig, g, gg, gh = fused(
        chain, patches, cotangent, image_lengths, attn_gain, mlp_gain, query_gain, key_gain, wq,
        out_weight[0], up_weight[0], down_weight[0],
    )
    if not chain:
        theirs = lax.ppermute(g[1 - s], "section", [(0, 1), (1, 0)])
        g = lax.psum((g[s].astype(F32) + theirs.astype(F32)).astype(BF), "batch")
        gg = lax.psum(gg, ("section", "batch", "tensor"))[s]
        gh = lax.psum(gh, ("section", "batch"))[s]
    y, ig, gd, gu, go, gq, gattn, gmlp, gqg, gkg = final(y, ig, g, gg, gh, up_weight.shape[2], D, HD)
    return (
        y[None],
        ig[None],
        gattn,
        gq.T.reshape(D, 3, HD)[None],
        gqg.reshape(1, NH, HEAD),
        gkg.reshape(1, NH, HEAD),
        go[None],
        gmlp,
        gu[None],
        gd[None],
    )


def solution(mesh):
    return jax.shard_map(
        shards,
        mesh=mesh,
        in_specs=(
            P(None, ("batch", "tensor"), None),
            P(None, ("batch", "tensor"), None),
            P(None, "batch", None),
            P("section", None),
            P("section", None, None, "tensor"),
            P("section", "tensor", None),
            P("section", "tensor", None),
            P("section", "tensor", None),
            P("section", None),
            P("section", None, "tensor"),
            P("section", "tensor", None),
        ),
        out_specs=(
            P("section", None, ("batch", "tensor"), None),
            P("section", None, ("batch", "tensor"), None),
            P("section", None),
            P("section", None, None, "tensor"),
            P("section", "tensor", None),
            P("section", "tensor", None),
            P("section", "tensor", None),
            P("section", None),
            P("section", None, "tensor"),
            P("section", "tensor", None),
        ),
        check_vma=False,
    )
```

```python
import functools

import jax
import jax.numpy as jnp
from jax import lax
from jax.experimental import pallas as pl
from jax.experimental.pallas import tpu as pltpu
from jax.sharding import PartitionSpec as P

HEAD = 64
EPS = 1e-06
MESH = pl.DeviceIdType.MESH
BF = jnp.bfloat16
F32 = jnp.float32
KEY_BLOCK = 208
COLS = 384
SUB = 192
CHUNKS = 2
TAKEN = (
    (0, 0, 0, 0, 0, 0, 0, 0, 0, 1, 1, 2, 3, 4, 5, 6) + tuple(range(7, 13)),
    (0, 0, 0, 0, 1, 1, 2, 3, 4, 5, 5, 6, 6, 7, 8, 9) + tuple(range(10, 13)),
)
LAGS = (0, 2, 3, 4, 5)
LAYER_POINTS = 8


def ceil_to(n, m):
    return -(-n // m) * m


def chunks_of(rows):
    step = max(32, rows // CHUNKS // 32 * 32)
    starts = [i * step for i in range(CHUNKS) if i * step < rows]
    return [(a, b - a) for a, b in zip(starts, starts[1:] + [rows])]


def mm(a, b):
    return lax.dot_general(a, b, (((1,), (0,)), ((), ())), preferred_element_type=F32)


def mm_nt(a, b):
    return lax.dot_general(a, b, (((1,), (1,)), ((), ())), preferred_element_type=F32)


def mm_tn(a, b):
    return lax.dot_general(a, b, (((0,), (0,)), ((), ())), preferred_element_type=F32)


def normed(v):
    centre = v - jnp.mean(v, axis=-1, keepdims=True)
    r = lax.rsqrt(jnp.mean(centre * centre, axis=-1, keepdims=True) + EPS)
    return centre * r, r


def normed_back(dv, gain, xh, r):
    g = dv * gain
    return r * (g - jnp.mean(g, axis=-1, keepdims=True) - xh * jnp.mean(g * xh, axis=-1, keepdims=True))


def body(
    chain,
    x_ref, ct_ref, len_ref, again_ref, mgain_ref, qgain_ref, kgain_ref, wq_in, wo_in, wu_in, wd_in,
    y_out, ig_out, g_out, gg_out, gh_out,
    wq, wo, wu, wd, sml, qkg, segc_ref, segr_ref, square,
    xres, xh1, r1, xh2, r2,
    a_all, b_all, dm_all, da_all,
    qkh, qkr, qkvb, lse, o_t, g_all, gp_all,
    rows_buf, rows_two, part, sendbuf, ysend, crecv, yrecv,
    e_buf, d_buf, dot_buf, dqkv_t,
    ybuf, dxbuf, ylo, dxlo,
    grads, gains, hgains,
    w_loc, w_send, w_recv, wz_s, wz_r, ag_s, ag_r, rs_s, rs_r, x_s, x_r,
    gx, gz, gpart, gains_x, hgains_x, gains_z, hgains_z, gains_t,
    gx_s, gx_r, gz_s, gz_r, g_loc, sm_s, sm_r,
):
    s, b, t = lax.axis_index("section"), lax.axis_index("batch"), lax.axis_index("tensor")
    y, c = t // 2, lax.rem(t, 2)
    core_id = (s, b, y * 2 + 1 - c)
    y_id = (s, b, (1 - y) * 2 + c)
    x_id = (1 - s, b, t)
    own, D = x_ref.shape[1:]
    R = ceil_to(own, 16)
    N = 4 * R
    FF = wu.shape[2]
    HD = wo.shape[1]
    NH = HD // HEAD
    NB = N // KEY_BLOCK
    pos = c * 2 + y
    ypos = c * 2 + 1 - y
    CH = chunks_of(R)

    def block_rows(k, at):
        off, n = CH[k]
        return pl.ds(pl.multiple_of(4 * off + at * n, 16), n)

    def own_rows(k):
        return pl.ds(CH[k][0], CH[k][1])

    diag_id = (s, b, (1 - y) * 2 + 1 - c)
    z_ids = [(s, lax.rem(b + k, 4), t) for k in (1, 2, 3)] if chain else []
    barrier = pltpu.get_barrier_semaphore()
    for peer in [core_id, y_id, diag_id, x_id] + z_ids:
        pl.semaphore_signal(barrier, inc=1, device_id=peer, device_id_type=MESH)
    pl.semaphore_wait(barrier, 4 + len(z_ids))

    def remote(src, dst, ss, rs, peer):
        return pltpu.make_async_remote_copy(
            src_ref=src, dst_ref=dst, send_sem=ss, recv_sem=rs, device_id=peer, device_id_type=MESH
        )

    def arrived(ref, sem):
        pltpu.make_async_copy(ref, ref, sem).wait()

    sml[s] = jnp.zeros(sml.shape[1:], F32)
    sml[s, 0:1] = again_ref[...].astype(F32)
    sml[s, 1:2] = mgain_ref[...].astype(F32)
    square[...] = jnp.zeros_like(square)
    square[0:NH, 0:HEAD] = qgain_ref[0].astype(F32)
    square[NH : 2 * NH, 0:HEAD] = kgain_ref[0].astype(F32)
    qkg[s] = square[...].T[0:HEAD]
    moves = ((sml.at[s], sml), (qkg.at[s], qkg), (wq_in, wq), (wo_in, wo), (wu_in, wu), (wd_in, wd))
    pair_id = (s, b + 1 - 2 * lax.rem(b, 2), t)
    near = lax.rem(b, 2)
    blocks = []
    for i in range(2, 6):
        rows = moves[i][0].shape[0]
        step = min(rows, 2 * SUB if i > 3 else SUB)
        blocks += [(i, at, step) for at in range(0, rows, step)]

    def half_block(ref, j, h):
        _, at, n = blocks[j]
        return ref.at[pl.ds(pl.multiple_of(at + h * (n // 2), 16), n // 2)]

    def send_block(j):
        src, dst = moves[blocks[j][0]]
        if chain:
            remote(half_block(src, j, near), half_block(dst.at[s], j, near), w_send.at[j], w_recv.at[j], x_id).start()
        else:
            _, at, n = blocks[j]
            remote(src.at[at : at + n], dst.at[s, at : at + n], w_send.at[j], w_recv.at[j], x_id).start()

    def forward_blocks(lo, hi):
        if chain:
            for j in range(lo, hi):
                got = half_block(moves[blocks[j][0]][1].at[1 - s], j, near)
                arrived(got, w_recv.at[j])
                remote(got, got, wz_s.at[j], wz_r.at[j], pair_id).start()

    for i, (src, dst) in enumerate(moves):
        if i < 2:
            remote(src, dst.at[s], w_send.at[len(blocks) + i], w_recv.at[len(blocks) + i], x_id).start()
        else:
            for j in range(len(blocks)):
                if blocks[j][0] == i:
                    send_block(j)
            pltpu.make_async_copy(src, dst.at[s], w_loc.at[i]).start()

    def weights_here(l, i):
        src, dst = moves[i]

        if i > 1:

            @pl.when(l == s)
            def _():
                pltpu.make_async_copy(src, dst.at[s], w_loc.at[i]).wait()

        @pl.when(l != s)
        def _():
            if i < 2:
                arrived(dst.at[1 - s], w_recv.at[len(blocks) + i])
            for j in range(len(blocks)):
                if blocks[j][0] == i:
                    if chain:
                        arrived(half_block(dst.at[1 - s], j, 1 - near), wz_r.at[j])
                    else:
                        _, at, n = blocks[j]
                        arrived(dst.at[1 - s, at : at + n], w_recv.at[j])

    def finish_weights():
        for i in range(2):
            arrived(moves[i][1].at[s], w_send.at[len(blocks) + i])
        for j in range(len(blocks)):
            i, at, n = blocks[j]
            if chain:
                arrived(half_block(moves[i][1].at[s], j, near), w_send.at[j])
                arrived(half_block(moves[i][1].at[1 - s], j, near), wz_s.at[j])
            else:
                arrived(moves[i][1].at[s, at : at + n], w_send.at[j])

    def gather_start(buf, slot, l, op, k):
        mine = buf.at[slot, block_rows(k, pos)]
        remote(mine, mine, ag_s.at[l, op, 0, k], ag_r.at[l, op, 0, k], core_id).start()
        remote(mine, mine, ag_s.at[l, op, 1, k], ag_r.at[l, op, 1, k], y_id).start()

    def gather_pass(buf, slot, l, op, k):
        theirs = buf.at[slot, block_rows(k, ypos)]
        arrived(theirs, ag_r.at[l, op, 1, k])
        remote(theirs, theirs, ag_s.at[l, op, 2, k], ag_r.at[l, op, 2, k], core_id).start()

    def gather_finish(buf, slot, l, op, k):
        mine = buf.at[slot, block_rows(k, pos)]
        arrived(mine, ag_r.at[l, op, 0, k])
        arrived(mine, ag_r.at[l, op, 2, k])
        arrived(mine, ag_s.at[l, op, 0, k])
        arrived(mine, ag_s.at[l, op, 1, k])
        arrived(mine, ag_s.at[l, op, 2, k])

    def pair_rows(k):
        return pl.ds(2 * CH[k][0], 2 * CH[k][1])

    def scatter_start(product, l, op, k):
        slot = op % 2
        off, n = CH[k]

        def send_tile(j, carry):
            cols = pl.ds(pl.multiple_of(j * COLS, COLS), COLS)
            at = pl.ds(pl.multiple_of(4 * off + (1 - c) * 2 * n, 16), 2 * n)
            sendbuf[pair_rows(k), cols] = product(at, cols).astype(BF)
            return carry

        lax.fori_loop(0, D // COLS, send_tile, 0)
        mine = sendbuf.at[pair_rows(k)]
        remote(mine, crecv.at[slot, pair_rows(k)], rs_s.at[l, op, 0, k], rs_r.at[l, op, 0, k], core_id).start()

        def own_tile(j, carry):
            cols = pl.ds(pl.multiple_of(j * COLS, COLS), COLS)
            at = pl.ds(pl.multiple_of(4 * off + c * 2 * n, 16), 2 * n)
            part[pair_rows(k), cols] = product(at, cols)
            return carry

        lax.fori_loop(0, D // COLS, own_tile, 0)
        arrived(mine, rs_r.at[l, op, 0, k])
        other = pl.ds(pl.multiple_of(2 * off + (1 - y) * n, 16), n)
        ysend[own_rows(k)] = (part[other] + crecv[slot, other].astype(F32)).astype(BF)
        remote(
            ysend.at[own_rows(k)], yrecv.at[slot, own_rows(k)], rs_s.at[l, op, 1, k], rs_r.at[l, op, 1, k], y_id
        ).start()

    def scatter_finish(l, op, k):
        slot = op % 2
        off, n = CH[k]
        mine = pl.ds(pl.multiple_of(2 * off + y * n, 16), n)
        arrived(sendbuf.at[pair_rows(k)], rs_s.at[l, op, 0, k])
        arrived(ysend.at[own_rows(k)], rs_s.at[l, op, 1, k])
        arrived(ysend.at[own_rows(k)], rs_r.at[l, op, 1, k])
        return part[mine] + crecv[slot, mine].astype(F32) + yrecv[slot, own_rows(k)].astype(F32)

    FD, UP, OUT = 0, FF, FF + D
    QKV = OUT + HD
    KS = grads.shape[1] // SUB
    HALF = SUB // 2
    middle = (b == 1) | (b == 2)
    end = jnp.logical_not(middle)
    inner_id = (s, jnp.where(b == 0, 1, 2), t)
    outer_id = (s, jnp.where(b == 1, 0, 3), t)
    partner_id = (s, jnp.where(b == 1, 2, 1), t)
    mine_at = jnp.where(b == 1, 0, HALF)
    other_at = HALF - mine_at

    def sub_rows(k):
        return pl.ds(pl.multiple_of(k * SUB, 16), SUB)

    def half_rows(k, at):
        return pl.ds(pl.multiple_of(k * SUB + at, 16), HALF)

    def send_grads(l, lo, hi):
        if not chain:
            return

        @pl.when(l != s)
        def _():
            def one(k, carry):
                rows = sub_rows(k)
                remote(grads.at[l, rows], gx.at[rows], gx_s.at[k], gx_r.at[k], x_id).start()
                return carry

            lax.fori_loop(lo, hi, one, 0)

    def step1(k, carry):
        rows = sub_rows(k)
        arrived(gx.at[rows], gx_r.at[k])
        grads[s, rows] = (grads[s, rows].astype(F32) + gx[rows].astype(F32)).astype(BF)

        @pl.when(end)
        def _():
            remote(grads.at[s, rows], gz.at[rows], gz_s.at[0, k], gz_r.at[0, k], inner_id).start()

        return carry

    def step2(k, carry):
        @pl.when(middle)
        def _():
            rows = sub_rows(k)
            arrived(gz.at[rows], gz_r.at[0, k])
            grads[s, rows] = (grads[s, rows].astype(F32) + gz[rows].astype(F32)).astype(BF)
            other = grads.at[s, half_rows(k, other_at)]
            remote(other, gpart.at[k], gz_s.at[0, k], gz_r.at[1, k], partner_id).start()

        return carry

    def step3(k, carry):
        @pl.when(middle)
        def _():
            rows = half_rows(k, mine_at)
            arrived(gpart.at[k], gz_r.at[1, k])
            grads[s, rows] = (grads[s, rows].astype(F32) + gpart[k].astype(F32)).astype(BF)
            done = grads.at[s, rows]
            remote(done, gz.at[rows], gz_s.at[1, k], gz_r.at[2, k], partner_id).start()
            remote(done, gz.at[rows], gz_s.at[2, k], gz_r.at[0, k], outer_id).start()
            pltpu.make_async_copy(done, g_out.at[rows], g_loc.at[0, k]).start()

        return carry

    def step4(k, carry):
        @pl.when(middle)
        def _():
            rows = half_rows(k, other_at)
            done = gz.at[rows]
            arrived(done, gz_r.at[2, k])
            remote(done, done, gz_s.at[3, k], gz_r.at[1, k], outer_id).start()
            pltpu.make_async_copy(done, g_out.at[rows], g_loc.at[1, k]).start()

        return carry

    def step5(k, carry):
        @pl.when(end)
        def _():
            rows = sub_rows(k)
            arrived(gz.at[half_rows(k, 0)], gz_r.at[0, k])
            arrived(gz.at[half_rows(k, HALF)], gz_r.at[1, k])
            pltpu.make_async_copy(gz.at[rows], g_out.at[rows], g_loc.at[0, k]).start()

        return carry

    steps = (step1, step2, step3, step4, step5)
    last_point = max(len(row) for row in TAKEN) + LAGS[-1]

    def progress(point):
        if not chain:
            return

        def taken(p):
            first, second = ((0 if p < 0 else row[min(p, len(row) - 1)]) for row in TAKEN)
            return first if first == second else jnp.where(s == 0, first, second)

        for step, lag in zip(steps, LAGS):
            lo, hi = taken(point - lag - 1), taken(point - lag)
            if not (isinstance(lo, int) and isinstance(hi, int) and lo == hi):
                lax.fori_loop(lo, hi, step, 0)

    def finish_grads():
        def one(k, carry):
            rows = sub_rows(k)
            half = grads.at[1 - s, half_rows(k, 0)]
            arrived(grads.at[1 - s, rows], gx_s.at[k])

            @pl.when(end)
            def _():
                arrived(grads.at[s, rows], gz_s.at[0, k])
                arrived(g_out.at[rows], g_loc.at[0, k])

            @pl.when(middle)
            def _():
                for j in range(4):
                    arrived(half, gz_s.at[j, k])
                for j in range(2):
                    arrived(g_out.at[half_rows(k, 0)], g_loc.at[j, k])

            return carry

        lax.fori_loop(0, KS, one, 0)

    def q_rows(h):
        return pl.ds(pl.multiple_of(h * HEAD, HEAD), HEAD)

    def segments():
        wide = lax.broadcasted_iota(jnp.int32, (128, 128), 1)
        tall = lax.broadcasted_iota(jnp.int32, (128, 128), 0)
        slots = len_ref.shape[2]
        square[...] = jnp.zeros_like(square)
        square[0:1, 0:slots] = len_ref[s].astype(F32)
        row = jnp.broadcast_to(square[0:1], (128, 128))
        column = row.T
        column_sums = jnp.sum(jnp.where(wide <= tall, row, 0.0), axis=1, keepdims=True)
        row_sums = jnp.sum(jnp.where(tall <= wide, column, 0.0), axis=0, keepdims=True)
        used = (lax.broadcasted_iota(jnp.int32, (128, 1), 0) < slots).astype(F32)
        used_row = (lax.broadcasted_iota(jnp.int32, (1, 128), 1) < slots).astype(F32)
        lane = lax.broadcasted_iota(jnp.int32, (1, N), 1)
        place = lane
        padding = jnp.zeros((1, N), F32)
        for off, n in CH:
            for at in range(4):
                start = 4 * off + at * n
                device = at % 2 * 2 + at // 2
                here = lane >= start
                place = jnp.where(here, lane - start + device * own + off, place)
                padding = jnp.where(here, jnp.where(lane - start + off >= own, 1.0, 0.0), padding)
                r = lax.broadcasted_iota(jnp.int32, (n, 1), 0) + off
                after = jnp.where((r + device * own).astype(F32) >= row_sums, used_row, 0.0)
                seg = jnp.sum(after, axis=1, keepdims=True)
                segc_ref[start : start + n] = jnp.where(r >= own, -1.0, seg)
        seg = jnp.sum(jnp.where(place.astype(F32) >= column_sums, used, 0.0), axis=0, keepdims=True)
        segr_ref[...] = jnp.where(padding > 0, -1.0, seg)

    def padded_rows(ref, k):
        off, n = CH[k]
        v = ref[s, off : min(off + n, own)].astype(F32)
        if off + n > own:
            v = jnp.concatenate([v, jnp.zeros((off + n - own, D), F32)], axis=0)
        return v

    def attention_input(l, k):
        xh, r = normed(xres[own_rows(k)])
        xh1[l, own_rows(k)] = xh
        r1[l, own_rows(k)] = r
        a_all[l, block_rows(k, pos)] = (xh * sml[l, 0:1]).astype(BF)
        gather_start(a_all, l, l, 0, k)

    def project(l, k):
        off, n = CH[k]
        rows, lanes = slice(4 * off, 4 * (off + n)), slice(4 * off, 4 * (off + n))

        def query_key(i, carry):
            at = pl.ds(pl.multiple_of(i * HD, HEAD), HD)
            v = mm_nt(wq[l, at], a_all[l, rows])
            for h in range(NH):
                u = v[h * HEAD : (h + 1) * HEAD]
                u = u - jnp.mean(u, axis=0, keepdims=True)
                rr = lax.rsqrt(jnp.mean(u * u, axis=0, keepdims=True) + EPS)
                u = u * rr
                at = pl.ds(pl.multiple_of(i * HD + h * HEAD, HEAD), HEAD)
                qkh[l, at, lanes] = u
                qkr[l, i, pl.ds(h, 1), lanes] = rr
                scale = jnp.where(i == 0, HEAD**-0.5, 1.0).astype(F32)
                gain = jnp.where(i == 0, qkg[l, :, h : h + 1], qkg[l, :, NH + h : NH + h + 1])
                qkvb[l, at, lanes] = ((u * gain).astype(BF).astype(F32) * scale).astype(BF)
            return carry

        lax.fori_loop(0, 2, query_key, 0)
        qkvb[l, 2 * HD :, lanes] = mm_nt(wq[l, 2 * HD :], a_all[l, rows]).astype(BF)

    def attention(l):
        def head(h, carry):
            q_t = qkvb[l, q_rows(h)]
            v_t = qkvb[l, q_rows(2 * NH + h)]
            rows_buf[:, :HEAD] = qkvb[l, q_rows(NH + h)].astype(F32).T.astype(BF)

            def block(i, total):
                at = pl.ds(pl.multiple_of(i * KEY_BLOCK, KEY_BLOCK), KEY_BLOCK)
                sc = mm(rows_buf[at, :HEAD], q_t)
                e = jnp.where(segc_ref[at] == segr_ref[...], jnp.exp(sc), 0.0)
                e_buf[at] = e.astype(BF)
                return total + jnp.sum(e, axis=0, keepdims=True)

            total = lax.fori_loop(0, NB, block, jnp.zeros((1, N), F32), unroll=True)
            lse[l, pl.ds(h, 1)] = jnp.log(total)
            o_t[l, q_rows(h)] = (mm(v_t, e_buf[...]) * (1.0 / total)).astype(BF)
            return carry

        lax.fori_loop(0, NH, head, 0)
        rows_two[:, :HD] = o_t[l].astype(F32).T.astype(BF)

    def hidden(l, k):
        off, n = CH[k]

        def tile(i, carry):
            rows = pl.ds(pl.multiple_of(4 * off + lax.rem(i, 2) * 2 * n, 16), 2 * n)
            cols = pl.ds(pl.multiple_of((i // 2) * COLS, COLS), COLS)
            u = mm(b_all[l, rows], wu[l, :, cols])
            cdf = 0.5 * (1.0 + lax.erf(u * 0.7071067811865476))
            pdf = jnp.exp(-0.5 * u * u) * 0.3989422804014327
            g_all[l, rows, cols] = (u * cdf).astype(BF)
            gp_all[l, rows, cols] = (cdf + u * pdf).astype(BF)
            return carry

        lax.fori_loop(0, 2 * (FF // COLS), tile, 0)

    def hidden_back(l, k):
        off, n = CH[k]

        def tile(i, carry):
            rows = pl.ds(pl.multiple_of(4 * off + lax.rem(i, 2) * 2 * n, 16), 2 * n)
            cols = pl.ds(pl.multiple_of((i // 2) * COLS, COLS), COLS)
            dg = mm_nt(dm_all[0, rows], wd[l, cols])
            gp_all[l, rows, cols] = (dg * gp_all[l, rows, cols].astype(F32)).astype(BF)
            return carry

        lax.fori_loop(0, 2 * (FF // COLS), tile, 0)

    def down_grad(l):
        def tile(i, carry):
            cols = pl.ds(pl.multiple_of(i * COLS, COLS), COLS)
            at = pl.ds(pl.multiple_of(FD + i * COLS, COLS), COLS)
            grads[l, at] = mm_tn(g_all[l, :, cols], dm_all[0]).astype(BF)
            send_grads(l, i * (COLS // SUB), (i + 1) * (COLS // SUB))
            return carry

        lax.fori_loop(0, FF // COLS, tile, 0)

    def up_grad(l):
        def tile(i, carry):
            cols = pl.ds(pl.multiple_of(i * COLS, COLS), COLS)
            at = pl.ds(pl.multiple_of(UP + i * COLS, COLS), COLS)
            grads[l, at] = mm_tn(b_all[l, :, cols], gp_all[l]).astype(BF)
            send_grads(l, UP // SUB + i * (COLS // SUB), UP // SUB + (i + 1) * (COLS // SUB))
            return carry

        lax.fori_loop(0, D // COLS, tile, 0)

    def gains_of(l, i, h):
        out = qkg[l, :, i * NH : i * NH + 1]
        for k in range(1, NH):
            out = jnp.where(h == k, qkg[l, :, i * NH + k : i * NH + k + 1], out)
        return out

    def attention_back(l):
        def head(h, carry):
            q_t = qkvb[l, q_rows(h)]
            k_t = qkvb[l, q_rows(NH + h)]
            v_t = qkvb[l, q_rows(2 * NH + h)]
            rows_buf[:, :HEAD] = k_t.astype(F32).T.astype(BF)
            rows_two[:, :HEAD] = v_t.astype(F32).T.astype(BF)
            do_t = dot_buf[q_rows(h)]
            delta = jnp.sum(do_t.astype(F32) * o_t[l, q_rows(h)].astype(F32), axis=0, keepdims=True)
            log_total = lse[l, pl.ds(h, 1)]

            def block(i, carry):
                at = pl.ds(pl.multiple_of(i * KEY_BLOCK, KEY_BLOCK), KEY_BLOCK)
                sc = mm(rows_buf[at, :HEAD], q_t)
                p = jnp.where(segc_ref[at] == segr_ref[...], jnp.exp(sc - log_total), 0.0)
                dp = mm(rows_two[at, :HEAD], do_t)
                e_buf[at] = p.astype(BF)
                d_buf[at] = (p * (dp - delta)).astype(BF)
                return carry

            lax.fori_loop(0, NB, block, 0, unroll=True)
            dqkv_t[q_rows(2 * NH + h)] = mm_nt(do_t, e_buf[...]).astype(BF)
            dk = mm_nt(q_t, d_buf[...])
            dq = mm(k_t, d_buf[...]) * (HEAD**-0.5)
            for i, dv in ((0, dq), (1, dk)):
                at = q_rows(i * NH + h)
                dv = dv.astype(BF).astype(F32)
                uh = qkh[l, at]
                lanes = lax.broadcasted_iota(jnp.int32, (HEAD, 128), 1) == i * NH + h
                hgains[l] = jnp.where(lanes, jnp.sum(dv * uh, axis=1, keepdims=True), hgains[l])
                g = dv * gains_of(l, i, h)
                back = g - jnp.mean(g, axis=0, keepdims=True) - uh * jnp.mean(g * uh, axis=0, keepdims=True)
                dqkv_t[at] = (qkr[l, i, pl.ds(h, 1)] * back).astype(BF)
            return carry

        hgains[l] = jnp.zeros((HEAD, 128), F32)
        lax.fori_loop(0, NH, head, 0)
        rows_buf[...] = dqkv_t[...].astype(F32).T.astype(BF)

    each = range(len(CH))
    gains[...] = jnp.zeros_like(gains)

    for l in range(2):
        if l == 0:
            weights_here(l, 0)
            weights_here(l, 1)
            for k in each:
                xres[own_rows(k)] = padded_rows(x_ref, k)
                attention_input(l, k)
                dm_all[0, block_rows(k, pos)] = padded_rows(ct_ref, k).astype(BF)
            segments()
            forward_blocks(0, 3)
        else:
            weights_here(l, 1)
        weights_here(l, 2)
        for k in each:
            gather_pass(a_all, l, l, 0, k)
        for k in each:
            gather_finish(a_all, l, l, 0, k)
            project(l, k)
        if l == 0:
            for k in each:
                gather_start(dm_all, 0, 1, 2, k)
            forward_blocks(3, 4)
        attention(l)
        if l == 0:
            forward_blocks(4, 6)
            for k in each:
                gather_pass(dm_all, 0, 1, 2, k)
        weights_here(l, 3)
        for k in each:
            scatter_start(lambda at, cols: mm(rows_two[at, :HD], wo[l, :, cols]), l, 0, k)
        if l == 0:
            forward_blocks(6, 7)
        for k in each:
            residual = xres[own_rows(k)] + scatter_finish(l, 0, k)
            xres[own_rows(k)] = residual
            xh, r = normed(residual)
            xh2[l, own_rows(k)] = xh
            r2[l, own_rows(k)] = r
            b_all[l, block_rows(k, pos)] = (xh * sml[l, 1:2]).astype(BF)
            gather_start(b_all, l, l, 1, k)
        if l == 0:
            forward_blocks(7, len(blocks))
        weights_here(l, 4)
        gather_pass(b_all, l, l, 1, 0)
        for k in each:
            gather_finish(b_all, l, l, 1, k)
            hidden(l, k)
            if k + 1 < len(CH):
                gather_pass(b_all, l, l, 1, k + 1)
            if k == 0:
                weights_here(l, 5)
            scatter_start(lambda at, cols: mm(g_all[l, at], wd[l, :, cols]), l, 1, k)
        if l == 0:
            for k in each:
                rounded = (xres[own_rows(k)] + scatter_finish(l, 1, k)).astype(BF)
                ybuf[l, own_rows(k)] = rounded
                xres[own_rows(k)] = rounded.astype(F32)
                if k == 0:
                    weights_here(1, 0)
                attention_input(1, k)

    for l in (1, 0):
        base = LAYER_POINTS * (1 - l)
        progress(base)
        if l == 1:
            for k in each:
                gather_finish(dm_all, 0, l, 2, k)
                hidden_back(l, k)
            down_grad(l)
            for k in each:
                ybuf[l, own_rows(k)] = (xres[own_rows(k)] + scatter_finish(l, 1, k)).astype(BF)
                xres[own_rows(k)] = padded_rows(ct_ref, k)
            y_move = remote(ybuf.at[1 - s], ylo, x_s.at[0], x_r.at[0], x_id)
            y_move.start()
            for k in each:
                scatter_start(lambda at, cols: mm_nt(gp_all[l, at], wu[l, cols]), l, 2, k)
        else:
            for k in each:
                gather_pass(dm_all, 0, l, 2, k)
            for k in each:
                gather_finish(dm_all, 0, l, 2, k)
            down_grad(l)
            for k in each:
                hidden_back(l, k)
                scatter_start(lambda at, cols: mm_nt(gp_all[l, at], wu[l, cols]), l, 2, k)
        progress(base + 1)
        up_grad(l)
        progress(base + 2)
        for k in each:
            db = scatter_finish(l, 2, k)
            xh = xh2[l, own_rows(k)]
            dh = xres[own_rows(k)] + normed_back(db, sml[l, 1:2], xh, r2[l, own_rows(k)])
            xres[own_rows(k)] = dh
            da_all[0, block_rows(k, pos)] = dh.astype(BF)
            gather_start(da_all, 0, l, 3, k)
            gains[l, 1:2] = gains[l, 1:2] + jnp.sum(db * xh, axis=0, keepdims=True)
        progress(base + 3)
        for k in each:
            gather_pass(da_all, 0, l, 3, k)
        for k in each:
            gather_finish(da_all, 0, l, 3, k)
        dot_buf[...] = mm_nt(wo[l], da_all[0]).astype(BF)
        progress(base + 4)
        attention_back(l)
        progress(base + 5)
        for k in each:
            scatter_start(lambda at, cols: mm(rows_buf[at], wq[l, :, cols]), l, 3, k)
        grads[l, OUT:QKV] = mm(o_t[l], da_all[0]).astype(BF)
        send_grads(l, OUT // SUB, QKV // SUB)
        grads[l, QKV:] = mm(dqkv_t[...], a_all[l]).astype(BF)
        send_grads(l, QKV // SUB, KS)
        progress(base + 6)
        for k in each:
            da = scatter_finish(l, 3, k)
            xh = xh1[l, own_rows(k)]
            dx = xres[own_rows(k)] + normed_back(da, sml[l, 0:1], xh, r1[l, own_rows(k)])
            rounded = dx.astype(BF)
            dxbuf[l, own_rows(k)] = rounded
            if l == 1:
                xres[own_rows(k)] = rounded.astype(F32)
                dm_all[0, block_rows(k, pos)] = rounded
                gather_start(dm_all, 0, 0, 2, k)
            else:
                xres[own_rows(k)] = dx
            gains[l, 0:1] = gains[l, 0:1] + jnp.sum(da * xh, axis=0, keepdims=True)

        progress(base + 7)

        @pl.when(l == s)
        def _():
            ig_out[s] = dxbuf[1, 0:own].astype(F32) if l == 1 else xres[0:own]

        @pl.when(l != s)
        def _():
            if chain:
                remote(gains.at[1 - s], gains_x, sm_s.at[0], sm_r.at[0], x_id).start()
                remote(hgains.at[1 - s], hgains_x, sm_s.at[1], sm_r.at[1], x_id).start()
            remote(dxbuf.at[1 - s], dxlo, x_s.at[1], x_r.at[1], x_id).start()

    y_move.wait()
    y_out[s] = ybuf[s, 0:own]
    y_out[1 - s] = ylo[0:own]
    finish_weights()

    def finish_inputs():
        arrived(dxlo, x_s.at[1])
        arrived(dxlo, x_r.at[1])
        ig_out[1 - s] = dxlo[0:own].astype(F32)

    taken_all = max(len(row) for row in TAKEN)
    for point in range(2 * LAYER_POINTS, taken_all):
        progress(point)
    if chain:
        arrived(gains_x, sm_r.at[0])
        arrived(hgains_x, sm_r.at[1])
        gains_z[b] = gains[s] + gains_x[...]
        hgains_z[b] = hgains[s] + hgains_x[...]
        for i, peer in enumerate(z_ids):
            remote(gains_z.at[b], gains_z.at[b], sm_s.at[2 + i], sm_r.at[2 + i], peer).start()
            remote(hgains_z.at[b], hgains_z.at[b], sm_s.at[5 + i], sm_r.at[5 + i], peer).start()
        progress(taken_all)
        progress(taken_all + 1)
        for i in range(3):
            arrived(gains_x, sm_r.at[2 + i])
            arrived(hgains_x, sm_r.at[5 + i])
        gh_out[...] = hgains_z[0] + hgains_z[1] + hgains_z[2] + hgains_z[3]
        gains_t[t] = gains_z[0] + gains_z[1] + gains_z[2] + gains_z[3]
        for i, peer in enumerate((core_id, y_id, diag_id)):
            remote(gains_t.at[t], gains_t.at[t], sm_s.at[8 + i], sm_r.at[8 + i], peer).start()
        for point in range(taken_all + 2, last_point):
            if point == last_point - 2:
                finish_inputs()
            progress(point)
        for i in range(3):
            arrived(gains_x, sm_r.at[8 + i])
        gg_out[...] = gains_t[0] + gains_t[1] + gains_t[2] + gains_t[3]
    else:
        g_out[...] = grads[...]
        gg_out[...] = gains[...]
        gh_out[...] = hgains[...]
    if not chain:
        finish_inputs()
    if chain:
        finish_grads()
        for i in range(2, 5):
            arrived(gains_x, sm_s.at[i])
            arrived(hgains_x, sm_s.at[3 + i])
            arrived(gains_x, sm_s.at[6 + i])
        arrived(gains_x, sm_s.at[0])
        arrived(hgains_x, sm_s.at[1])


def fused(chain, x, ct, lengths, again, mgain, qgain, kgain, wq, wo, wu, wd):
    own, D = x.shape[1:]
    R = ceil_to(own, 16)
    N = 4 * R
    QD, HD, FF = wq.shape[0], wo.shape[0], wu.shape[1]
    NH = HD // HEAD
    CH = len(chunks_of(R))
    vmem = pl.BlockSpec(memory_space=pltpu.VMEM)
    hbm = pl.BlockSpec(memory_space=pl.ANY)
    shape = jax.ShapeDtypeStruct
    V = pltpu.VMEM
    dma = pltpu.SemaphoreType.DMA
    G = FF + D + HD + QD
    KS = G // SUB
    ahead = () if chain else (2,)
    extra = [
        V((G, D), BF), V((G, D), BF), V((KS, SUB // 2, D), BF),
        V((8, D), F32), V((HEAD, 128), F32), V((4, 8, D), F32), V((4, HEAD, 128), F32), V((4, 8, D), F32),
        dma((KS,)), dma((KS,)), dma((4, KS)), dma((3, KS)), dma((2, KS)), dma((11,)), dma((11,)),
    ]
    if not chain:
        extra = [V((8, 128), F32)] * 8 + [dma((1,))] * 7
    return pl.pallas_call(
        functools.partial(body, chain),
        out_shape=(
            shape((2, own, D), BF),
            shape((2, own, D), F32),
            shape(ahead + (G, D), BF),
            shape(ahead + (8, D), F32),
            shape(ahead + (HEAD, 128), F32),
        ),
        in_specs=[vmem] * 7 + [hbm] * 4,
        out_specs=(vmem, vmem, hbm if chain else vmem, vmem, vmem),
        scratch_shapes=[
            V((2, QD, D), BF), V((2, HD, D), BF), V((2, D, FF), BF), V((2, FF, D), BF),
            V((2, 8, D), F32), V((2, HEAD, 128), F32), V((N, 1), F32), V((1, N), F32), V((128, 128), F32),
            V((R, D), F32), V((2, R, D), F32), V((2, R, 1), F32), V((2, R, D), F32), V((2, R, 1), F32),
            V((2, N, D), BF), V((2, N, D), BF), V((1, N, D), BF), V((1, N, D), BF),
            V((2, 2 * HD, N), F32), V((2, 2, 8, N), F32), V((2, QD, N), BF), V((2, 8, N), F32),
            V((2, HD, N), BF), V((2, N, FF), BF), V((2, N, FF), BF),
            V((N, QD), BF), V((N, HD), BF), V((2 * R, D), F32), V((2 * R, D), BF), V((R, D), BF),
            V((2, 2 * R, D), BF), V((2, R, D), BF),
            V((N, N), BF), V((N, N), BF), V((HD, N), BF), V((QD, N), BF),
            V((2, R, D), BF), V((2, R, D), BF), V((R, D), BF), V((R, D), BF),
            V((2, G, D), BF), V((2, 8, D), F32), V((2, HEAD, 128), F32),
            dma((6,)), dma((16,)), dma((16,)), dma((16,)), dma((16,)),
            dma((2, 4, 3, CH)), dma((2, 4, 3, CH)), dma((2, 4, 2, CH)), dma((2, 4, 2, CH)), dma((2,)), dma((2,)),
        ] + extra,
        name="layers",
        compiler_params=pltpu.CompilerParams(
            collective_id=0, has_side_effects=True, vmem_limit_bytes=63 * 2**20
        ),
    )(x, ct, lengths, again, mgain, qgain, kgain, wq, wo, wu, wd)


def widen(
    y_in, ig_in, g_in, gg_ref, gh_ref,
    y_out, ig_out, gd_out, gu_out, go_out, gq_out, gattn_out, gmlp_out, gqg_out, gkg_out,
    low, wide, y_buf, ig_buf, in_sem, out_sem, move_sem,
):
    fetch = [
        pltpu.make_async_copy(y_in, y_buf, move_sem.at[0]),
        pltpu.make_async_copy(ig_in, ig_buf, move_sem.at[1]),
    ]
    put = [
        pltpu.make_async_copy(y_buf, y_out, move_sem.at[2]),
        pltpu.make_async_copy(ig_buf, ig_out, move_sem.at[3]),
    ]
    pieces = []
    at = 0
    for out in (gd_out, gu_out, go_out, gq_out):
        for row in range(0, out.shape[0], SUB):
            pieces.append((at, row, out))
            at += SUB
    loads = [pltpu.make_async_copy(g_in.at[a : a + SUB], low.at[a : a + SUB], in_sem.at[i]) for i, (a, _, _) in enumerate(pieces)]
    stores = [
        pltpu.make_async_copy(wide.at[a : a + SUB], out.at[row : row + SUB], out_sem.at[i])
        for i, (a, row, out) in enumerate(pieces)
    ]
    for copy in fetch + loads:
        copy.start()
    gattn_out[...] = gg_ref[0:1]
    gmlp_out[...] = gg_ref[1:2]
    heads = gqg_out.shape[0]
    by_head = gh_ref[...].T
    for h in range(heads):
        gqg_out[h] = by_head[h : h + 1]
        gkg_out[h] = by_head[heads + h : heads + h + 1]
    for i in range(2):
        fetch[i].wait()
        put[i].start()
    for i, (a, _, _) in enumerate(pieces):
        loads[i].wait()
        wide[a : a + SUB] = low[a : a + SUB].astype(F32)
        stores[i].start()
    for copy in stores + put:
        copy.wait()


def final(y, ig, g, gg, gh, FF, D, HD):
    G = g.shape[0]
    NH = HD // HEAD
    vmem = pl.BlockSpec(memory_space=pltpu.VMEM)
    hbm = pl.BlockSpec(memory_space=pl.ANY)
    shape = jax.ShapeDtypeStruct
    dma = pltpu.SemaphoreType.DMA
    return pl.pallas_call(
        widen,
        out_shape=(
            shape(y.shape, BF), shape(ig.shape, F32), shape((FF, D), F32), shape((D, FF), F32), shape((HD, D), F32),
            shape((3 * HD, D), F32), shape((1, D), F32), shape((1, D), F32), shape((NH, 1, HEAD), F32),
            shape((NH, 1, HEAD), F32),
        ),
        in_specs=[hbm] * 3 + [vmem] * 2,
        out_specs=(hbm,) * 6 + (vmem,) * 4,
        scratch_shapes=[
            pltpu.VMEM((G, D), BF), pltpu.VMEM((G, D), F32), pltpu.VMEM(y.shape, BF),
            pltpu.VMEM(ig.shape, F32), dma((G // SUB,)), dma((G // SUB,)), dma((4,)),
        ],
        name="widen",
        compiler_params=pltpu.CompilerParams(vmem_limit_bytes=60 * 2**20),
    )(y, ig, g, gg, gh)


def shards(
    patches, cotangent, image_lengths, attn_gain, qkv_weight, query_gain, key_gain, out_weight,
    mlp_gain, up_weight, down_weight,
):
    s = lax.axis_index("section")
    own, D = patches.shape[1:]
    HD = out_weight.shape[1]
    NH = HD // HEAD
    wq = qkv_weight[0].reshape(D, 3 * HD).T
    chain = lax.axis_size("batch") == 4
    y, ig, g, gg, gh = fused(
        chain, patches, cotangent, image_lengths, attn_gain, mlp_gain, query_gain, key_gain, wq,
        out_weight[0], up_weight[0], down_weight[0],
    )
    if not chain:
        theirs = lax.ppermute(g[1 - s], "section", [(0, 1), (1, 0)])
        g = lax.psum((g[s].astype(F32) + theirs.astype(F32)).astype(BF), "batch")
        gg = lax.psum(gg, ("section", "batch", "tensor"))[s]
        gh = lax.psum(gh, ("section", "batch"))[s]
    y, ig, gd, gu, go, gq, gattn, gmlp, gqg, gkg = final(y, ig, g, gg, gh, up_weight.shape[2], D, HD)
    return (
        y[None],
        ig[None],
        gattn,
        gq.T.reshape(D, 3, HD)[None],
        gqg.reshape(1, NH, HEAD),
        gkg.reshape(1, NH, HEAD),
        go[None],
        gmlp,
        gu[None],
        gd[None],
    )


def solution(mesh):
    return jax.shard_map(
        shards,
        mesh=mesh,
        in_specs=(
            P(None, ("batch", "tensor"), None),
            P(None, ("batch", "tensor"), None),
            P(None, "batch", None),
            P("section", None),
            P("section", None, None, "tensor"),
            P("section", "tensor", None),
            P("section", "tensor", None),
            P("section", "tensor", None),
            P("section", None),
            P("section", None, "tensor"),
            P("section", "tensor", None),
        ),
        out_specs=(
            P("section", None, ("batch", "tensor"), None),
            P("section", None, ("batch", "tensor"), None),
            P("section", None),
            P("section", None, None, "tensor"),
            P("section", "tensor", None),
            P("section", "tensor", None),
            P("section", "tensor", None),
            P("section", None),
            P("section", None, "tensor"),
            P("section", "tensor", None),
        ),
        check_vma=False,
    )
```
